32 devices in a mesh: dp: 4 (over y, core), gx: 4 (over z), gy: 2 (over x).
Axes of the slice: x: 2, y: 2, z: 4, core: 2. Of those that a mesh axis runs over, the one named last changes fastest.
Arguments:
- prompt: bfloat16 [16, 2048, 1088], P(('dp', 'gx'), 'gy'), may hold values from -6 to 6
- continuations: bfloat16 [32, 256, 1088], P(('dp', 'gx', 'gy')), may hold values from -6 to 6
- prefix_len: int32 [32], P(('dp', 'gx', 'gy')), may hold values from 512 to 2048, as said below
- attn_gain: float32 [1088], replicated, may hold values from 0.5 to 1.5
- attn_shift: float32 [1088], replicated, may hold values from -1.25 to 1.25
- qkv_weight: bfloat16 [1088, 3264], P('gx', 'gy'), may hold values from -0.25 to 0.25
- query_bias: float32 [1088], replicated, may hold values from -1.25 to 1.25
- value_bias: float32 [1088], replicated, may hold values from -1.25 to 1.25
- out_weight: bfloat16 [1088, 1088], P('gx', 'gy'), may hold values from -0.75 to 0.75
- out_bias: float32 [1088], replicated, may hold values from -1.25 to 1.25
- mlp_gain: float32 [1088], replicated, may hold values from 0.5 to 1.5
- mlp_shift: float32 [1088], replicated, may hold values from -1.25 to 1.25
- up_weight: bfloat16 [1088, 4352], P('gx', 'gy'), may hold values from -0.1875 to 0.1875
- up_bias: float32 [4352], replicated, may hold values from -1.25 to 1.25
- down_weight: bfloat16 [4352, 1088], P('gy', 'gx'), may hold values from -0.09375 to 0.09375
- down_bias: float32 [1088], replicated, may hold values from -1.25 to 1.25
- grad_prompt: bfloat16 [16, 2048, 1088], P(('dp', 'gx'), 'gy'), may hold values from -6 to 6
- grad_continuations: bfloat16 [32, 256, 1088], P(('dp', 'gx', 'gy')), may hold values from -6 to 6
Outputs:
- prompt_out: bfloat16 [16, 2048, 1088], P(('dp', 'gx'), 'gy')
- continuation_out: bfloat16 [32, 256, 1088], P(('dp', 'gx', 'gy'))
- prompt_grad: float32 [16, 2048, 1088], P(('dp', 'gx'), 'gy')
- continuation_grad: float32 [32, 256, 1088], P(('dp', 'gx', 'gy'))
- attn_gain_grad: float32 [1088], replicated
- attn_shift_grad: float32 [1088], replicated
- qkv_weight_grad: float32 [1088, 3264], P('gx', 'gy')
- query_bias_grad: float32 [1088], replicated
- value_bias_grad: float32 [1088], replicated
- out_weight_grad: float32 [1088, 1088], P('gx', 'gy')
- out_bias_grad: float32 [1088], replicated
- mlp_gain_grad: float32 [1088], replicated
- mlp_shift_grad: float32 [1088], replicated
- up_weight_grad: float32 [1088, 4352], P('gx', 'gy')
- up_bias_grad: float32 [4352], replicated
- down_weight_grad: float32 [4352, 1088], P('gy', 'gx')
- down_bias_grad: float32 [1088], replicated
The draws below stay inside these ranges and needn't reach their ends.
Inputs may be any that keep to these rules, and one draw needn't show every extreme that they name: `prefix_len`: in every group one continuation reads all 2048 prompt tokens and another reads 2048 // 4.
All inputs are finite; a program needn't handle non-finite values.
Results may differ from the reference program's by a relative error of at most 0.019.
Values may be sent and summed in bfloat16 or wider, within the bound.
No kernel may reach another device: no remote copies, remote signals or barrier semaphores. Data moves between devices by JAX's collectives and lax.ppermute only.
A program may use at most 256 MiB of HBM per device.

```python
import jax
import jax.numpy as jnp
from jax import lax

D = 1088
HEADS = 17
HEAD_DIM = 64
FF = 4352
PROMPT = 2048
CONT_LEN = 256
BRANCHES = 2
GROUPS = 16
CONTINUATIONS = 32


def draw_prefix_len(key, part):
    key = jax.random.fold_in(key, 11)
    key_base, key_full, key_short = jax.random.split(key, 3)
    lengths_drawn = jax.random.randint(key_base, (GROUPS, BRANCHES), PROMPT // 4, PROMPT + 1)
    full_pick = jax.random.randint(key_full, (GROUPS, 1), 0, BRANCHES)
    short_pick = (full_pick + 1 + jax.random.randint(key_short, (GROUPS, 1), 0, BRANCHES - 1)) % BRANCHES
    branch_ids = jnp.arange(BRANCHES)[None, :]
    lengths_drawn = jnp.where(branch_ids == full_pick, PROMPT, lengths_drawn)
    lengths_drawn = jnp.where(branch_ids == short_pick, PROMPT // 4, lengths_drawn)
    return lengths_drawn.reshape(GROUPS * BRANCHES).astype(jnp.int32)


def block_levels(stream_key, dims, pieces, smallest, top_value):
    level, own = 1.0, jax.random.fold_in(stream_key, 6)
    for axis_at, parts in pieces:
        draws = jnp.exp(jax.random.uniform(jax.random.fold_in(own, axis_at), (parts,), jnp.float32, smallest / len(pieces), top_value / len(pieces)))
        level = level * jnp.repeat(draws, dims[axis_at] // parts).reshape([-1 if axis == axis_at else 1 for axis in range(len(dims))])
    return level


def bell_draw(rng, extent, deviation, most, cuts=(), kind=jnp.bfloat16):
    level = block_levels(rng, extent, cuts, -0.22, 0.18) if cuts else 1.0
    values = jax.random.normal(rng, extent, jnp.float32) * deviation * level
    return jnp.minimum(jnp.maximum(values, -most), most).astype(kind)


def setup_inputs(seed: int = 0) -> dict:
    seeds = jax.random.split(jax.random.key(seed), 19)
    return {
        "prompt": bell_draw(seeds[0], (GROUPS, PROMPT, D), 1.0, 6.0, ((0, 16), (1, 2))),
        "continuations": bell_draw(seeds[1], (CONTINUATIONS, CONT_LEN, D), 1.0, 6.0, ((0, 32),)),
        "prefix_len": draw_prefix_len(jax.random.fold_in(seeds[18], 71), 0),
        "attn_gain": jnp.clip(1.0 + 0.1 * jax.random.normal(seeds[3], (D,), jnp.float32), 0.5, 1.5),
        "attn_shift": bell_draw(seeds[4], (D,), 0.2, 1.25, (), jnp.float32),
        "qkv_weight": bell_draw(seeds[5], (D, 3 * D), (D // 2) ** -0.5, 0.25, ((0, 4), (1, 2))),
        "query_bias": bell_draw(seeds[6], (D,), 0.2, 1.25, (), jnp.float32),
        "value_bias": bell_draw(seeds[7], (D,), 0.2, 1.25, (), jnp.float32),
        "out_weight": bell_draw(seeds[8], (D, D), (D // 16) ** -0.5, 0.75, ((0, 4), (1, 2))),
        "out_bias": bell_draw(seeds[9], (D,), 0.2, 1.25, (), jnp.float32),
        "mlp_gain": jnp.clip(1.0 + 0.1 * jax.random.normal(seeds[10], (D,), jnp.float32), 0.5, 1.5),
        "mlp_shift": bell_draw(seeds[11], (D,), 0.2, 1.25, (), jnp.float32),
        "up_weight": bell_draw(seeds[12], (D, FF), D ** -0.5, 0.1875, ((0, 4), (1, 2))),
        "up_bias": bell_draw(seeds[13], (FF,), 0.2, 1.25, (), jnp.float32),
        "down_weight": bell_draw(seeds[14], (FF, D), FF ** -0.5, 0.09375, ((0, 2), (1, 4))),
        "down_bias": bell_draw(seeds[15], (D,), 0.2, 1.25, (), jnp.float32),
        "grad_prompt": bell_draw(seeds[16], (GROUPS, PROMPT, D), 1.0, 6.0, ((0, 16), (1, 2))),
        "grad_continuations": bell_draw(seeds[17], (CONTINUATIONS, CONT_LEN, D), 1.0, 6.0, ((0, 32),)),
    }


epsilon = 1e-05
masked_score = -1e+30
highest = lax.Precision.HIGHEST

@jax.custom_vjp
def low(v):
    return lax.optimization_barrier(v.astype(jnp.bfloat16)).astype(jnp.float32)

@jax.custom_vjp
def low_back(v):
    return v

def low_keep(v):
    return (low(v), None)

def low_pass(kept, grad):
    return (grad,)

def back_keep(v):
    return (v, None)

def back_low(kept, grad):
    return (low(grad),)
low.defvjp(low_keep, low_pass)
low_back.defvjp(back_keep, back_low)

def layer_norm(values_in, norm_gain, norm_shift):
    centre = lax.optimization_barrier(jnp.mean(values_in, axis=-1, keepdims=True))
    centred = values_in - centre
    spread = lax.optimization_barrier(jnp.mean(centred * centred, axis=-1, keepdims=True))
    return centred * lax.rsqrt(spread + epsilon) * norm_gain + norm_shift

def attend(query_heads, key_heads, value_heads, allowed):
    scale = HEAD_DIM ** (-0.5)
    raw_scores = jnp.einsum('ihd,jhd->hij', query_heads, key_heads, precision=highest) * scale
    scores = jnp.where(allowed[None], low_back(raw_scores), masked_score)
    probs = low(jax.nn.softmax(scores, axis=-1))
    return jnp.einsum('hij,jhd->ihd', probs, value_heads, precision=highest)

def group_layer(weights, inputs):
    attn_gain, attn_shift, qkv_weight, query_bias, value_bias, out_weight, out_bias, mlp_gain, mlp_shift, up_weight, up_bias, down_weight, down_bias = weights
    prompt_rows, branch_rows, limits = inputs
    token_rows = jnp.concatenate([prompt_rows, branch_rows.reshape(BRANCHES * CONT_LEN, D)], axis=0)
    act_one = low(layer_norm(token_rows, attn_gain, attn_shift))
    projected = jnp.dot(act_one, qkv_weight, precision=highest)
    queries = low(low_back(projected[:, :D] + query_bias)).reshape(-1, HEADS, HEAD_DIM)
    keys = low(low_back(projected[:, D:2 * D])).reshape(-1, HEADS, HEAD_DIM)
    values = low(low_back(projected[:, 2 * D:] + value_bias)).reshape(-1, HEADS, HEAD_DIM)
    order = jnp.arange(PROMPT)
    prompt_mixed = attend(queries[:PROMPT], keys[:PROMPT], values[:PROMPT], order[:, None] >= order[None, :])
    spans = jnp.arange(PROMPT + CONT_LEN)[None, :]
    places = jnp.arange(CONT_LEN)[:, None]

    def one_branch(branch_q, branch_k, branch_v, limit):
        allowed = jnp.where(spans < PROMPT, spans < limit, spans - PROMPT <= places)
        all_keys = jnp.concatenate([keys[:PROMPT], branch_k], axis=0)
        all_values = jnp.concatenate([values[:PROMPT], branch_v], axis=0)
        return attend(branch_q, all_keys, all_values, allowed)
    shape_branch = (BRANCHES, CONT_LEN, HEADS, HEAD_DIM)
    branch_mixed = jax.vmap(one_branch)(queries[PROMPT:].reshape(shape_branch), keys[PROMPT:].reshape(shape_branch), values[PROMPT:].reshape(shape_branch), limits)
    mixed = jnp.concatenate([prompt_mixed.reshape(PROMPT, D), branch_mixed.reshape(BRANCHES * CONT_LEN, D)], axis=0)
    mixed = low(low_back(mixed))
    resid = token_rows + low_back(jnp.dot(mixed, out_weight, precision=highest) + out_bias)
    act_two = low(layer_norm(resid, mlp_gain, mlp_shift))
    pre_act = low_back(jnp.dot(act_two, up_weight, precision=highest) + up_bias)
    hidden = low(jax.nn.gelu(pre_act, approximate=False))
    result = resid + jnp.dot(hidden, down_weight, precision=highest) + down_bias
    return (result[:PROMPT], result[PROMPT:].reshape(BRANCHES, CONT_LEN, D))

def reference(prompt, continuations, prefix_len, attn_gain, attn_shift, qkv_weight, query_bias, value_bias, out_weight, out_bias, mlp_gain, mlp_shift, up_weight, up_bias, down_weight, down_bias, grad_prompt, grad_continuations):
    limits = prefix_len.reshape(GROUPS, BRANCHES)
    params = (attn_gain.astype(jnp.float32), attn_shift.astype(jnp.float32), qkv_weight.astype(jnp.float32), query_bias.astype(jnp.float32), value_bias.astype(jnp.float32), out_weight.astype(jnp.float32), out_bias.astype(jnp.float32), mlp_gain.astype(jnp.float32), mlp_shift.astype(jnp.float32), up_weight.astype(jnp.float32), up_bias.astype(jnp.float32), down_weight.astype(jnp.float32), down_bias.astype(jnp.float32))

    def whole(prompt_in, branch_in, *weights):

        def one_group(inputs):
            return group_layer(weights, inputs)
        layer_step = jax.checkpoint(one_group)
        out_prompt, out_branch = lax.map(layer_step, (prompt_in, branch_in.reshape(GROUPS, BRANCHES, CONT_LEN, D), limits))
        return (out_prompt, out_branch.reshape(CONTINUATIONS, CONT_LEN, D))
    (out_prompt, out_branch), pullback = jax.vjp(whole, prompt.astype(jnp.float32), continuations.astype(jnp.float32), *params)
    grads = pullback((grad_prompt.astype(jnp.float32), grad_continuations.astype(jnp.float32)))
    return (out_prompt.astype(jnp.bfloat16), out_branch.astype(jnp.bfloat16), grads[0], grads[1], grads[2], grads[3], grads[4], grads[5], grads[6], grads[7], grads[8], grads[9], grads[10], grads[11], grads[12], grads[13], grads[14])
```

```python
import functools
import jax
import jax.numpy as jnp
from jax import lax
from jax.sharding import PartitionSpec as P
from jax.experimental import pallas as pl
from jax.experimental.pallas import tpu as pltpu

HEADS = 17
HEAD_DIM = 64
LOG2E = 1.4426950408889634
NEG = -1e30
BK = 512


def nt(a, b):
    return lax.dot_general(a, b, (((1,), (1,)), ((), ())), preferred_element_type=jnp.float32)


def nn(a, b):
    return jnp.dot(a, b, preferred_element_type=jnp.float32)


def tn(a, b):
    return lax.dot_general(a, b, (((0,), (0,)), ((), ())), preferred_element_type=jnp.float32)


def halves(pair, total):
    lane = lax.broadcasted_iota(jnp.int32, (1, 128), 1)
    left = jnp.minimum(total - pair * 128, 128)
    return lane < 64, jnp.logical_and(lane >= 64, lane < left), lane < left


def norm_bounds(ref, valid, spread):
    part = jnp.where(valid, ref[...], jnp.zeros((), jnp.bfloat16))
    return jnp.max(nn(part * part, spread), axis=0, keepdims=True)


def forward_kernel(pos, q, k, v, kb, vb, o, lse, va, vc, vab, vcb, tops, accs, *, block):
    pair = pl.program_id(0)
    scale = HEAD_DIM ** (-0.5) * LOG2E
    low, high, valid = halves(pair, HEADS * HEAD_DIM)
    zero = jnp.zeros((), jnp.bfloat16)
    one = jnp.ones((), jnp.bfloat16)
    for src, first, second in ((v, va, vc), (vb, vab, vcb)):
        whole = src[...]
        first[...] = jnp.where(low, whole, one)
        second[...] = jnp.where(low, one, jnp.where(high, whole, zero))
    spread = (
        (lax.broadcasted_iota(jnp.int32, (128, 128), 0) < 64)
        == (lax.broadcasted_iota(jnp.int32, (128, 128), 1) < 64)
    ).astype(jnp.bfloat16)
    key_bound = jnp.maximum(norm_bounds(k, valid, spread), norm_bounds(kb, valid, spread))
    bound = jnp.max(key_bound * norm_bounds(q, valid, spread)) * (scale * scale)
    plain = bound < 90.0 * 90.0
    rows = q.shape[0]
    branch = kb.shape[0]
    blocks = [(start, block, False) for start in range(0, rows - branch, block)]
    blocks.append((rows - branch, branch, True))

    def finish(start, size, acc_a, acc_b, top):
        total = pltpu.roll(jnp.where(low, acc_b, acc_a), 64, 1)
        o[start : start + size, :] = (jnp.where(low, acc_a, acc_b) / total).astype(o.dtype)
        turned = (top + jnp.log2(total)).T
        lse[0, 0:1, start : start + size] = turned[0:1, :]
        lse[0, 1:2, start : start + size] = turned[64:65, :]

    def setup(number, start, size, is_branch):
        at = pos[number]
        query = q[start : start + size, :]
        queries = (jnp.where(low, query, zero), jnp.where(high, query, zero))
        row = lax.broadcasted_iota(jnp.int32, (size, BK), 0)
        column = lax.broadcasted_iota(jnp.int32, (size, BK), 1)
        triangle = lax.broadcasted_iota(jnp.int32, (size, size), 1) <= lax.broadcasted_iota(
            jnp.int32, (size, size), 0
        )
        whole_blocks = at // BK

        def allowed(index):
            if is_branch:
                return column + index * BK < at
            return column + index * BK <= row + at

        end = (at + BK - 1) // BK if is_branch else whole_blocks + 1
        return queries, triangle, whole_blocks, allowed, end

    def read(index):
        rows_at = pl.ds(pl.multiple_of(index * BK, BK), BK)
        return jnp.where(valid, k[rows_at, :], zero), va[rows_at, :], vc[rows_at, :]

    def own():
        return jnp.where(valid, kb[...], zero), vab[...], vcb[...]

    @pl.when(plain)
    def _():
        for number, (start, size, is_branch) in enumerate(blocks):
            queries, triangle, whole_blocks, allowed, end = setup(number, start, size, is_branch)

            def step(key, first, second, carry, mask):
                out = []
                for query_h, value_h, acc in zip(queries, (first, second), carry):
                    probs = jnp.exp2(nt(query_h, key) * scale)
                    if mask is not None:
                        probs = jnp.where(mask, probs, 0.0)
                    out.append(acc + nn(probs.astype(jnp.bfloat16), value_h))
                return tuple(out)

            carry = (jnp.zeros((size, 128), jnp.float32),) * 2
            carry = lax.fori_loop(0, whole_blocks, lambda i, c: step(*read(i), c, None), carry)
            if is_branch:
                carry = lax.fori_loop(
                    whole_blocks, end, lambda i, c: step(*read(i), c, allowed(i)), carry
                )
                carry = step(*own(), carry, triangle)
            else:
                carry = step(*read(whole_blocks), carry, allowed(whole_blocks))
            finish(start, size, *carry, 0.0)

    @pl.when(jnp.logical_not(plain))
    def _():
        for number, (start, size, is_branch) in enumerate(blocks):
            queries, triangle, whole_blocks, allowed, end = setup(number, start, size, is_branch)

            def step(key, first, second, mask):
                for head, value_h in enumerate((first, second)):
                    top = tops[head, 0:size, :]
                    scores = jnp.where(mask, nt(queries[head], key), NEG)
                    new_top = jnp.maximum(top, jnp.max(scores, axis=1, keepdims=True))
                    probs = jnp.exp2((scores - new_top[:, 0:1]) * scale).astype(jnp.bfloat16)
                    fade = jnp.exp2((top - new_top) * scale)
                    accs[head, 0:size, :] = accs[head, 0:size, :] * fade + nn(probs, value_h)
                    tops[head, 0:size, :] = new_top

            accs[:, 0:size, :] = jnp.zeros((2, size, 128), jnp.float32)
            tops[:, 0:size, :] = jnp.full((2, size, 128), NEG, jnp.float32)

            @pl.loop(0, end)
            def _(index):
                step(*read(index), allowed(index))

            if is_branch:
                step(*own(), triangle)
            top = jnp.where(low, tops[0, 0:size, :], tops[1, 0:size, :]) * scale
            finish(start, size, accs[0, 0:size, :], accs[1, 0:size, :], top)


def attention_forward(pos, q, k, v, kb, vb, block):
    rows, width = q.shape
    branch = kb.shape[0]
    span = k.shape[0]
    pairs = (HEADS + 1) // 2

    def col(n):
        return pl.BlockSpec((n, 128), lambda p, pos: (0, p))

    return pl.pallas_call(
        functools.partial(forward_kernel, block=block),
        grid_spec=pltpu.PrefetchScalarGridSpec(
            num_scalar_prefetch=1,
            grid=(pairs,),
            in_specs=[col(rows), col(span), col(span), col(branch), col(branch)],
            out_specs=[col(rows), pl.BlockSpec((1, 8, rows), lambda p, pos: (p, 0, 0))],
            scratch_shapes=[
                pltpu.VMEM((span, 128), jnp.bfloat16),
                pltpu.VMEM((span, 128), jnp.bfloat16),
                pltpu.VMEM((branch, 128), jnp.bfloat16),
                pltpu.VMEM((branch, 128), jnp.bfloat16),
                pltpu.VMEM((2, max(block, branch), 128), jnp.float32),
                pltpu.VMEM((2, max(block, branch), 128), jnp.float32),
            ],
        ),
        out_shape=[
            jax.ShapeDtypeStruct((rows, width), jnp.bfloat16),
            jax.ShapeDtypeStruct((pairs, 8, rows), jnp.float32),
        ],
        compiler_params=pltpu.CompilerParams(
            dimension_semantics=("arbitrary",), vmem_limit_bytes=50 * 2**20
        ),
        name="attention_forward",
    )(pos, q, k, v, kb, vb)


def backward_kernel(
    pos, q, k, v, kb, vb, o, do, lse, dq, dk, dv, dkb, dvb,
    ka, kc, kta, ktc, kam, vm, kab, kcb, ktab, ktcb, kbm, vbm, dks, dvs, *, block, span, mode
):
    pair = pl.program_id(0)
    scale = HEAD_DIM ** (-0.5)
    low, high, valid = halves(pair, HEADS * HEAD_DIM)
    zero = jnp.zeros((), jnp.bfloat16)
    for src, whole_ref, first, second, turn_a, turn_b in (
        (k, kam, ka, kc, kta, ktc),
        (kb, kbm, kab, kcb, ktab, ktcb),
    ):
        whole = jnp.where(valid, src[...], zero)
        whole_ref[...] = whole
        if mode == "t":
            first[...] = jnp.where(low, whole, zero)
            second[...] = jnp.where(high, whole, zero)
        else:
            turned = whole.T
            turn_a[...] = turned[0:64, :]
            turn_b[...] = turned[64:128, :]
    vm[...] = jnp.where(valid, v[...], zero)
    vbm[...] = jnp.where(valid, vb[...], zero)
    dks[...] = jnp.zeros_like(dks)
    dvs[...] = jnp.zeros_like(dvs)
    rows = q.shape[0]
    branch = kb.shape[0]
    blocks = [(start, block, False) for start in range(0, rows - branch, block)]
    blocks.append((rows - branch, branch, True))
    ones_a = jnp.broadcast_to(low, (8, 128)).astype(jnp.bfloat16)
    ones_b = jnp.broadcast_to(high, (8, 128)).astype(jnp.bfloat16)
    for number, (start, size, is_branch) in enumerate(blocks):
        at = pos[number]
        here = slice(start, start + size)
        query = q[here, :]
        grad = do[here, :]
        queries = (jnp.where(low, query, zero), jnp.where(high, query, zero))
        grads = (jnp.where(low, grad, zero), jnp.where(high, grad, zero))
        product = jnp.where(valid, grad.astype(jnp.float32) * o[here, :].astype(jnp.float32), 0.0)
        upper = product.astype(jnp.bfloat16)
        lower = (product - upper.astype(jnp.float32)).astype(jnp.bfloat16)
        deltas = tuple((nt(m, upper) + nt(m, lower))[0:1, :] for m in (ones_a, ones_b))
        stats = (lse[0, 0:1, here], lse[0, 1:2, here])
        queries_cat = jnp.concatenate(queries, axis=0)
        grads_cat = jnp.concatenate(grads, axis=0)

        def step(key, value, first, second, mask):
            probs, dscores = [], []
            for query_h, grad_h, delta, stat in zip(queries, grads, deltas, stats):
                scores = nt(key, query_h)
                prob = jnp.exp2(scores * (scale * LOG2E) - stat)
                if mask is not None:
                    prob = jnp.where(mask, prob, 0.0)
                dprob = nt(value, grad_h)
                probs.append(prob.astype(jnp.bfloat16))
                dscores.append((prob * (dprob - delta)).astype(jnp.bfloat16))
            dscores_cat = jnp.concatenate(dscores, axis=1)
            dvalue = nn(jnp.concatenate(probs, axis=1), grads_cat)
            dkey = nn(dscores_cat, queries_cat)
            if mode == "t":
                dquery = tn(dscores[0], first) + tn(dscores[1], second)
            else:
                dquery = jnp.concatenate([nn(first, dscores[0]), nn(second, dscores[1])], axis=0)
            return dquery, dkey, dvalue

        def read(base):
            rows_at = pl.ds(pl.multiple_of(base, BK), BK)
            if mode == "t":
                return kam[rows_at, :], vm[rows_at, :], ka[rows_at, :], kc[rows_at, :]
            return kam[rows_at, :], vm[rows_at, :], kta[:, rows_at], ktc[:, rows_at]

        def accumulate(index, carry, mask):
            rows_at = pl.ds(pl.multiple_of(index * BK, BK), BK)
            dquery, dkey, dvalue = step(*read(index * BK), mask)
            dks[rows_at, :] += dkey
            dvs[rows_at, :] += dvalue
            return carry + dquery

        dim = (size, 128) if mode == "t" else (128, size)
        carry = jnp.zeros(dim, jnp.float32)
        whole_blocks = at // BK
        carry = lax.fori_loop(0, whole_blocks, lambda i, c: accumulate(i, c, None), carry)
        row = lax.broadcasted_iota(jnp.int32, (BK, size), 0)
        column = lax.broadcasted_iota(jnp.int32, (BK, size), 1)
        if is_branch:
            carry = lax.fori_loop(
                whole_blocks,
                (at + BK - 1) // BK,
                lambda i, c: accumulate(i, c, row + i * BK < at),
                carry,
            )
            triangle = lax.broadcasted_iota(jnp.int32, (size, size), 0) <= lax.broadcasted_iota(
                jnp.int32, (size, size), 1
            )
            own = (kab[...], kcb[...]) if mode == "t" else (ktab[...], ktcb[...])
            dquery, dkey, dvalue = step(kbm[...], vbm[...], *own, triangle)
            carry = carry + dquery
            dkb[...] = (dkey * scale).astype(dkb.dtype)
            dvb[...] = dvalue.astype(dvb.dtype)
        else:
            carry = accumulate(whole_blocks, carry, row + whole_blocks * BK <= column + at)
        if mode != "t":
            carry = carry.T
        dq[here, :] = (carry * scale).astype(dq.dtype)
    dk[...] = (dks[...] * scale).astype(dk.dtype)
    dv[...] = dvs[...].astype(dv.dtype)


def attention_backward(pos, q, k, v, kb, vb, o, do, lse, block, mode="n"):
    rows, width = q.shape
    branch = kb.shape[0]
    span = k.shape[0]
    pairs = (HEADS + 1) // 2

    def col(n):
        return pl.BlockSpec((n, 128), lambda p, pos: (0, p))

    def scratch(n):
        tall = pltpu.VMEM((n, 128) if mode == "t" else (8, 128), jnp.bfloat16)
        wide = pltpu.VMEM((64, n) if mode != "t" else (8, 128), jnp.bfloat16)
        return [tall, tall, wide, wide, pltpu.VMEM((n, 128), jnp.bfloat16), pltpu.VMEM((n, 128), jnp.bfloat16)]

    def shape(n, t=jnp.bfloat16):
        return jax.ShapeDtypeStruct((n, width), t)

    return pl.pallas_call(
        functools.partial(backward_kernel, block=block, span=span, mode=mode),
        grid_spec=pltpu.PrefetchScalarGridSpec(
            num_scalar_prefetch=1,
            grid=(pairs,),
            in_specs=[col(rows), col(span), col(span), col(branch), col(branch), col(rows), col(rows),
                      pl.BlockSpec((1, 8, rows), lambda p, pos: (p, 0, 0))],
            out_specs=[col(rows), col(span), col(span), col(branch), col(branch)],
            scratch_shapes=scratch(span) + scratch(branch)
            + [pltpu.VMEM((span, 128), jnp.float32), pltpu.VMEM((span, 128), jnp.float32)],
        ),
        out_shape=[shape(rows), shape(span), shape(span), shape(branch), shape(branch)],
        compiler_params=pltpu.CompilerParams(
            dimension_semantics=("arbitrary",), vmem_limit_bytes=56 * 2**20
        ),
        name="attention_backward",
    )(pos, q, k, v, kb, vb, o, do, lse)


epsilon = 1e-05


def layer_norm(values_in, norm_gain, norm_shift):
    centre = jnp.mean(values_in, axis=-1, keepdims=True)
    centred = values_in - centre
    spread = jnp.mean(centred * centred, axis=-1, keepdims=True)
    return centred * lax.rsqrt(spread + epsilon) * norm_gain + norm_shift


def smooth_gate(pre_act):
    return jax.nn.gelu(pre_act, approximate=False)


def swap(value, axis, bit):
    count = lax.axis_size(axis)
    return lax.ppermute(value, axis, [(i, i ^ bit) for i in range(count)])


def ahead(value, axis, step):
    count = lax.axis_size(axis)
    return lax.ppermute(value, axis, [(i, (i + step) % count) for i in range(count)])


def total_over(value, axes):
    for axis in axes:
        count = lax.axis_size(axis)
        if count & (count - 1):
            value = lax.psum(value, axis)
            continue
        bit = 1
        while bit < count:
            value = value + swap(value, axis, bit)
            bit *= 2
    return value


def by_halves():
    return lax.axis_size("dp") % 2 == 0 and lax.axis_size("gy") == 2


def half_index():
    return lax.axis_index("dp") % 2


def pair_rows(mine, theirs):
    first = half_index() == 0
    return jnp.stack([jnp.where(first, mine, theirs), jnp.where(first, theirs, mine)], axis=-3)


def along_gx(block):
    count = lax.axis_size("gx")
    here = lax.axis_index("gx")
    out = jnp.zeros((count,) + block.shape, block.dtype)
    for step in range(count):
        got = block if step == 0 else ahead(block, "gx", step)
        out = lax.dynamic_update_index_in_dim(out, got, (here - step) % count, 0)
    return out


def order_columns(mine, theirs):
    first = lax.axis_index("gy") == 0
    return jnp.concatenate([jnp.where(first, mine, theirs), jnp.where(first, theirs, mine)], axis=-1)


def gather_ordered(part):
    rows, columns = part.shape
    if not by_halves():
        part = lax.all_gather(part, "gy", axis=1, tiled=True)
        return lax.all_gather(part, "gx", axis=0, tiled=True)
    mine = lax.dynamic_index_in_dim(part.reshape(2, rows // 2, columns), half_index(), 0, False)
    both = order_columns(mine, swap(mine, "gy", 1))
    blocks = along_gx(both)
    return pair_rows(blocks, swap(blocks, "dp", 1)).reshape(-1, 2 * columns)


def gather_parts(part):
    rows, columns = part.shape
    if not by_halves():
        part = lax.all_gather(part, "gx", axis=0, tiled=True)
        return [part] + [ahead(part, "gy", step) for step in range(1, lax.axis_size("gy"))]
    mine = lax.dynamic_index_in_dim(part.reshape(2, rows // 2, columns), half_index(), 0, False)
    blocks = along_gx(mine)
    out = []
    for piece in (blocks, swap(blocks, "gy", 1)):
        out.append(pair_rows(piece, swap(piece, "dp", 1)).reshape(-1, columns))
    return out


def scatter_parts(parts):
    rows, columns = parts[0].shape
    count = lax.axis_size("gx")
    here = lax.axis_index("gx")
    if not by_halves():
        total = parts[0].astype(jnp.float32)
        for step in range(1, len(parts)):
            total = total + ahead(parts[step], "gy", -step).astype(jnp.float32)
        total = lax.psum_scatter(
            total.astype(jnp.bfloat16), "gx", scatter_dimension=0, tiled=True
        )
        return lax.psum(total, "dp").astype(jnp.float32)
    wide = [p.reshape(count, 2, rows // count // 2, columns) for p in parts]
    half = half_index()
    sums = []
    for piece in (wide[1], wide[0]):
        keep = lax.dynamic_index_in_dim(piece, half, 1, False)
        give = lax.dynamic_index_in_dim(piece, 1 - half, 1, False)
        sums.append(keep.astype(jnp.float32) + swap(give, "dp", 1).astype(jnp.float32))
    block = sums[1] + swap(sums[0].astype(jnp.bfloat16), "gy", 1).astype(jnp.float32)
    block = block.astype(jnp.bfloat16)
    total = lax.dynamic_index_in_dim(block, here, 0, False).astype(jnp.float32)
    for step in range(1, count):
        give = lax.dynamic_index_in_dim(block, (here + step) % count, 0, False)
        total = total + ahead(give, "gx", step).astype(jnp.float32)
    mine = total.astype(jnp.bfloat16)
    bit = 2
    while bit < lax.axis_size("dp"):
        mine = (mine.astype(jnp.float32) + swap(mine, "dp", bit).astype(jnp.float32)).astype(jnp.bfloat16)
        bit *= 2
    return pair_rows(mine, swap(mine, "dp", 1)).reshape(-1, columns).astype(jnp.float32)


def split_columns(whole):
    count = lax.axis_size("gy")
    here = lax.axis_index("gy")
    columns = whole.shape[1] // count
    if count == 2:
        first, second = whole[:, :columns], whole[:, columns:]
        swapped = here == 1
        return [jnp.where(swapped, second, first), jnp.where(swapped, first, second)]
    return [
        lax.dynamic_slice_in_dim(whole, (here - step) % count * columns, columns, 1)
        for step in range(count)
    ]


def own_vector(vector):
    count = lax.axis_size("gy")
    here = lax.axis_index("gy")
    pieces = vector.reshape(count, -1)
    return [lax.dynamic_index_in_dim(pieces, (here - step) % count, 0, False) for step in range(count)]


def order_vector(pieces):
    count = lax.axis_size("gy")
    here = lax.axis_index("gy")
    out = jnp.zeros((count,) + pieces[0].shape, pieces[0].dtype)
    for step, piece in enumerate(pieces):
        out = lax.dynamic_update_index_in_dim(out, piece, (here - step) % count, 0)
    return out.reshape(-1)


def all_tokens(own):
    count = lax.axis_size("gy")
    here = lax.axis_index("gy")
    if count != 2:
        return lax.all_gather(own, "gy", axis=0, tiled=True)
    other = swap(own, "gy", 1)
    first = here == 0
    return jnp.concatenate([jnp.where(first, own, other), jnp.where(first, other, own)], axis=0)


def own_tokens_sum(whole):
    count = lax.axis_size("gy")
    here = lax.axis_index("gy")
    rows = whole.shape[0] // count
    if count != 2:
        return lax.psum_scatter(
            whole.astype(jnp.bfloat16), "gy", scatter_dimension=0, tiled=True
        ).astype(jnp.float32)
    give = lax.dynamic_slice_in_dim(whole, (1 - here) * rows, rows, 0)
    keep = lax.dynamic_slice_in_dim(whole, here * rows, rows, 0)
    return keep + swap(give.astype(jnp.bfloat16), "gy", 1).astype(jnp.float32)


def dot(a, b):
    return jnp.dot(a, b, preferred_element_type=jnp.float32)


def local(
    prompt,
    continuations,
    prefix_len,
    attn_gain,
    attn_shift,
    qkv_weight,
    query_bias,
    value_bias,
    out_weight,
    out_bias,
    mlp_gain,
    mlp_shift,
    up_weight,
    up_bias,
    down_weight,
    down_bias,
    grad_prompt,
    grad_continuations,
):
    groups, shard, width = prompt.shape
    length = continuations.shape[1]
    first_pos = lax.axis_index("gy") * shard
    prompt_len = shard * lax.axis_size("gy")
    block = min(512, shard)
    places = [first_pos + start for start in range(0, shard, block)] + [prefix_len[0]]
    places = jnp.stack(places).astype(jnp.int32)

    qkv = gather_ordered(qkv_weight)
    qkv_split = [qkv[:, :width], qkv[:, width : 2 * width], qkv[:, 2 * width :]]
    own_prompt = prompt.reshape(shard, width)
    branch = continuations.reshape(length, width)
    whole_prompt = all_tokens(own_prompt)
    out_full = gather_ordered(out_weight)
    up_parts = gather_parts(up_weight)
    down_parts = gather_parts(down_weight.T)

    token_rows = jnp.concatenate([own_prompt, branch], axis=0).astype(jnp.float32)
    normed_one, norm_one_back = jax.vjp(layer_norm, token_rows, attn_gain, attn_shift)
    act_one = normed_one.astype(jnp.bfloat16)
    key_rows = jnp.concatenate([whole_prompt, branch], axis=0).astype(jnp.float32)
    key_act = layer_norm(key_rows, attn_gain, attn_shift).astype(jnp.bfloat16)
    queries = (dot(act_one, qkv_split[0]) + query_bias).astype(jnp.bfloat16)
    keys = dot(key_act, qkv_split[1]).astype(jnp.bfloat16)
    values = (dot(key_act, qkv_split[2]) + value_bias).astype(jnp.bfloat16)
    parts_in = (queries, keys[:prompt_len], values[:prompt_len], keys[prompt_len:], values[prompt_len:])
    mixed, stats = attention_forward(places, *parts_in, block)

    resid = token_rows + (dot(mixed, out_full) + out_bias)
    normed_two, norm_two_back = jax.vjp(layer_norm, resid, mlp_gain, mlp_shift)
    act_two = normed_two.astype(jnp.bfloat16)
    result = resid + down_bias
    hidden_parts, gates_back = [], []
    for up_part, down_part, bias in zip(up_parts, down_parts, own_vector(up_bias)):
        pre_act = dot(act_two, up_part) + bias
        hidden_exact, gate_back = jax.vjp(smooth_gate, pre_act)
        hidden_parts.append(hidden_exact.astype(jnp.bfloat16))
        gates_back.append(gate_back)
        result = result + nt(hidden_parts[-1], down_part)
    prompt_out = result[:shard].reshape(groups, shard, width).astype(jnp.bfloat16)
    continuation_out = result[shard:].reshape(1, length, width).astype(jnp.bfloat16)

    cotangent = jnp.concatenate(
        [grad_prompt.reshape(shard, width), grad_continuations.reshape(length, width)], axis=0
    )
    cot_exact = cotangent.astype(jnp.float32)
    down_bias_grad = jnp.sum(cot_exact, axis=0)
    down_grads, up_grads, bias_grads = [], [], []
    d_act_two = 0.0
    for hidden, gate_back, up_part, down_part in zip(hidden_parts, gates_back, up_parts, down_parts):
        down_grads.append(tn(cotangent, hidden).astype(jnp.bfloat16))
        d_pre = gate_back(dot(cotangent, down_part))[0].astype(jnp.bfloat16)
        up_grads.append(tn(act_two, d_pre).astype(jnp.bfloat16))
        bias_grads.append(jnp.sum(d_pre.astype(jnp.float32), axis=0))
        d_act_two = d_act_two + nt(d_pre, up_part)
    down_total = scatter_parts(down_grads).T
    up_total = scatter_parts(up_grads)
    up_bias_grad = order_vector(bias_grads)
    resid_part, mlp_gain_grad, mlp_shift_grad = norm_two_back(d_act_two)
    d_resid = cot_exact + resid_part
    d_branch = d_resid.astype(jnp.bfloat16)
    out_total = scatter_parts(split_columns(tn(mixed, d_branch).astype(jnp.bfloat16)))
    out_bias_grad = jnp.sum(d_branch.astype(jnp.float32), axis=0)
    d_mixed = nt(d_branch, out_full).astype(jnp.bfloat16)
    d_queries, dk, dv, dkb, dvb = attention_backward(places, *parts_in, mixed, d_mixed, stats, block)

    d_keys = jnp.concatenate([dk, dkb], axis=0)
    d_values = jnp.concatenate([dv, dvb], axis=0)
    d_key_act = nt(d_keys, qkv_split[1]) + nt(d_values, qkv_split[2])
    shared = own_tokens_sum(d_key_act[:prompt_len])
    qkv_grad = jnp.concatenate([tn(act_one, d_queries), tn(key_act, d_keys), tn(key_act, d_values)], axis=1)
    qkv_total = scatter_parts(split_columns(qkv_grad.astype(jnp.bfloat16)))
    query_bias_grad = jnp.sum(d_queries.astype(jnp.float32), axis=0)
    value_bias_grad = jnp.sum(d_values.astype(jnp.float32), axis=0)
    d_act_one = nt(d_queries, qkv_split[0]) + jnp.concatenate([shared, d_key_act[prompt_len:]], axis=0)
    rows_part, attn_gain_grad, attn_shift_grad = norm_one_back(d_act_one)
    d_rows = d_resid + rows_part
    prompt_grad = d_rows[:shard].reshape(groups, shard, width)
    continuation_grad = d_rows[shard:].reshape(1, length, width)
    vectors = (
        attn_gain_grad,
        attn_shift_grad,
        query_bias_grad,
        value_bias_grad,
        out_bias_grad,
        mlp_gain_grad,
        mlp_shift_grad,
        up_bias_grad,
        down_bias_grad,
    )
    joined = total_over(jnp.concatenate(vectors), ("dp", "gy", "gx"))
    totals = []
    at = 0
    for vector in vectors:
        totals.append(joined[at : at + vector.shape[0]])
        at += vector.shape[0]
    return (
        prompt_out,
        continuation_out,
        prompt_grad,
        continuation_grad,
        totals[0],
        totals[1],
        qkv_total,
        totals[2],
        totals[3],
        out_total,
        totals[4],
        totals[5],
        totals[6],
        up_total,
        totals[7],
        down_total,
        totals[8],
    )


def solution(mesh):
    placed = (
        P(("dp", "gx"), "gy", None),
        P(("dp", "gx", "gy"), None, None),
        P(("dp", "gx", "gy")),
        P(),
        P(),
        P("gx", "gy"),
        P(),
        P(),
        P("gx", "gy"),
        P(),
        P(),
        P(),
        P("gx", "gy"),
        P(),
        P("gy", "gx"),
        P(),
        P(("dp", "gx"), "gy", None),
        P(("dp", "gx", "gy"), None, None),
    )
    return jax.shard_map(
        local,
        mesh=mesh,
        in_specs=placed,
        out_specs=(
            P(("dp", "gx"), "gy", None),
            P(("dp", "gx", "gy"), None, None),
            P(("dp", "gx"), "gy", None),
            P(("dp", "gx", "gy"), None, None),
            P(),
            P(),
            P("gx", "gy"),
            P(),
            P(),
            P("gx", "gy"),
            P(),
            P(),
            P(),
            P("gx", "gy"),
            P(),
            P("gy", "gx"),
            P(),
        ),
        check_vma=False,
    )
```

```python
import functools
import jax
import jax.numpy as jnp
from jax import lax
from jax.sharding import PartitionSpec as P
from jax.experimental import pallas as pl
from jax.experimental.pallas import tpu as pltpu

HEAD_DIM = 64
LOG2E = 1.4426950408889634
NEG = -1e30
BK = 512


def nt(a, b):
    return lax.dot_general(a, b, (((1,), (1,)), ((), ())), preferred_element_type=jnp.float32)


def nn(a, b):
    return jnp.dot(a, b, preferred_element_type=jnp.float32)


def tn(a, b):
    return lax.dot_general(a, b, (((0,), (0,)), ((), ())), preferred_element_type=jnp.float32)


def halves(pair, total):
    lane = lax.broadcasted_iota(jnp.int32, (1, 128), 1)
    left = jnp.minimum(total - pair * 128, 128)
    return lane < 64, jnp.logical_and(lane >= 64, lane < left), lane < left


def norm_bounds(ref, valid, spread):
    part = jnp.where(valid, ref[...], jnp.zeros((), jnp.bfloat16))
    return jnp.max(nn(part * part, spread), axis=0, keepdims=True)


def query_rows(pos, number, size, span, is_branch):
    if is_branch:
        return pl.ds(span, size)
    return pl.ds(pl.multiple_of(pos[number], size), size)


def forward_kernel(pos, q, k, v, *rest, block, branch, width):
    o, lse, va, vc, vab, vcb, tops, accs = rest[-8:]
    pair = pl.program_id(0)
    scale = HEAD_DIM ** (-0.5) * LOG2E
    low, high, valid = halves(pair, width)
    zero = jnp.zeros((), jnp.bfloat16)
    one = jnp.ones((), jnp.bfloat16)
    span = k.shape[0] - branch
    for part, first, second in ((slice(0, span), va, vc), (slice(span, None), vab, vcb)):
        whole = v[part, :]
        first[...] = jnp.where(low, whole, one)
        second[...] = jnp.where(low, one, jnp.where(high, whole, zero))
    spread = (
        (lax.broadcasted_iota(jnp.int32, (128, 128), 0) < 64)
        == (lax.broadcasted_iota(jnp.int32, (128, 128), 1) < 64)
    ).astype(jnp.bfloat16)
    bound = jnp.max(norm_bounds(k, valid, spread) * norm_bounds(q, valid, spread)) * (scale * scale)
    plain = bound < 90.0 * 90.0
    rows = o.shape[0]
    blocks = [(start, block, False) for start in range(0, rows - branch, block)]
    blocks.append((rows - branch, branch, True))

    def finish(start, size, acc_a, acc_b, top):
        total = pltpu.roll(jnp.where(low, acc_b, acc_a), 64, 1)
        o[start : start + size, :] = (jnp.where(low, acc_a, acc_b) / total).astype(o.dtype)
        turned = (top + jnp.log2(total)).T
        lse[0, 0:1, start : start + size] = turned[0:1, :]
        lse[0, 1:2, start : start + size] = turned[64:65, :]

    def setup(number, start, size, is_branch):
        at = pos[number]
        query = q[query_rows(pos, number, size, span, is_branch), :]
        queries = (jnp.where(low, query, zero), jnp.where(high, query, zero))
        row = lax.broadcasted_iota(jnp.int32, (size, BK), 0)
        column = lax.broadcasted_iota(jnp.int32, (size, BK), 1)
        triangle = lax.broadcasted_iota(jnp.int32, (size, size), 1) <= lax.broadcasted_iota(
            jnp.int32, (size, size), 0
        )
        whole_blocks = at // BK

        def allowed(index):
            if is_branch:
                return column + index * BK < at
            return column + index * BK <= row + at

        end = (at + BK - 1) // BK if is_branch else whole_blocks + 1
        return queries, triangle, whole_blocks, allowed, end

    def read(index):
        rows_at = pl.ds(pl.multiple_of(index * BK, BK), BK)
        return jnp.where(valid, k[rows_at, :], zero), va[rows_at, :], vc[rows_at, :]

    def own():
        return jnp.where(valid, k[span:, :], zero), vab[...], vcb[...]

    @pl.when(plain)
    def _():
        for number, (start, size, is_branch) in enumerate(blocks):
            queries, triangle, whole_blocks, allowed, end = setup(number, start, size, is_branch)

            def step(key, first, second, carry, mask):
                out = []
                for query_h, value_h, acc in zip(queries, (first, second), carry):
                    probs = jnp.exp2(nt(query_h, key) * scale)
                    if mask is not None:
                        probs = jnp.where(mask, probs, 0.0)
                    out.append(acc + nn(probs.astype(jnp.bfloat16), value_h))
                return tuple(out)

            carry = (jnp.zeros((size, 128), jnp.float32),) * 2
            carry = lax.fori_loop(0, whole_blocks, lambda i, c: step(*read(i), c, None), carry)
            if is_branch:
                carry = lax.fori_loop(
                    whole_blocks, end, lambda i, c: step(*read(i), c, allowed(i)), carry
                )
                carry = step(*own(), carry, triangle)
            else:
                carry = step(*read(whole_blocks), carry, allowed(whole_blocks))
            finish(start, size, *carry, 0.0)

    @pl.when(jnp.logical_not(plain))
    def _():
        for number, (start, size, is_branch) in enumerate(blocks):
            queries, triangle, whole_blocks, allowed, end = setup(number, start, size, is_branch)

            def step(key, first, second, mask):
                for head, value_h in enumerate((first, second)):
                    top = tops[head, 0:size, :]
                    scores = jnp.where(mask, nt(queries[head], key), NEG)
                    new_top = jnp.maximum(top, jnp.max(scores, axis=1, keepdims=True))
                    probs = jnp.exp2((scores - new_top[:, 0:1]) * scale).astype(jnp.bfloat16)
                    fade = jnp.exp2((top - new_top) * scale)
                    accs[head, 0:size, :] = accs[head, 0:size, :] * fade + nn(probs, value_h)
                    tops[head, 0:size, :] = new_top

            accs[:, 0:size, :] = jnp.zeros((2, size, 128), jnp.float32)
            tops[:, 0:size, :] = jnp.full((2, size, 128), NEG, jnp.float32)

            @pl.loop(0, end)
            def _(index):
                step(*read(index), allowed(index))

            if is_branch:
                step(*own(), triangle)
            top = jnp.where(low, tops[0, 0:size, :], tops[1, 0:size, :]) * scale
            finish(start, size, accs[0, 0:size, :], accs[1, 0:size, :], top)


def busy(microseconds):
    return pl.CostEstimate(
        flops=int(microseconds * 1.0e9), bytes_accessed=int(microseconds * 1.0e6), transcendentals=0
    )


def attention_forward(pos, q, k, v, block, branch, after=()):
    total, width = q.shape
    span = total - branch
    rows = block * (pos.shape[0] - 1) + branch
    pairs = pl.cdiv(width, 128)

    def col(n):
        return pl.BlockSpec((n, 128), lambda p, pos: (0, p))

    return pl.pallas_call(
        functools.partial(forward_kernel, block=block, branch=branch, width=width),
        grid_spec=pltpu.PrefetchScalarGridSpec(
            num_scalar_prefetch=1,
            grid=(pairs,),
            in_specs=[col(total)] * 3 + [pl.BlockSpec(memory_space=pl.ANY)] * len(after),
            out_specs=[col(rows), pl.BlockSpec((1, 8, rows), lambda p, pos: (p, 0, 0))],
            scratch_shapes=[
                pltpu.VMEM((span, 128), jnp.bfloat16),
                pltpu.VMEM((span, 128), jnp.bfloat16),
                pltpu.VMEM((branch, 128), jnp.bfloat16),
                pltpu.VMEM((branch, 128), jnp.bfloat16),
                pltpu.VMEM((2, max(block, branch), 128), jnp.float32),
                pltpu.VMEM((2, max(block, branch), 128), jnp.float32),
            ],
        ),
        out_shape=[
            jax.ShapeDtypeStruct((rows, width), jnp.bfloat16),
            jax.ShapeDtypeStruct((pairs, 8, rows), jnp.float32),
        ],
        compiler_params=pltpu.CompilerParams(
            dimension_semantics=("arbitrary",), vmem_limit_bytes=32 * 2**20
        ),
        cost_estimate=busy(7 * pairs),
        name="attention_forward",
    )(pos, q, k, v, *after)


def backward_kernel(pos, q, k, v, o, do, lse, *rest, block, branch, width):
    dq, dk, dv = rest[-13:-10]
    kta, ktc, kam, vm, ktab, ktcb, kbm, vbm, dks, dvs = rest[-10:]
    pair = pl.program_id(0)
    scale = HEAD_DIM ** (-0.5)
    low, high, valid = halves(pair, width)
    zero = jnp.zeros((), jnp.bfloat16)
    span = k.shape[0] - branch
    prompt_part, branch_part = slice(0, span), slice(span, None)
    for part, whole_ref, turn_a, turn_b in ((prompt_part, kam, kta, ktc), (branch_part, kbm, ktab, ktcb)):
        whole = jnp.where(valid, k[part, :], zero)
        whole_ref[...] = whole
        turned = whole.T
        turn_a[...] = turned[0:64, :]
        turn_b[...] = turned[64:128, :]
    vm[...] = jnp.where(valid, v[prompt_part, :], zero)
    vbm[...] = jnp.where(valid, v[branch_part, :], zero)
    dq[...] = jnp.zeros_like(dq)
    dks[...] = jnp.zeros_like(dks)
    dvs[...] = jnp.zeros_like(dvs)
    rows = o.shape[0]
    blocks = [(start, block, False) for start in range(0, rows - branch, block)]
    blocks.append((rows - branch, branch, True))
    ones_a = jnp.broadcast_to(low, (8, 128)).astype(jnp.bfloat16)
    ones_b = jnp.broadcast_to(high, (8, 128)).astype(jnp.bfloat16)
    for number, (start, size, is_branch) in enumerate(blocks):
        at = pos[number]
        here = slice(start, start + size)
        query_at = query_rows(pos, number, size, span, is_branch)
        query = q[query_at, :]
        grad = do[here, :]
        queries = (jnp.where(low, query, zero), jnp.where(high, query, zero))
        grads = (jnp.where(low, grad, zero), jnp.where(high, grad, zero))
        product = jnp.where(valid, grad.astype(jnp.float32) * o[here, :].astype(jnp.float32), 0.0)
        upper = product.astype(jnp.bfloat16)
        lower = (product - upper.astype(jnp.float32)).astype(jnp.bfloat16)
        deltas = tuple((nt(m, upper) + nt(m, lower))[0:1, :] for m in (ones_a, ones_b))
        stats = (lse[0, 0:1, here], lse[0, 1:2, here])
        queries_cat = jnp.concatenate(queries, axis=0)
        grads_cat = jnp.concatenate(grads, axis=0)

        def step(key, value, first, second, mask):
            probs, dscores = [], []
            for query_h, grad_h, delta, stat in zip(queries, grads, deltas, stats):
                scores = nt(key, query_h)
                prob = jnp.exp2(scores * (scale * LOG2E) - stat)
                if mask is not None:
                    prob = jnp.where(mask, prob, 0.0)
                dprob = nt(value, grad_h)
                probs.append(prob.astype(jnp.bfloat16))
                dscores.append((prob * (dprob - delta)).astype(jnp.bfloat16))
            dscores_cat = jnp.concatenate(dscores, axis=1)
            dvalue = nn(jnp.concatenate(probs, axis=1), grads_cat)
            dkey = nn(dscores_cat, queries_cat)
            dquery = jnp.concatenate([nn(first, dscores[0]), nn(second, dscores[1])], axis=0)
            return dquery, dkey, dvalue

        def read(base):
            rows_at = pl.ds(pl.multiple_of(base, BK), BK)
            return kam[rows_at, :], vm[rows_at, :], kta[:, rows_at], ktc[:, rows_at]

        def accumulate(index, carry, mask):
            rows_at = pl.ds(pl.multiple_of(index * BK, BK), BK)
            dquery, dkey, dvalue = step(*read(index * BK), mask)
            dks[rows_at, :] += dkey
            dvs[rows_at, :] += dvalue
            return carry + dquery

        carry = jnp.zeros((128, size), jnp.float32)
        whole_blocks = at // BK
        carry = lax.fori_loop(0, whole_blocks, lambda i, c: accumulate(i, c, None), carry)
        row = lax.broadcasted_iota(jnp.int32, (BK, size), 0)
        column = lax.broadcasted_iota(jnp.int32, (BK, size), 1)
        if is_branch:
            carry = lax.fori_loop(
                whole_blocks,
                (at + BK - 1) // BK,
                lambda i, c: accumulate(i, c, row + i * BK < at),
                carry,
            )
            triangle = lax.broadcasted_iota(jnp.int32, (size, size), 0) <= lax.broadcasted_iota(
                jnp.int32, (size, size), 1
            )
            dquery, dkey, dvalue = step(kbm[...], vbm[...], ktab[...], ktcb[...], triangle)
            carry = carry + dquery
            dk[branch_part, :] = (dkey * scale).astype(dk.dtype)
            dv[branch_part, :] = dvalue.astype(dv.dtype)
        else:
            carry = accumulate(whole_blocks, carry, row + whole_blocks * BK <= column + at)
        dq[query_at, :] = (carry.T * scale).astype(dq.dtype)
    dk[prompt_part, :] = (dks[...] * scale).astype(dk.dtype)
    dv[prompt_part, :] = dvs[...].astype(dv.dtype)


def attention_backward(pos, q, k, v, o, do, lse, block, branch, after=()):
    total, width = q.shape
    span = total - branch
    rows = o.shape[0]
    pairs = pl.cdiv(width, 128)

    def col(n):
        return pl.BlockSpec((n, 128), lambda p, pos: (0, p))

    def scratch(n):
        wide = pltpu.VMEM((64, n), jnp.bfloat16)
        tall = pltpu.VMEM((n, 128), jnp.bfloat16)
        return [wide, wide, tall, tall]

    return pl.pallas_call(
        functools.partial(backward_kernel, block=block, branch=branch, width=width),
        grid_spec=pltpu.PrefetchScalarGridSpec(
            num_scalar_prefetch=1,
            grid=(pairs,),
            in_specs=[col(total)] * 3
            + [col(rows)] * 2
            + [pl.BlockSpec((1, 8, rows), lambda p, pos: (p, 0, 0))]
            + [pl.BlockSpec(memory_space=pl.ANY)] * len(after),
            out_specs=[col(total)] * 3,
            scratch_shapes=scratch(span)
            + scratch(branch)
            + [pltpu.VMEM((span, 128), jnp.float32), pltpu.VMEM((span, 128), jnp.float32)],
        ),
        out_shape=[jax.ShapeDtypeStruct((total, width), jnp.bfloat16)] * 3,
        compiler_params=pltpu.CompilerParams(
            dimension_semantics=("arbitrary",), vmem_limit_bytes=40 * 2**20
        ),
        cost_estimate=busy(10 * pairs),
        name="attention_backward",
    )(pos, q, k, v, o, do, lse, *after)


TILE = 256


def mlp_forward_kernel(act, resid, up, up_bias, down, down_bias, *rest):
    hidden, slope, result, acc = rest[-4:]
    step = pl.program_id(0)

    @pl.when(step == 0)
    def _():
        acc[...] = resid[...] + down_bias[...]

    rows = act.shape[0]
    size = 256 if rows % 256 == 0 else rows
    for start in range(0, rows, size):
        here = slice(start, start + size)
        pre = nn(act[here, :], up[...]) + up_bias[...]
        bell = jnp.exp(pre * pre * -0.5)
        t = 1.0 / (1.0 + (0.3275911 * 0.7071067811865476) * jnp.abs(pre))
        series = t * (
            0.127414796 + t * (-0.142248368 + t * (0.7107068705 + t * (-0.7265760135 + t * 0.5307027145)))
        )
        tail = series * bell
        below = jnp.where(pre >= 0.0, 1.0 - tail, tail)
        exact = (pre * below).astype(jnp.bfloat16)
        hidden[here, :] = exact
        slope[here, :] = (below + pre * bell * 0.3989422804014327).astype(jnp.bfloat16)
        acc[here, :] += nt(exact, down[...])

    @pl.when(step == pl.num_programs(0) - 1)
    def _():
        result[...] = acc[...].astype(result.dtype)


def whole_block(shape):
    return pl.BlockSpec(shape, lambda j: (0,) * len(shape))


def mlp_forward(act, resid, up, up_bias, down, down_bias, after=()):
    rows, width = act.shape
    inner = up.shape[1]
    column = pl.BlockSpec((width, TILE), lambda j: (0, j))
    tall = pl.BlockSpec((rows, TILE), lambda j: (0, j))
    return pl.pallas_call(
        mlp_forward_kernel,
        grid=(inner // TILE,),
        in_specs=[
            whole_block((rows, width)),
            whole_block((rows, width)),
            column,
            pl.BlockSpec((1, TILE), lambda j: (0, j)),
            column,
            whole_block((1, width)),
        ]
        + [pl.BlockSpec(memory_space=pl.ANY)] * len(after),
        out_specs=[tall, tall, whole_block((rows, width))],
        out_shape=[
            jax.ShapeDtypeStruct((rows, inner), jnp.bfloat16),
            jax.ShapeDtypeStruct((rows, inner), jnp.bfloat16),
            jax.ShapeDtypeStruct((rows, width), jnp.bfloat16),
        ],
        scratch_shapes=[pltpu.VMEM((rows, width), jnp.float32)],
        compiler_params=pltpu.CompilerParams(
            dimension_semantics=("arbitrary",), vmem_limit_bytes=44 * 2**20
        ),
        cost_estimate=busy(40),
        name="mlp_forward",
    )(act, resid, up, up_bias.reshape(1, inner), down, down_bias.reshape(1, width), *after)


def mlp_backward_kernel(act, cot, hidden, slope, up, down, *rest):
    d_act, up_grad, down_grad, bias_grad, act_turned, cot_turned = rest[-6:]
    step = pl.program_id(0)

    @pl.when(step == 0)
    def _():
        act_turned[...] = act[...].T
        cot_turned[...] = cot[...].T
        d_act[...] = jnp.zeros_like(d_act)

    rows = act.shape[0]
    size = 256 if rows % 256 == 0 else rows
    bias = jnp.zeros((1, TILE), jnp.float32)
    pieces = []
    for start in range(0, rows, size):
        here = slice(start, start + size)
        d_pre = (nn(cot[here, :], down[...]) * slope[here, :].astype(jnp.float32)).astype(jnp.bfloat16)
        bias = bias + jnp.sum(d_pre.astype(jnp.float32), axis=0, keepdims=True)
        d_act[here, :] += nt(d_pre, up[...])
        pieces.append(d_pre)
    bias_grad[...] = bias
    up_grad[...] = nn(act_turned[...], jnp.concatenate(pieces, axis=0)).astype(jnp.bfloat16)
    down_grad[...] = nn(cot_turned[...], hidden[...]).astype(jnp.bfloat16)


def mlp_backward(act, cot, hidden, slope, up, down, after=()):
    rows, width = act.shape
    inner = up.shape[1]
    column = pl.BlockSpec((width, TILE), lambda j: (0, j))
    tall = pl.BlockSpec((rows, TILE), lambda j: (0, j))
    return pl.pallas_call(
        mlp_backward_kernel,
        grid=(inner // TILE,),
        in_specs=[whole_block((rows, width)), whole_block((rows, width)), tall, tall, column, column]
        + [pl.BlockSpec(memory_space=pl.ANY)] * len(after),
        out_specs=[
            whole_block((rows, width)),
            column,
            column,
            pl.BlockSpec((1, TILE), lambda j: (0, j)),
        ],
        out_shape=[
            jax.ShapeDtypeStruct((rows, width), jnp.float32),
            jax.ShapeDtypeStruct((width, inner), jnp.bfloat16),
            jax.ShapeDtypeStruct((width, inner), jnp.bfloat16),
            jax.ShapeDtypeStruct((1, inner), jnp.float32),
        ],
        scratch_shapes=[
            pltpu.VMEM((width, rows), jnp.bfloat16),
            pltpu.VMEM((width, rows), jnp.bfloat16),
        ],
        compiler_params=pltpu.CompilerParams(
            dimension_semantics=("arbitrary",), vmem_limit_bytes=48 * 2**20
        ),
        cost_estimate=busy(60),
        name="mlp_backward",
    )(act, cot, hidden, slope, up, down, *after)


def gate_kernel(*refs):
    pass


def gate(value, after):
    if not after:
        return value
    anywhere = pl.BlockSpec(memory_space=pl.ANY)
    return pl.pallas_call(
        gate_kernel,
        in_specs=[anywhere] * (1 + len(after)),
        out_specs=anywhere,
        out_shape=jax.ShapeDtypeStruct(value.shape, value.dtype),
        input_output_aliases={0: 0},
        cost_estimate=busy(1),
        name="gate",
    )(value, *after)


GROUP = 512

epsilon = 1e-05


def normalise(values_in):
    centre = jnp.mean(values_in, axis=-1, keepdims=True)
    centred = values_in - centre
    spread = jnp.mean(centred * centred, axis=-1, keepdims=True)
    pace = lax.rsqrt(spread + epsilon)
    return centred * pace, pace


def norm_back(grad, norm, pace, gain):
    scaled = grad * gain
    return pace * (
        scaled
        - jnp.mean(scaled, axis=-1, keepdims=True)
        - norm * jnp.mean(scaled * norm, axis=-1, keepdims=True)
    )


def swap(value, axis, bit):
    count = lax.axis_size(axis)
    return lax.ppermute(value, axis, [(i, i ^ bit) for i in range(count)])


def ahead(value, axis, step):
    count = lax.axis_size(axis)
    return lax.ppermute(value, axis, [(i, (i + step) % count) for i in range(count)])


def total_over(value, axes):
    for axis in axes:
        count = lax.axis_size(axis)
        if count & (count - 1):
            value = lax.psum(value, axis)
            continue
        bit = 1
        while bit < count:
            value = value + swap(value, axis, bit)
            bit *= 2
    return value


def by_halves(half_width):
    return lax.axis_size("dp") == 4 and lax.axis_size("gy") == 2 and half_width > GROUP


def half_index():
    return lax.axis_index("dp") % 2


def pair_rows(mine, theirs):
    first = half_index() == 0
    return jnp.stack([jnp.where(first, mine, theirs), jnp.where(first, theirs, mine)], axis=-3)


def gather_plain(part):
    part = lax.all_gather(part, "gy", axis=1, tiled=True)
    return lax.all_gather(part, "gx", axis=0, tiled=True)


def gather_quarters(part):
    rows, columns = part.shape
    copies, gx, gy = (lax.axis_size(axis) for axis in ("dp", "gx", "gy"))
    size = columns // copies
    mine = lax.dynamic_slice_in_dim(part, lax.axis_index("dp") * size, size, 1)
    raw = lax.all_gather(mine, ("dp", "gx", "gy"))
    got = raw.reshape(copies, gx, gy, rows, size)
    return raw, [
        [got[quarter, :, side].reshape(gx * rows, size) for quarter in range(copies)]
        for side in range(gy)
    ]


def gather_projections(qkv_part, out_part, width):
    rows = qkv_part.shape[0]
    half = width // 2
    first_side = lax.axis_index("gy") == 0
    key_at = width - half
    here = jnp.where(
        first_side,
        qkv_part[:, :GROUP],
        qkv_part[:, half : half + GROUP],
    )
    keys_here = jnp.where(first_side, qkv_part[:, width : width + GROUP], qkv_part[:, :GROUP])
    raw, one = gather_quarters(jnp.concatenate([here, keys_here], axis=1))
    rest = width - GROUP
    spare = half - GROUP
    queries_rest = jnp.where(first_side, qkv_part[:, GROUP:width], qkv_part[:, half + GROUP :])
    keys_rest = jnp.where(first_side, qkv_part[:, width + GROUP :], qkv_part[:, GROUP:half])

    def pad(value, size):
        return jnp.pad(value, ((0, 0), (0, size - value.shape[1])))

    outer = pl.cdiv(rest + spare, 128) * 128
    out_size = pl.cdiv(half, 128) * 128
    total = pl.cdiv(outer + out_size, 512) * 512
    packed = pad(jnp.concatenate([queries_rest, keys_rest], axis=1), outer)
    packed = pad(jnp.concatenate([packed, pad(out_part, out_size)], axis=1), total)
    two = [jnp.concatenate(side, axis=1) for side in gather_quarters(packed)[1]]
    first = [
        jnp.concatenate(one[0][:2], axis=1),
        jnp.concatenate(one[0][2:], axis=1),
        jnp.concatenate(one[1][:2], axis=1),
    ]
    second = [
        two[0][:, :rest],
        jnp.concatenate(
            [two[0][:, rest : rest + spare]] + one[1][2:] + [two[1][:, rest : rest + spare]], axis=1
        ),
        two[1][:, :rest],
    ]
    out_full = jnp.concatenate([side[:, outer : outer + half] for side in two], axis=1)
    return [first, second], out_full, raw


def gather_feed_forward(up_part, down_part, after):
    columns = up_part.shape[1]
    shared = columns // 2 // 512 * 512
    _, quarters = gather_quarters(jnp.concatenate([up_part[:, :shared], down_part[:, :shared]], axis=1))
    first_half = half_index() == 0
    first_side = lax.axis_index("gy") == 0
    mine = gate(jnp.where(first_half, up_part[:, shared:], down_part[:, shared:]), after)
    rows, size = mine.shape
    count = lax.axis_size("gx")
    here = lax.axis_index("gx")
    blocks = jnp.zeros((count, rows, size), mine.dtype)
    for step in range(count):
        got = mine if step == 0 else ahead(mine, "gx", step)
        blocks = lax.dynamic_update_index_in_dim(blocks, got, (here - step) % count, 0)
    own = blocks.reshape(count * rows, size)
    theirs = swap(own, "gy", 1)
    sides = (jnp.where(first_side, own, theirs), jnp.where(first_side, theirs, own))
    others = [swap(side, "dp", 1) for side in sides]
    ups = [jnp.where(first_half, a, b) for a, b in zip(sides, others)]
    downs = [jnp.where(first_half, b, a) for a, b in zip(sides, others)]
    wholes = []
    for pieces, rest in ((slice(0, 2), ups), (slice(2, 4), downs)):
        wholes.append(
            jnp.concatenate([p for side in range(2) for p in quarters[side][pieces] + [rest[side]]], axis=1)
        )
    return wholes, own


def core_step(whole):
    count = lax.axis_size("gx")
    rows, columns = whole.shape
    pieces = whole.reshape(count, 2, rows // count // 2, columns)
    half = half_index()
    keep = lax.dynamic_index_in_dim(pieces, half, 1, False)
    give = lax.dynamic_index_in_dim(pieces, 1 - half, 1, False)
    return add(keep, swap(give, "dp", 1))


def add(a, b):
    return (a.astype(jnp.float32) + b.astype(jnp.float32)).astype(jnp.bfloat16)


def halves_step(value, axis, bit, here):
    size = value.shape[-1] // 2
    first, second = value[..., :size], value[..., size:]
    own_first = here == 0
    keep = jnp.where(own_first, first, second)
    give = jnp.where(own_first, second, first)
    return add(keep, swap(give, axis, bit))


def columns_step(value):
    return halves_step(value, "gy", 1, lax.axis_index("gy"))


def overlap_step(value):
    columns = value.shape[-1] // 2
    size = pl.cdiv(columns // 128, 2) * 128
    first, second = (
        jnp.concatenate([value[..., at : at + size], value[..., columns + at : columns + at + size]], axis=-1)
        for at in (0, columns - size)
    )
    own_first = lax.axis_index("dp") // 2 == 0
    return add(jnp.where(own_first, first, second), swap(jnp.where(own_first, second, first), "dp", 2))


def overlap_join(value, columns):
    size = value.shape[-1]
    other = swap(value, "dp", 2)
    own_first = lax.axis_index("dp") // 2 == 0
    first, second = jnp.where(own_first, value, other), jnp.where(own_first, other, value)
    return jnp.concatenate([first, second[..., 2 * size - columns :]], axis=-1)


def blocks_step(value):
    count = lax.axis_size("gx")
    here = lax.axis_index("gx")
    total = lax.dynamic_index_in_dim(value, here, 0, False).astype(jnp.float32)
    for step in range(1, count):
        give = lax.dynamic_index_in_dim(value, (here + step) % count, 0, False)
        total = total + ahead(give, "gx", step).astype(jnp.float32)
    return total.astype(jnp.bfloat16)


def copies_step(value):
    bit = 2
    while bit < lax.axis_size("dp"):
        value = add(value, swap(value, "dp", bit))
        bit *= 2
    return value


def join_step(value):
    columns = value.shape[-1]
    return pair_rows(value, swap(value, "dp", 1)).reshape(-1, columns).astype(jnp.float32)


def side_exchange(first, second):
    first_side = lax.axis_index("gy") == 0
    keep = jnp.where(first_side, first, second)
    return add(keep, swap(jnp.where(first_side, second, first), "gy", 1))


def rest_exchange(rest_flow, out_flow, width):
    rest = width - GROUP
    spare = width // 2 - GROUP
    query, key, value = (rest_flow[..., rest * kind : rest * (kind + 1)] for kind in range(3))
    return side_exchange(
        jnp.concatenate([query, key[..., :spare], out_flow[..., : width // 2]], axis=-1),
        jnp.concatenate([value, key[..., rest - spare :], out_flow[..., width // 2 :]], axis=-1),
    )


def first_exchange(first_flow, rest_flow, width):
    rest = width - GROUP
    spare = width // 2 - GROUP
    query, key, value = (first_flow[..., GROUP * kind : GROUP * (kind + 1)] for kind in range(3))
    return side_exchange(
        jnp.concatenate([query, key], axis=-1),
        jnp.concatenate([value, rest_flow[..., rest + spare : 2 * rest - spare]], axis=-1),
    )


def join_projections(first, second, width):
    rest = width - GROUP
    one, two = first[:, :GROUP], first[:, GROUP:]
    three, four = second[:, :rest], second[:, rest:]
    return jnp.where(
        lax.axis_index("gy") == 0,
        jnp.concatenate([one, three, two, four], axis=1),
        jnp.concatenate([two, four, one, three], axis=1),
    )


def scatter_plain(whole):
    part = lax.psum_scatter(whole, "gy", scatter_dimension=1, tiled=True)
    part = lax.psum_scatter(part, "gx", scatter_dimension=0, tiled=True)
    return lax.psum(part, "dp").astype(jnp.float32)


def all_tokens(own):
    count = lax.axis_size("gy")
    here = lax.axis_index("gy")
    if count != 2:
        return lax.all_gather(own, "gy", axis=0, tiled=True)
    other = swap(own, "gy", 1)
    first = here == 0
    return jnp.concatenate([jnp.where(first, own, other), jnp.where(first, other, own)], axis=0)


def own_tokens_sum(whole):
    count = lax.axis_size("gy")
    here = lax.axis_index("gy")
    rows = whole.shape[0] // count
    if count != 2:
        return lax.psum_scatter(
            whole.astype(jnp.bfloat16), "gy", scatter_dimension=0, tiled=True
        ).astype(jnp.float32)
    give = lax.dynamic_slice_in_dim(whole, (1 - here) * rows, rows, 0)
    keep = lax.dynamic_slice_in_dim(whole, here * rows, rows, 0)
    return keep + swap(give.astype(jnp.bfloat16), "gy", 1).astype(jnp.float32)


def dot(a, b):
    return jnp.dot(a, b, preferred_element_type=jnp.float32)


def local(
    prompt,
    continuations,
    prefix_len,
    attn_gain,
    attn_shift,
    qkv_weight,
    query_bias,
    value_bias,
    out_weight,
    out_bias,
    mlp_gain,
    mlp_shift,
    up_weight,
    up_bias,
    down_weight,
    down_bias,
    grad_prompt,
    grad_continuations,
):
    groups, shard, width = prompt.shape
    length = continuations.shape[1]
    first_pos = lax.axis_index("gy") * shard
    prompt_len = shard * lax.axis_size("gy")
    block = shard // 2
    halved = by_halves(width // 2)
    spans = [slice(0, GROUP), slice(GROUP, width)]

    if halved:
        limit, other_limit = prefix_len[0], swap(prefix_len, "gy", 1)[0]
        is_first = first_pos == 0
        is_long = jnp.logical_or(limit > other_limit, jnp.logical_and(limit == other_limit, is_first))
        kept_at = jnp.where(is_long, 0, block)
        places = [first_pos + kept_at, shard - first_pos + kept_at, limit]
    else:
        places = [first_pos, first_pos + block, prefix_len[0]]
    places = jnp.stack(places).astype(jnp.int32)

    def kept_rows(own):
        return lax.dynamic_slice_in_dim(own, kept_at, block, 0)

    def given_rows(own):
        return lax.dynamic_slice_in_dim(own, block - kept_at, block, 0)

    def back_home(done):
        if not halved:
            return done
        kept, home = done[:block], swap(done[block:], "gy", 1)
        return jnp.concatenate([jnp.where(is_long, kept, home), jnp.where(is_long, home, kept)], axis=0)

    own_prompt = prompt.reshape(shard, width)
    branch = continuations.reshape(length, width)
    own_cot = grad_prompt.reshape(shard, width)
    branch_cot = grad_continuations.reshape(length, width)
    whole_prompt = all_tokens(own_prompt)
    if halved:
        weights, out_full, raw = gather_projections(qkv_weight, out_weight, width)
        (up_full, down_full), fetched = gather_feed_forward(up_weight, down_weight.T, (raw,))
        fetched = (fetched,)
        other_cot = swap(gate(given_rows(own_cot), (raw,)), "gy", 1)
        cotangent = jnp.concatenate([kept_rows(own_cot), other_cot, branch_cot], axis=0)
    else:
        qkv = gather_plain(qkv_weight)
        weights = [[qkv[:, c.start + s : c.stop + s] for s in (0, width, 2 * width)] for c in spans]
        out_full, up_full, down_full = (gather_plain(w) for w in (out_weight, up_weight, down_weight.T))
        fetched = ()
        cotangent = jnp.concatenate([own_cot, branch_cot], axis=0)

    all_rows = jnp.concatenate([whole_prompt, branch], axis=0)
    norm_all, _ = normalise(all_rows.astype(jnp.float32))
    act_all = (norm_all * attn_gain + attn_shift).astype(jnp.bfloat16)
    projected, mixed, stats = [], [], []
    for number, (cols, (w_query, w_key, w_value)) in enumerate(zip(spans, weights)):
        projected.append(
            (
                (dot(act_all, w_query) + query_bias[cols]).astype(jnp.bfloat16),
                dot(act_all, w_key).astype(jnp.bfloat16),
                (dot(act_all, w_value) + value_bias[cols]).astype(jnp.bfloat16),
            )
        )
        got, stat = attention_forward(
            places, *projected[-1], block, length, fetched if number == 1 else ()
        )
        mixed.append(got)
        stats.append(stat)

    token_rows = jnp.concatenate(
        [lax.dynamic_slice_in_dim(whole_prompt, places[n], block, 0) for n in range(2)] + [branch], axis=0
    ).astype(jnp.float32)
    resid = token_rows + (sum(dot(m, out_full[c]) for m, c in zip(mixed, spans)) + out_bias)
    norm_two, pace_two = normalise(resid)
    act_two = (norm_two * mlp_gain + mlp_shift).astype(jnp.bfloat16)
    hidden, slope, result = mlp_forward(act_two, resid, up_full, up_bias, down_full, down_bias)
    prompt_out = back_home(result[:shard]).reshape(groups, shard, width)
    continuation_out = result[shard:].reshape(1, length, width)

    cot_exact = cotangent.astype(jnp.float32)
    down_bias_grad = jnp.sum(cot_exact, axis=0)
    d_act_two, up_grad, down_grad, up_bias_grad = mlp_backward(
        act_two, cotangent, hidden, slope, up_full, down_full
    )
    up_bias_grad = up_bias_grad.reshape(-1)
    after = ()
    if halved:
        up_flow, down_flow = core_step(up_grad), core_step(down_grad)
        after = (up_flow, down_flow)
    mlp_gain_grad = jnp.sum(d_act_two * norm_two, axis=0)
    mlp_shift_grad = jnp.sum(d_act_two, axis=0)
    d_resid = cot_exact + norm_back(d_act_two, norm_two, pace_two, mlp_gain)
    d_branch = d_resid.astype(jnp.bfloat16)
    out_grad = jnp.concatenate([tn(m, d_branch) for m in mixed], axis=0).astype(jnp.bfloat16)
    out_bias_grad = jnp.sum(d_branch.astype(jnp.float32), axis=0)
    d_act_all = 0.0
    grads, flows, bias_grads = [None, None], [None, None], [None, None]
    for number in (1, 0):
        cols = spans[number]
        d_mixed = nt(d_branch, out_full[cols]).astype(jnp.bfloat16)
        d_parts = list(
            attention_backward(
                places, *projected[number], mixed[number], d_mixed, stats[number], block, length, after
            )
        )
        if halved and number == 0:
            d_parts[0] = gate(d_parts[0], (up_flow, down_flow, rest_flow))
        for d_part, weight in zip(d_parts, weights[number]):
            d_act_all = d_act_all + nt(d_part, weight)
        grads[number] = jnp.concatenate([tn(act_all, d).astype(jnp.bfloat16) for d in d_parts], axis=1)
        bias_grads[number] = [jnp.sum(d_parts[n].astype(jnp.float32), axis=0) for n in (0, 2)]
        if halved and number == 1:
            joint = core_step(jnp.concatenate([grads[1], out_grad], axis=1))
            flows[1], out_flow = joint[..., :-width], joint[..., -width:]
            up_flow, down_flow = columns_step(up_flow), overlap_step(down_flow)
            after = (up_flow, down_flow, joint)
            up_flow, down_flow = blocks_step(up_flow), columns_step(down_flow)
            rest_flow = rest_exchange(flows[1], out_flow, width)
    shared = own_tokens_sum(d_act_all[:prompt_len])
    if halved:
        flows[0] = core_step(grads[0])
        first_flow = first_exchange(flows[0], flows[1], width)
        up_total = join_step(copies_step(up_flow))
        down_total = join_step(overlap_join(blocks_step(down_flow), up_weight.shape[1]))
        first_total, rest_total = (
            join_step(copies_step(blocks_step(f))) for f in (first_flow, rest_flow)
        )
        qkv_total = join_projections(first_total, rest_total[:, : -(width // 2)], width)
        out_total = rest_total[:, -(width // 2) :]
    else:
        qkv_grad = jnp.concatenate(
            [
                grads[n][:, kind * (c.stop - c.start) : (kind + 1) * (c.stop - c.start)]
                for kind in range(3)
                for n, c in enumerate(spans)
            ],
            axis=1,
        )
        up_total, down_total, out_total, qkv_total = (
            scatter_plain(g) for g in (up_grad, down_grad, out_grad, qkv_grad)
        )
    query_bias_grad, value_bias_grad = (
        jnp.concatenate([bias_grads[n][kind] for n in range(2)]) for kind in range(2)
    )
    attn_gain_grad = jnp.sum(d_act_all * norm_all, axis=0)
    attn_shift_grad = jnp.sum(d_act_all, axis=0)
    norm_own, pace_own = normalise(jnp.concatenate([own_prompt, branch], axis=0).astype(jnp.float32))
    d_act_own = jnp.concatenate([shared, d_act_all[prompt_len:]], axis=0)
    rows_part = norm_back(d_act_own, norm_own, pace_own, attn_gain)
    prompt_resid = d_resid[:shard]
    if halved:
        home = back_home(d_branch[:shard]).astype(jnp.float32)
        kept = jnp.where(is_long, prompt_resid[:block], home[:block]), jnp.where(
            is_long, home[block:], prompt_resid[:block]
        )
        prompt_resid = jnp.concatenate(kept, axis=0)
    d_rows = jnp.concatenate([prompt_resid, d_resid[shard:]], axis=0) + rows_part
    prompt_grad = d_rows[:shard].reshape(groups, shard, width)
    continuation_grad = d_rows[shard:].reshape(1, length, width)
    vectors = (
        attn_gain_grad,
        attn_shift_grad,
        query_bias_grad,
        value_bias_grad,
        out_bias_grad,
        mlp_gain_grad,
        mlp_shift_grad,
        up_bias_grad,
        down_bias_grad,
    )
    joined = total_over(jnp.concatenate(vectors), ("dp", "gy", "gx"))
    totals = []
    at = 0
    for vector in vectors:
        totals.append(joined[at : at + vector.shape[0]])
        at += vector.shape[0]
    return (
        prompt_out,
        continuation_out,
        prompt_grad,
        continuation_grad,
        totals[0],
        totals[1],
        qkv_total,
        totals[2],
        totals[3],
        out_total,
        totals[4],
        totals[5],
        totals[6],
        up_total,
        totals[7],
        down_total.T,
        totals[8],
    )


def solution(mesh):
    placed = (
        P(("dp", "gx"), "gy", None),
        P(("dp", "gx", "gy"), None, None),
        P(("dp", "gx", "gy")),
        P(),
        P(),
        P("gx", "gy"),
        P(),
        P(),
        P("gx", "gy"),
        P(),
        P(),
        P(),
        P("gx", "gy"),
        P(),
        P("gy", "gx"),
        P(),
        P(("dp", "gx"), "gy", None),
        P(("dp", "gx", "gy"), None, None),
    )
    return jax.shard_map(
        local,
        mesh=mesh,
        in_specs=placed,
        out_specs=(
            P(("dp", "gx"), "gy", None),
            P(("dp", "gx", "gy"), None, None),
            P(("dp", "gx"), "gy", None),
            P(("dp", "gx", "gy"), None, None),
            P(),
            P(),
            P("gx", "gy"),
            P(),
            P(),
            P("gx", "gy"),
            P(),
            P(),
            P(),
            P("gx", "gy"),
            P(),
            P("gy", "gx"),
            P(),
        ),
        check_vma=False,
    )
```

```python
import functools
import jax
import jax.numpy as jnp
from jax import lax
from jax.sharding import PartitionSpec as P
from jax.experimental import pallas as pl
from jax.experimental.pallas import tpu as pltpu

HEAD_DIM = 64
LOG2E = 1.4426950408889634
NEG = -1e30
BK = 512
GROUP = 512
epsilon = 1e-05


def nt(a, b):
    return lax.dot_general(a, b, (((1,), (1,)), ((), ())), preferred_element_type=jnp.float32)


def nn(a, b):
    return jnp.dot(a, b, preferred_element_type=jnp.float32)


def tn(a, b):
    return lax.dot_general(a, b, (((0,), (0,)), ((), ())), preferred_element_type=jnp.float32)


def halves(pair, total):
    lane = lax.broadcasted_iota(jnp.int32, (1, 128), 1)
    left = jnp.minimum(total - pair * 128, 128)
    return lane < 64, jnp.logical_and(lane >= 64, lane < left), lane < left


def norm_bounds(ref, valid, spread):
    part = jnp.where(valid, ref[...], jnp.zeros((), jnp.bfloat16))
    return jnp.max(nn(part * part, spread), axis=0, keepdims=True)


def query_rows(pos, number, size, span, is_branch):
    if is_branch:
        return pl.ds(span, size)
    return pl.ds(pl.multiple_of(pos[number], size), size)


def forward_kernel(pos, q, k, v, *rest, block, branch, width):
    o, lse, va, vc, vab, vcb, tops, accs = rest[-8:]
    pair = pl.program_id(0)
    scale = HEAD_DIM ** (-0.5) * LOG2E
    low, high, valid = halves(pair, width)
    zero = jnp.zeros((), jnp.bfloat16)
    one = jnp.ones((), jnp.bfloat16)
    span = k.shape[0] - branch
    for part, first, second in ((slice(0, span), va, vc), (slice(span, None), vab, vcb)):
        whole = v[part, :]
        first[...] = jnp.where(low, whole, one)
        second[...] = jnp.where(low, one, jnp.where(high, whole, zero))
    spread = (
        (lax.broadcasted_iota(jnp.int32, (128, 128), 0) < 64)
        == (lax.broadcasted_iota(jnp.int32, (128, 128), 1) < 64)
    ).astype(jnp.bfloat16)
    bound = jnp.max(norm_bounds(k, valid, spread) * norm_bounds(q, valid, spread)) * (scale * scale)
    plain = bound < 90.0 * 90.0
    rows = o.shape[0]
    blocks = [(start, block, False) for start in range(0, rows - branch, block)]
    blocks.append((rows - branch, branch, True))

    def finish(start, size, acc_a, acc_b, top):
        total = pltpu.roll(jnp.where(low, acc_b, acc_a), 64, 1)
        o[start : start + size, :] = (jnp.where(low, acc_a, acc_b) / total).astype(o.dtype)
        turned = (top + jnp.log2(total)).T
        lse[0, 0:1, start : start + size] = turned[0:1, :]
        lse[0, 1:2, start : start + size] = turned[64:65, :]

    def setup(number, start, size, is_branch):
        at = pos[number]
        query = q[query_rows(pos, number, size, span, is_branch), :]
        queries = (jnp.where(low, query, zero), jnp.where(high, query, zero))
        row = lax.broadcasted_iota(jnp.int32, (size, BK), 0)
        column = lax.broadcasted_iota(jnp.int32, (size, BK), 1)
        triangle = lax.broadcasted_iota(jnp.int32, (size, size), 1) <= lax.broadcasted_iota(
            jnp.int32, (size, size), 0
        )
        whole_blocks = at // BK

        def allowed(index):
            if is_branch:
                return column + index * BK < at
            return column + index * BK <= row + at

        end = (at + BK - 1) // BK if is_branch else whole_blocks + 1
        return queries, triangle, whole_blocks, allowed, end

    def read(index):
        rows_at = pl.ds(pl.multiple_of(index * BK, BK), BK)
        return jnp.where(valid, k[rows_at, :], zero), va[rows_at, :], vc[rows_at, :]

    def own():
        return jnp.where(valid, k[span:, :], zero), vab[...], vcb[...]

    @pl.when(plain)
    def _():
        for number, (start, size, is_branch) in enumerate(blocks):
            queries, triangle, whole_blocks, allowed, end = setup(number, start, size, is_branch)

            def step(key, first, second, carry, mask):
                out = []
                for query_h, value_h, acc in zip(queries, (first, second), carry):
                    probs = jnp.exp2(nt(query_h, key) * scale)
                    if mask is not None:
                        probs = jnp.where(mask, probs, 0.0)
                    out.append(acc + nn(probs.astype(jnp.bfloat16), value_h))
                return tuple(out)

            carry = (jnp.zeros((size, 128), jnp.float32),) * 2
            carry = lax.fori_loop(0, whole_blocks, lambda i, c: step(*read(i), c, None), carry)
            if is_branch:
                carry = lax.fori_loop(
                    whole_blocks, end, lambda i, c: step(*read(i), c, allowed(i)), carry
                )
                carry = step(*own(), carry, triangle)
            else:
                carry = step(*read(whole_blocks), carry, allowed(whole_blocks))
            finish(start, size, *carry, 0.0)

    @pl.when(jnp.logical_not(plain))
    def _():
        for number, (start, size, is_branch) in enumerate(blocks):
            queries, triangle, whole_blocks, allowed, end = setup(number, start, size, is_branch)

            def step(key, first, second, mask):
                for head, value_h in enumerate((first, second)):
                    top = tops[head, 0:size, :]
                    scores = jnp.where(mask, nt(queries[head], key), NEG)
                    new_top = jnp.maximum(top, jnp.max(scores, axis=1, keepdims=True))
                    probs = jnp.exp2((scores - new_top[:, 0:1]) * scale).astype(jnp.bfloat16)
                    fade = jnp.exp2((top - new_top) * scale)
                    accs[head, 0:size, :] = accs[head, 0:size, :] * fade + nn(probs, value_h)
                    tops[head, 0:size, :] = new_top

            accs[:, 0:size, :] = jnp.zeros((2, size, 128), jnp.float32)
            tops[:, 0:size, :] = jnp.full((2, size, 128), NEG, jnp.float32)

            @pl.loop(0, end)
            def _(index):
                step(*read(index), allowed(index))

            if is_branch:
                step(*own(), triangle)
            top = jnp.where(low, tops[0, 0:size, :], tops[1, 0:size, :]) * scale
            finish(start, size, accs[0, 0:size, :], accs[1, 0:size, :], top)


def busy(microseconds):
    return pl.CostEstimate(
        flops=int(microseconds * 1.0e9), bytes_accessed=int(microseconds * 1.0e6), transcendentals=0
    )


def attention_forward(pos, q, k, v, block, branch, after=()):
    total, width = q.shape
    span = total - branch
    rows = block * (pos.shape[0] - 1) + branch
    pairs = pl.cdiv(width, 128)

    def col(n):
        return pl.BlockSpec((n, 128), lambda p, pos: (0, p))

    return pl.pallas_call(
        functools.partial(forward_kernel, block=block, branch=branch, width=width),
        grid_spec=pltpu.PrefetchScalarGridSpec(
            num_scalar_prefetch=1,
            grid=(pairs,),
            in_specs=[col(total)] * 3 + [pl.BlockSpec(memory_space=pl.ANY)] * len(after),
            out_specs=[col(rows), pl.BlockSpec((1, 8, rows), lambda p, pos: (p, 0, 0))],
            scratch_shapes=[
                pltpu.VMEM((span, 128), jnp.bfloat16),
                pltpu.VMEM((span, 128), jnp.bfloat16),
                pltpu.VMEM((branch, 128), jnp.bfloat16),
                pltpu.VMEM((branch, 128), jnp.bfloat16),
                pltpu.VMEM((2, max(block, branch), 128), jnp.float32),
                pltpu.VMEM((2, max(block, branch), 128), jnp.float32),
            ],
        ),
        out_shape=[
            jax.ShapeDtypeStruct((rows, width), jnp.bfloat16),
            jax.ShapeDtypeStruct((pairs, 8, rows), jnp.float32),
        ],
        compiler_params=pltpu.CompilerParams(
            dimension_semantics=("arbitrary",), vmem_limit_bytes=32 * 2**20
        ),
        cost_estimate=busy(7 * pairs),
        name="attention_forward",
    )(pos, q, k, v, *after)


def backward_kernel(pos, q, k, v, o, do, lse, *rest, block, branch, width):
    dq, dk, dv = rest[-13:-10]
    kta, ktc, kam, vm, ktab, ktcb, kbm, vbm, dks, dvs = rest[-10:]
    pair = pl.program_id(0)
    scale = HEAD_DIM ** (-0.5)
    low, high, valid = halves(pair, width)
    zero = jnp.zeros((), jnp.bfloat16)
    span = k.shape[0] - branch
    prompt_part, branch_part = slice(0, span), slice(span, None)
    for part, whole_ref, turn_a, turn_b in ((prompt_part, kam, kta, ktc), (branch_part, kbm, ktab, ktcb)):
        whole = jnp.where(valid, k[part, :], zero)
        whole_ref[...] = whole
        turned = whole.T
        turn_a[...] = turned[0:64, :]
        turn_b[...] = turned[64:128, :]
    vm[...] = jnp.where(valid, v[prompt_part, :], zero)
    vbm[...] = jnp.where(valid, v[branch_part, :], zero)
    dq[...] = jnp.zeros_like(dq)
    dks[...] = jnp.zeros_like(dks)
    dvs[...] = jnp.zeros_like(dvs)
    rows = o.shape[0]
    blocks = [(start, block, False) for start in range(0, rows - branch, block)]
    blocks.append((rows - branch, branch, True))
    ones_a = jnp.broadcast_to(low, (8, 128)).astype(jnp.bfloat16)
    ones_b = jnp.broadcast_to(high, (8, 128)).astype(jnp.bfloat16)
    for number, (start, size, is_branch) in enumerate(blocks):
        at = pos[number]
        here = slice(start, start + size)
        query_at = query_rows(pos, number, size, span, is_branch)
        query = q[query_at, :]
        grad = do[here, :]
        queries = (jnp.where(low, query, zero), jnp.where(high, query, zero))
        grads = (jnp.where(low, grad, zero), jnp.where(high, grad, zero))
        product = jnp.where(valid, grad.astype(jnp.float32) * o[here, :].astype(jnp.float32), 0.0)
        upper = product.astype(jnp.bfloat16)
        lower = (product - upper.astype(jnp.float32)).astype(jnp.bfloat16)
        deltas = tuple((nt(m, upper) + nt(m, lower))[0:1, :] for m in (ones_a, ones_b))
        stats = (lse[0, 0:1, here], lse[0, 1:2, here])
        queries_cat = jnp.concatenate(queries, axis=0)
        grads_cat = jnp.concatenate(grads, axis=0)

        def step(key, value, first, second, mask):
            probs, dscores = [], []
            for query_h, grad_h, delta, stat in zip(queries, grads, deltas, stats):
                scores = nt(key, query_h)
                prob = jnp.exp2(scores * (scale * LOG2E) - stat)
                if mask is not None:
                    prob = jnp.where(mask, prob, 0.0)
                dprob = nt(value, grad_h)
                probs.append(prob.astype(jnp.bfloat16))
                dscores.append((prob * (dprob - delta)).astype(jnp.bfloat16))
            dscores_cat = jnp.concatenate(dscores, axis=1)
            dvalue = nn(jnp.concatenate(probs, axis=1), grads_cat)
            dkey = nn(dscores_cat, queries_cat)
            dquery = jnp.concatenate([nn(first, dscores[0]), nn(second, dscores[1])], axis=0)
            return dquery, dkey, dvalue

        def read(base):
            rows_at = pl.ds(pl.multiple_of(base, BK), BK)
            return kam[rows_at, :], vm[rows_at, :], kta[:, rows_at], ktc[:, rows_at]

        def accumulate(index, carry, mask):
            rows_at = pl.ds(pl.multiple_of(index * BK, BK), BK)
            dquery, dkey, dvalue = step(*read(index * BK), mask)
            dks[rows_at, :] += dkey
            dvs[rows_at, :] += dvalue
            return carry + dquery

        carry = jnp.zeros((128, size), jnp.float32)
        whole_blocks = at // BK
        carry = lax.fori_loop(0, whole_blocks, lambda i, c: accumulate(i, c, None), carry)
        row = lax.broadcasted_iota(jnp.int32, (BK, size), 0)
        column = lax.broadcasted_iota(jnp.int32, (BK, size), 1)
        if is_branch:
            carry = lax.fori_loop(
                whole_blocks,
                (at + BK - 1) // BK,
                lambda i, c: accumulate(i, c, row + i * BK < at),
                carry,
            )
            triangle = lax.broadcasted_iota(jnp.int32, (size, size), 0) <= lax.broadcasted_iota(
                jnp.int32, (size, size), 1
            )
            dquery, dkey, dvalue = step(kbm[...], vbm[...], ktab[...], ktcb[...], triangle)
            carry = carry + dquery
            dk[branch_part, :] = (dkey * scale).astype(dk.dtype)
            dv[branch_part, :] = dvalue.astype(dv.dtype)
        else:
            carry = accumulate(whole_blocks, carry, row + whole_blocks * BK <= column + at)
        dq[query_at, :] = (carry.T * scale).astype(dq.dtype)
    dk[prompt_part, :] = (dks[...] * scale).astype(dk.dtype)
    dv[prompt_part, :] = dvs[...].astype(dv.dtype)


def attention_backward(pos, q, k, v, o, do, lse, block, branch, after=()):
    total, width = q.shape
    span = total - branch
    rows = o.shape[0]
    pairs = pl.cdiv(width, 128)

    def col(n):
        return pl.BlockSpec((n, 128), lambda p, pos: (0, p))

    def scratch(n):
        wide = pltpu.VMEM((64, n), jnp.bfloat16)
        tall = pltpu.VMEM((n, 128), jnp.bfloat16)
        return [wide, wide, tall, tall]

    return pl.pallas_call(
        functools.partial(backward_kernel, block=block, branch=branch, width=width),
        grid_spec=pltpu.PrefetchScalarGridSpec(
            num_scalar_prefetch=1,
            grid=(pairs,),
            in_specs=[col(total)] * 3
            + [col(rows)] * 2
            + [pl.BlockSpec((1, 8, rows), lambda p, pos: (p, 0, 0))]
            + [pl.BlockSpec(memory_space=pl.ANY)] * len(after),
            out_specs=[col(total)] * 3,
            scratch_shapes=scratch(span)
            + scratch(branch)
            + [pltpu.VMEM((span, 128), jnp.float32), pltpu.VMEM((span, 128), jnp.float32)],
        ),
        out_shape=[jax.ShapeDtypeStruct((total, width), jnp.bfloat16)] * 3,
        compiler_params=pltpu.CompilerParams(
            dimension_semantics=("arbitrary",), vmem_limit_bytes=40 * 2**20
        ),
        cost_estimate=busy(10 * pairs),
        name="attention_backward",
    )(pos, q, k, v, o, do, lse, *after)


TILE = 256


def row_chunks(rows, size=256):
    return [slice(at, min(at + size, rows)) for at in range(0, rows, size)]


def fixed(shape):
    return pl.BlockSpec(shape, lambda *_: (0,) * len(shape), pipeline_mode=pl.Buffered(1))


def steady(shape):
    return pl.BlockSpec(shape, lambda *_: (0,) * len(shape))


def store_halves(value, half, keep, give):
    count, size = keep.shape[0], keep.shape[1]
    for block in range(count):
        first = value[2 * block * size : (2 * block + 1) * size, :]
        second = value[(2 * block + 1) * size : (2 * block + 2) * size, :]
        keep[block, :, :] = jnp.where(half == 0, first, second).astype(keep.dtype)
        give[block, :, :] = jnp.where(half == 0, second, first).astype(give.dtype)


def mlp_forward_kernel(
    mixed_a, mixed_b, tokens, out_w, out_bias, gain, shift, up, up_bias, down, down_bias, *rest
):
    hidden, slope, result, act_turned, norm, pace, act, acc = rest[-8:]
    step = pl.program_id(0)
    rows = tokens.shape[0]
    first = mixed_a.shape[1]

    @pl.when(step == 0)
    def _():
        for here in row_chunks(rows):
            resid = (
                tokens[here, :].astype(jnp.float32)
                + nn(mixed_a[here, :], out_w[:first, :])
                + nn(mixed_b[here, :], out_w[first:, :])
                + out_bias[...]
            )
            centred = resid - jnp.mean(resid, axis=1, keepdims=True)
            speed = lax.rsqrt(jnp.mean(centred * centred, axis=1, keepdims=True) + epsilon)
            normed = centred * speed
            acting = (normed * gain[...] + shift[...]).astype(jnp.bfloat16)
            act[here, :] = acting
            act_turned[:, here] = acting.T
            norm[here, :] = normed.astype(norm.dtype)
            pace[here, :] = jnp.broadcast_to(speed, (speed.shape[0], 128))
            acc[here, :] = resid + down_bias[...]

    for here in row_chunks(rows):
        pre = nn(act[here, :], up[...]) + up_bias[...]
        bell = jnp.exp(pre * pre * -0.5)
        t = 1.0 / (1.0 + (0.3275911 * 0.7071067811865476) * jnp.abs(pre))
        series = t * (
            0.127414796 + t * (-0.142248368 + t * (0.7107068705 + t * (-0.7265760135 + t * 0.5307027145)))
        )
        tail = series * bell
        below = jnp.where(pre >= 0.0, 1.0 - tail, tail)
        exact = (pre * below).astype(jnp.bfloat16)
        hidden[here, :] = exact
        slope[here, :] = (below + pre * bell * 0.3989422804014327).astype(jnp.bfloat16)
        acc[here, :] += nt(exact, down[...])

    @pl.when(step == pl.num_programs(0) - 1)
    def _():
        result[...] = acc[...].astype(result.dtype)


def mlp_forward(
    mixed, tokens, out_w, out_bias, gain, shift, up, up_bias, down, down_bias, after=()
):
    rows, width = tokens.shape
    inner = up.shape[1]
    column = pl.BlockSpec((width, TILE), lambda j: (0, j))
    tall = pl.BlockSpec((rows, TILE), lambda j: (0, j))
    line = fixed((1, width))
    like = jax.ShapeDtypeStruct
    return pl.pallas_call(
        mlp_forward_kernel,
        grid=(inner // TILE,),
        in_specs=[
            fixed(mixed[0].shape),
            fixed(mixed[1].shape),
            fixed((rows, width)),
            fixed((width, width)),
            line,
            line,
            line,
            column,
            pl.BlockSpec((1, TILE), lambda j: (0, j)),
            column,
            line,
        ]
        + [pl.BlockSpec(memory_space=pl.ANY)] * len(after),
        out_specs=[
            tall,
            tall,
            steady((rows, width)),
            steady((width, rows)),
            steady((rows, width)),
            steady((rows, 128)),
        ],
        out_shape=[
            like((rows, inner), jnp.bfloat16),
            like((rows, inner), jnp.bfloat16),
            like((rows, width), jnp.bfloat16),
            like((width, rows), jnp.bfloat16),
            like((rows, width), jnp.bfloat16),
            like((rows, 128), jnp.float32),
        ],
        scratch_shapes=[pltpu.VMEM((rows, width), jnp.bfloat16), pltpu.VMEM((rows, width), jnp.float32)],
        compiler_params=pltpu.CompilerParams(
            dimension_semantics=("arbitrary",), vmem_limit_bytes=52 * 2**20
        ),
        cost_estimate=busy(50),
        name="mlp_forward",
    )(
        *mixed,
        tokens,
        out_w,
        *(v.reshape(1, width) for v in (out_bias, gain, shift)),
        up,
        up_bias.reshape(1, inner),
        down,
        down_bias.reshape(1, width),
        *after,
    )


def mlp_backward_kernel(
    half, act_turned, cot, norm, pace, gain, mixed_a, mixed_b, out_w, hidden, slope, up, down, *rest
):
    outs = rest[-14:]
    d_resid, d_mixed_a, d_mixed_b, up_keep, up_give, down_keep, down_give, out_keep, out_give = outs[:9]
    bias_grad, lines, cot_turned, d_branch, piece = outs[9:]
    step = pl.program_id(0)
    rows, width = cot.shape
    first = mixed_a.shape[1]

    @pl.when(step == 0)
    def _():
        cot_turned[...] = cot[...].T
        d_resid[...] = jnp.zeros_like(d_resid)

    bias = jnp.zeros((1, TILE), jnp.float32)
    pieces = []
    for here in row_chunks(rows):
        d_pre = (nn(cot[here, :], down[...]) * slope[here, :].astype(jnp.float32)).astype(jnp.bfloat16)
        bias = bias + jnp.sum(d_pre.astype(jnp.float32), axis=0, keepdims=True)
        d_resid[here, :] += nt(d_pre, up[...])
        pieces.append(d_pre)
    bias_grad[...] = bias
    store_halves(nn(act_turned[...], jnp.concatenate(pieces, axis=0)), half[0], up_keep, up_give)
    store_halves(nn(cot_turned[...], hidden[...]), half[0], down_keep, down_give)

    @pl.when(step == pl.num_programs(0) - 1)
    def _():
        sums = [jnp.zeros((1, width), jnp.float32)] * 4
        for here in row_chunks(rows):
            grad = d_resid[here, :]
            normed = norm[here, :].astype(jnp.float32)
            scaled = grad * gain[...]
            inner = (
                scaled
                - jnp.mean(scaled, axis=1, keepdims=True)
                - normed * jnp.mean(scaled * normed, axis=1, keepdims=True)
            )
            exact = cot[here, :].astype(jnp.float32)
            total = exact + pace[here, 0:1] * inner
            d_resid[here, :] = total
            rounded = total.astype(jnp.bfloat16)
            d_branch[here, :] = rounded
            d_mixed_a[here, :] = nt(rounded, out_w[:first, :]).astype(d_mixed_a.dtype)
            d_mixed_b[here, :] = nt(rounded, out_w[first:, :]).astype(d_mixed_b.dtype)
            for n, term in enumerate((grad * normed, grad, rounded.astype(jnp.float32), exact)):
                sums[n] = sums[n] + jnp.sum(term, axis=0, keepdims=True)
        for n in range(4):
            lines[n : n + 1, :] = sums[n]
        for columns in row_chunks(width):
            size = columns.stop - columns.start
            piece[:first, :size] = tn(mixed_a[...], d_branch[:, columns])
            piece[first:, :size] = tn(mixed_b[...], d_branch[:, columns])
            value = piece[:, :size]
            store_halves(value, half[0], out_keep.at[:, :, columns], out_give.at[:, :, columns])


def mlp_backward(half, count, act_turned, cot, norm, pace, gain, mixed, out_w, hidden, slope, up, down):
    rows, width = cot.shape
    inner = up.shape[1]
    block = width // count // 2
    column = pl.BlockSpec((width, TILE), lambda j, half: (0, j))
    tall = pl.BlockSpec((rows, TILE), lambda j, half: (0, j))
    split = pl.BlockSpec((count, block, TILE), lambda j, half: (0, 0, j))
    like = jax.ShapeDtypeStruct
    return pl.pallas_call(
        mlp_backward_kernel,
        grid_spec=pltpu.PrefetchScalarGridSpec(
            num_scalar_prefetch=1,
            grid=(inner // TILE,),
            in_specs=[
                fixed((width, rows)),
                fixed((rows, width)),
                fixed((rows, width)),
                fixed((rows, 128)),
                fixed((1, width)),
                fixed(mixed[0].shape),
                fixed(mixed[1].shape),
                fixed((width, width)),
                tall,
                tall,
                column,
                column,
            ],
            out_specs=[
                steady((rows, width)),
                steady(mixed[0].shape),
                steady(mixed[1].shape),
                split,
                split,
                split,
                split,
                steady((count, block, width)),
                steady((count, block, width)),
                pl.BlockSpec((1, TILE), lambda j, half: (0, j)),
                steady((8, width)),
            ],
            scratch_shapes=[
                pltpu.VMEM((width, rows), jnp.bfloat16),
                pltpu.VMEM((rows, width), jnp.bfloat16),
                pltpu.VMEM((width, TILE), jnp.float32),
            ],
        ),
        out_shape=[like((rows, width), jnp.float32)]
        + [like(m.shape, jnp.bfloat16) for m in mixed]
        + [like((count, block, inner), jnp.bfloat16)] * 4
        + [like((count, block, width), jnp.bfloat16)] * 2
        + [like((1, inner), jnp.float32), like((8, width), jnp.float32)],
        compiler_params=pltpu.CompilerParams(
            dimension_semantics=("arbitrary",), vmem_limit_bytes=58 * 2**20
        ),
        cost_estimate=busy(80),
        name="mlp_backward",
    )(half, act_turned, cot, norm, pace, gain.reshape(1, width), *mixed, out_w, hidden, slope, up, down)


def projection_tiles(widths):
    first, second = (pl.cdiv(w, TILE) for w in widths)
    return first, second, [
        lambda t, *_: jnp.minimum(t, first - 1),
        lambda t, *_: jnp.maximum(t - first, 0),
    ]


def tile_of(ref, place, width):
    value = ref[...]
    if width % TILE == 0:
        return value
    lane = lax.broadcasted_iota(jnp.int32, (1, TILE), 1)
    return jnp.where(lane < width - place * TILE, value, jnp.zeros((), value.dtype))


def tokens_back_kernel(*refs, widths):
    grads, weights = (refs[0:3], refs[3:6]), (refs[6:9], refs[9:12])
    out, acc = refs[-2:]
    step = pl.program_id(0)
    first, second, _ = projection_tiles(widths)

    @pl.when(step == 0)
    def _():
        acc[...] = jnp.zeros_like(acc)

    for group in range(2):

        @pl.when(step < first if group == 0 else step >= first)
        def _():
            place = step if group == 0 else step - first
            weight = jnp.concatenate([tile_of(w, place, widths[group]) for w in weights[group]], axis=1)
            lane = lax.broadcasted_iota(jnp.int32, (1, TILE), 1)
            for here in row_chunks(acc.shape[0]):
                parts = []
                for ref in grads[group]:
                    part = ref[here, :]
                    if widths[group] % TILE:
                        part = jnp.where(lane < widths[group] - place * TILE, part, jnp.zeros((), part.dtype))
                    parts.append(part)
                acc[here, :] += nt(jnp.concatenate(parts, axis=1), weight)

    @pl.when(step == pl.num_programs(0) - 1)
    def _():
        out[...] = acc[...].astype(out.dtype)


def tokens_back(grads, weights, after=()):
    total = grads[0][0].shape[0]
    width = weights[0][0].shape[0]
    widths = [group[0].shape[1] for group in grads]
    first, second, places = projection_tiles(widths)

    def tiles(rows):
        return [pl.BlockSpec((rows, TILE), lambda t, at=at: (0, at(t))) for at in places for _ in range(3)]

    return pl.pallas_call(
        functools.partial(tokens_back_kernel, widths=widths),
        grid=(first + second,),
        in_specs=tiles(total) + tiles(width) + [pl.BlockSpec(memory_space=pl.ANY)] * len(after),
        out_specs=steady((total, width)),
        out_shape=jax.ShapeDtypeStruct((total, width), jnp.bfloat16),
        scratch_shapes=[pltpu.VMEM((total, width), jnp.float32)],
        compiler_params=pltpu.CompilerParams(
            dimension_semantics=("arbitrary",), vmem_limit_bytes=52 * 2**20
        ),
        cost_estimate=busy(20),
        name="tokens_back",
    )(*grads[0], *grads[1], *weights[0], *weights[1], *after)


def weights_back_kernel(half, turned, *refs, widths):
    grads = (refs[0:3], refs[3:6])
    outs = refs[-16:]
    step = pl.program_id(0)
    first, second, _ = projection_tiles(widths)
    for group in range(2):
        keeps = outs[group * 8 : group * 8 + 3]
        gives = outs[group * 8 + 3 : group * 8 + 6]
        biases = outs[group * 8 + 6 : group * 8 + 8]

        @pl.when(step < first if group == 0 else step >= first)
        def _():
            for kind in range(3):
                part = grads[group][kind][...]
                store_halves(nn(turned[...], part), half[0], keeps[kind], gives[kind])
                if kind != 1:
                    biases[kind // 2][...] = jnp.sum(part.astype(jnp.float32), axis=0, keepdims=True)


def weights_back(half, count, turned, grads, after=()):
    width, total = turned.shape
    widths = [group[0].shape[1] for group in grads]
    first, second, places = projection_tiles(widths)
    block = width // count // 2
    like = jax.ShapeDtypeStruct
    out_specs, out_shape = [], []
    for at, w in zip(places, widths):
        out_specs += [pl.BlockSpec((count, block, TILE), lambda t, half, at=at: (0, 0, at(t)))] * 6
        out_specs += [pl.BlockSpec((1, TILE), lambda t, half, at=at: (0, at(t)))] * 2
        out_shape += [like((count, block, w), jnp.bfloat16)] * 6 + [like((1, w), jnp.float32)] * 2
    return pl.pallas_call(
        functools.partial(weights_back_kernel, widths=widths),
        grid_spec=pltpu.PrefetchScalarGridSpec(
            num_scalar_prefetch=1,
            grid=(first + second,),
            in_specs=[fixed((width, total))]
            + [
                pl.BlockSpec((total, TILE), lambda t, half, at=at: (0, at(t)))
                for at in places
                for _ in range(3)
            ]
            + [pl.BlockSpec(memory_space=pl.ANY)] * len(after),
            out_specs=out_specs,
        ),
        out_shape=out_shape,
        compiler_params=pltpu.CompilerParams(
            dimension_semantics=("arbitrary",), vmem_limit_bytes=52 * 2**20
        ),
        cost_estimate=busy(20),
        name="weights_back",
    )(half, turned, *grads[0], *grads[1], *after)


def gate_kernel(*refs):
    pass


def gate(value, after):
    if not after:
        return value
    anywhere = pl.BlockSpec(memory_space=pl.ANY)
    return pl.pallas_call(
        gate_kernel,
        in_specs=[anywhere] * (1 + len(after)),
        out_specs=anywhere,
        out_shape=jax.ShapeDtypeStruct(value.shape, value.dtype),
        input_output_aliases={0: 0},
        cost_estimate=busy(1),
        name="gate",
    )(value, *after)


def normalise(values_in):
    centre = jnp.mean(values_in, axis=-1, keepdims=True)
    centred = values_in - centre
    spread = jnp.mean(centred * centred, axis=-1, keepdims=True)
    pace = lax.rsqrt(spread + epsilon)
    return centred * pace, pace


def norm_back(grad, norm, pace, gain):
    scaled = grad * gain
    return pace * (
        scaled
        - jnp.mean(scaled, axis=-1, keepdims=True)
        - norm * jnp.mean(scaled * norm, axis=-1, keepdims=True)
    )


def swap(value, axis, bit):
    count = lax.axis_size(axis)
    return lax.ppermute(value, axis, [(i, i ^ bit) for i in range(count)])


def ahead(value, axis, step):
    count = lax.axis_size(axis)
    return lax.ppermute(value, axis, [(i, (i + step) % count) for i in range(count)])


def total_over(value, axes):
    for axis in axes:
        count = lax.axis_size(axis)
        if count & (count - 1):
            value = lax.psum(value, axis)
            continue
        bit = 1
        while bit < count:
            value = value + swap(value, axis, bit)
            bit *= 2
    return value


def by_halves(half_width):
    return lax.axis_size("dp") == 4 and lax.axis_size("gy") == 2 and half_width > GROUP


def half_index():
    return lax.axis_index("dp") % 2


def pair_rows(mine, theirs):
    first = half_index() == 0
    return jnp.stack([jnp.where(first, mine, theirs), jnp.where(first, theirs, mine)], axis=-3)


def gather_plain(part):
    part = lax.all_gather(part, "gy", axis=1, tiled=True)
    return lax.all_gather(part, "gx", axis=0, tiled=True)


def gather_quarters(part):
    rows, columns = part.shape
    copies, gx, gy = (lax.axis_size(axis) for axis in ("dp", "gx", "gy"))
    size = columns // copies
    mine = lax.dynamic_slice_in_dim(part, lax.axis_index("dp") * size, size, 1)
    raw = lax.all_gather(mine, ("dp", "gx", "gy"))
    got = raw.reshape(copies, gx, gy, rows, size)
    return raw, [
        [got[quarter, :, side].reshape(gx * rows, size) for quarter in range(copies)]
        for side in range(gy)
    ]


def gather_projections(qkv_part, out_part, width):
    rows = qkv_part.shape[0]
    half = width // 2
    first_side = lax.axis_index("gy") == 0
    key_at = width - half
    here = jnp.where(
        first_side,
        qkv_part[:, :GROUP],
        qkv_part[:, half : half + GROUP],
    )
    keys_here = jnp.where(first_side, qkv_part[:, width : width + GROUP], qkv_part[:, :GROUP])
    raw, one = gather_quarters(jnp.concatenate([here, keys_here], axis=1))
    rest = width - GROUP
    spare = half - GROUP
    queries_rest = jnp.where(first_side, qkv_part[:, GROUP:width], qkv_part[:, half + GROUP :])
    keys_rest = jnp.where(first_side, qkv_part[:, width + GROUP :], qkv_part[:, GROUP:half])

    def pad(value, size):
        return jnp.pad(value, ((0, 0), (0, size - value.shape[1])))

    outer = pl.cdiv(rest + spare, 128) * 128
    out_size = pl.cdiv(half, 128) * 128
    total = pl.cdiv(outer + out_size, 512) * 512
    packed = pad(jnp.concatenate([queries_rest, keys_rest], axis=1), outer)
    packed = pad(jnp.concatenate([packed, pad(out_part, out_size)], axis=1), total)
    two = [jnp.concatenate(side, axis=1) for side in gather_quarters(packed)[1]]
    first = [
        jnp.concatenate(one[0][:2], axis=1),
        jnp.concatenate(one[0][2:], axis=1),
        jnp.concatenate(one[1][:2], axis=1),
    ]
    second = [
        two[0][:, :rest],
        jnp.concatenate(
            [two[0][:, rest : rest + spare]] + one[1][2:] + [two[1][:, rest : rest + spare]], axis=1
        ),
        two[1][:, :rest],
    ]
    out_full = jnp.concatenate([side[:, outer : outer + half] for side in two], axis=1)
    return [first, second], out_full, raw


def gather_feed_forward(up_part, down_part, after):
    columns = up_part.shape[1]
    shared = columns // 2 // 512 * 512
    _, quarters = gather_quarters(jnp.concatenate([up_part[:, :shared], down_part[:, :shared]], axis=1))
    first_half = half_index() == 0
    first_side = lax.axis_index("gy") == 0
    mine = gate(jnp.where(first_half, up_part[:, shared:], down_part[:, shared:]), after)
    rows, size = mine.shape
    count = lax.axis_size("gx")
    here = lax.axis_index("gx")
    blocks = jnp.zeros((count, rows, size), mine.dtype)
    for step in range(count):
        got = mine if step == 0 else ahead(mine, "gx", step)
        blocks = lax.dynamic_update_index_in_dim(blocks, got, (here - step) % count, 0)
    own = blocks.reshape(count * rows, size)
    theirs = swap(own, "gy", 1)
    sides = (jnp.where(first_side, own, theirs), jnp.where(first_side, theirs, own))
    others = [swap(side, "dp", 1) for side in sides]
    ups = [jnp.where(first_half, a, b) for a, b in zip(sides, others)]
    downs = [jnp.where(first_half, b, a) for a, b in zip(sides, others)]
    wholes = []
    for pieces, rest in ((slice(0, 2), ups), (slice(2, 4), downs)):
        wholes.append(
            jnp.concatenate([p for side in range(2) for p in quarters[side][pieces] + [rest[side]]], axis=1)
        )
    return wholes, own


def core_step(keep, give):
    return add(keep, swap(give, "dp", 1))


def both_halves(keep, give):
    count, size, columns = keep.shape
    return jnp.stack([keep, give], axis=1).reshape(2 * count * size, columns)


def add(a, b):
    return (a.astype(jnp.float32) + b.astype(jnp.float32)).astype(jnp.bfloat16)


def overlap_step(sides):
    columns = sides[0].shape[-1]
    size = pl.cdiv(pl.cdiv(columns, 128), 2) * 128
    own_first = lax.axis_index("dp") // 2 == 0
    first, second = (
        jnp.concatenate([side[..., at : at + size] for side in sides], axis=-1) for at in (0, columns - size)
    )
    done = add(jnp.where(own_first, first, second), swap(jnp.where(own_first, second, first), "dp", 2))
    return done[..., :size], done[..., size:]


def overlap_join(value, columns):
    size = value.shape[-1]
    other = swap(value, "dp", 2)
    own_first = lax.axis_index("dp") // 2 == 0
    first, second = jnp.where(own_first, value, other), jnp.where(own_first, other, value)
    return jnp.concatenate([first, second[..., 2 * size - columns :]], axis=-1)


def blocks_step(value):
    count = lax.axis_size("gx")
    here = lax.axis_index("gx")
    total = lax.dynamic_index_in_dim(value, here, 0, False).astype(jnp.float32)
    for step in range(1, count):
        give = lax.dynamic_index_in_dim(value, (here + step) % count, 0, False)
        total = total + ahead(give, "gx", step).astype(jnp.float32)
    return total.astype(jnp.bfloat16)


def copies_step(value):
    bit = 2
    while bit < lax.axis_size("dp"):
        value = add(value, swap(value, "dp", bit))
        bit *= 2
    return value


def join_step(value):
    columns = value.shape[-1]
    return pair_rows(value, swap(value, "dp", 1)).reshape(-1, columns).astype(jnp.float32)


def side_exchange(first, second):
    first_side = lax.axis_index("gy") == 0
    keep = jnp.where(first_side, first, second)
    return add(keep, swap(jnp.where(first_side, second, first), "gy", 1))


def projection_sides(first, rest, width):
    size = width - GROUP
    spare = width // 2 - GROUP
    query, key, value = first
    query_rest, key_rest, value_rest = rest
    return (
        jnp.concatenate([query, key, query_rest, key_rest[..., :spare]], axis=-1),
        jnp.concatenate(
            [value, key_rest[..., spare : size - spare], value_rest, key_rest[..., size - spare :]], axis=-1
        ),
    )


def join_projections(whole, width):
    rest = width - GROUP
    pieces = [
        whole[:, :GROUP],
        whole[:, GROUP : 2 * GROUP],
        whole[:, 2 * GROUP : 2 * GROUP + rest],
        whole[:, 2 * GROUP + rest :],
    ]
    return jnp.where(
        lax.axis_index("gy") == 0,
        jnp.concatenate([pieces[n] for n in (0, 2, 1, 3)], axis=1),
        jnp.concatenate([pieces[n] for n in (1, 3, 0, 2)], axis=1),
    )


def scatter_plain(whole):
    part = lax.psum_scatter(whole, "gy", scatter_dimension=1, tiled=True)
    part = lax.psum_scatter(part, "gx", scatter_dimension=0, tiled=True)
    return lax.psum(part, "dp").astype(jnp.float32)


def all_tokens(own):
    count = lax.axis_size("gy")
    here = lax.axis_index("gy")
    if count != 2:
        return lax.all_gather(own, "gy", axis=0, tiled=True)
    other = swap(own, "gy", 1)
    first = here == 0
    return jnp.concatenate([jnp.where(first, own, other), jnp.where(first, other, own)], axis=0)


def own_tokens_sum(whole):
    count = lax.axis_size("gy")
    here = lax.axis_index("gy")
    rows = whole.shape[0] // count
    if count != 2:
        return lax.psum_scatter(
            whole.astype(jnp.bfloat16), "gy", scatter_dimension=0, tiled=True
        ).astype(jnp.float32)
    give = lax.dynamic_slice_in_dim(whole, (1 - here) * rows, rows, 0)
    keep = lax.dynamic_slice_in_dim(whole, here * rows, rows, 0)
    return keep.astype(jnp.float32) + swap(give.astype(jnp.bfloat16), "gy", 1).astype(jnp.float32)


def dot(a, b):
    return jnp.dot(a, b, preferred_element_type=jnp.float32)


def local(
    prompt,
    continuations,
    prefix_len,
    attn_gain,
    attn_shift,
    qkv_weight,
    query_bias,
    value_bias,
    out_weight,
    out_bias,
    mlp_gain,
    mlp_shift,
    up_weight,
    up_bias,
    down_weight,
    down_bias,
    grad_prompt,
    grad_continuations,
):
    groups, shard, width = prompt.shape
    length = continuations.shape[1]
    first_pos = lax.axis_index("gy") * shard
    prompt_len = shard * lax.axis_size("gy")
    block = shard // 2
    halved = by_halves(width // 2)
    spans = [slice(0, GROUP), slice(GROUP, width)]

    if halved:
        limit, other_limit = prefix_len[0], swap(prefix_len, "gy", 1)[0]
        is_first = first_pos == 0
        is_long = jnp.logical_or(limit > other_limit, jnp.logical_and(limit == other_limit, is_first))
        kept_at = jnp.where(is_long, 0, block)
        places = [first_pos + kept_at, shard - first_pos + kept_at, limit]
    else:
        places = [first_pos, first_pos + block, prefix_len[0]]
    places = jnp.stack(places).astype(jnp.int32)

    def kept_rows(own):
        return lax.dynamic_slice_in_dim(own, kept_at, block, 0)

    def given_rows(own):
        return lax.dynamic_slice_in_dim(own, block - kept_at, block, 0)

    def back_home(done):
        if not halved:
            return done
        kept, home = done[:block], swap(done[block:], "gy", 1)
        return jnp.concatenate([jnp.where(is_long, kept, home), jnp.where(is_long, home, kept)], axis=0)

    own_prompt = prompt.reshape(shard, width)
    branch = continuations.reshape(length, width)
    own_cot = grad_prompt.reshape(shard, width)
    branch_cot = grad_continuations.reshape(length, width)
    whole_prompt = all_tokens(own_prompt)
    if halved:
        weights, out_full, raw = gather_projections(qkv_weight, out_weight, width)
        (up_full, down_full), fetched = gather_feed_forward(up_weight, down_weight.T, (raw,))
        fetched = (fetched,)
        other_cot = swap(gate(given_rows(own_cot), (raw,)), "gy", 1)
        cotangent = jnp.concatenate([kept_rows(own_cot), other_cot, branch_cot], axis=0)
    else:
        qkv = gather_plain(qkv_weight)
        weights = [[qkv[:, c.start + s : c.stop + s] for s in (0, width, 2 * width)] for c in spans]
        out_full, up_full, down_full = (gather_plain(w) for w in (out_weight, up_weight, down_weight.T))
        fetched = ()
        cotangent = jnp.concatenate([own_cot, branch_cot], axis=0)

    all_rows = jnp.concatenate([whole_prompt, branch], axis=0)
    norm_all, _ = normalise(all_rows.astype(jnp.float32))
    act_all = (norm_all * attn_gain + attn_shift).astype(jnp.bfloat16)
    projected, mixed, stats = [], [], []
    for number, (cols, (w_query, w_key, w_value)) in enumerate(zip(spans, weights)):
        projected.append(
            (
                (dot(act_all, w_query) + query_bias[cols]).astype(jnp.bfloat16),
                dot(act_all, w_key).astype(jnp.bfloat16),
                (dot(act_all, w_value) + value_bias[cols]).astype(jnp.bfloat16),
            )
        )
        got, stat = attention_forward(
            places, *projected[-1], block, length, fetched if number == 1 else ()
        )
        mixed.append(got)
        stats.append(stat)

    tokens = jnp.concatenate(
        [lax.dynamic_slice_in_dim(whole_prompt, places[n], block, 0) for n in range(2)] + [branch], axis=0
    )
    hidden, slope, result, act_turned, norm_two, pace_two = mlp_forward(
        mixed, tokens, out_full, out_bias, mlp_gain, mlp_shift, up_full, up_bias, down_full, down_bias
    )
    prompt_out = back_home(result[:shard]).reshape(groups, shard, width)
    continuation_out = result[shard:].reshape(1, length, width)

    count = lax.axis_size("gx")
    half = jnp.reshape(half_index() if halved else 0, (1,)).astype(jnp.int32)
    (
        d_resid,
        *d_mixed,
        up_keep,
        up_give,
        down_keep,
        down_give,
        out_keep,
        out_give,
        up_bias_grad,
        lines,
    ) = mlp_backward(
        half,
        count,
        act_turned,
        cotangent,
        norm_two,
        pace_two,
        mlp_gain,
        mixed,
        out_full,
        hidden,
        slope,
        up_full,
        down_full,
    )
    mlp_gain_grad, mlp_shift_grad, out_bias_grad, down_bias_grad = (lines[n] for n in range(4))
    after = ()
    if halved:
        up_flow, down_flow, out_flow = (
            core_step(*pair)
            for pair in ((up_keep, up_give), (down_keep, down_give), (out_keep, out_give))
        )
        after = (up_flow, down_flow, out_flow)
    d_parts = [None, None]
    for number in (1, 0):
        d_parts[number] = attention_backward(
            places, *projected[number], mixed[number], d_mixed[number], stats[number], block, length, after
        )
        if halved and number == 1:
            side = up_weight.shape[1]
            up_flow = side_exchange(
                jnp.concatenate([up_flow[..., :side], out_flow[..., : width // 2]], axis=-1),
                jnp.concatenate([up_flow[..., side:], out_flow[..., width // 2 :]], axis=-1),
            )
            down_sides = overlap_step((down_flow[..., :side], down_flow[..., side:]))
            after = (up_flow, *down_sides)
        if halved and number == 0:
            up_flow, down_flow = blocks_step(up_flow), side_exchange(*down_sides)
            after = (up_flow, down_flow)
    d_act_all = tokens_back(d_parts, weights, after)
    shared = own_tokens_sum(d_act_all[:prompt_len])
    grads = weights_back(half, count, act_all.T, d_parts, (d_act_all,))
    keeps, gives = (grads[0:3], grads[8:11]), (grads[3:6], grads[11:14])
    query_bias_grad, value_bias_grad = (
        jnp.concatenate([grads[6 + n], grads[14 + n]], axis=1).reshape(-1) for n in range(2)
    )
    if halved:
        sides = [
            core_step(keep, give)
            for keep, give in zip(projection_sides(*keeps, width), projection_sides(*gives, width))
        ]
        qkv_flow = side_exchange(*overlap_step(sides))
        qkv_total = join_projections(
            join_step(overlap_join(blocks_step(qkv_flow), qkv_weight.shape[1])),
            width,
        )
        up_total = join_step(copies_step(up_flow))
        up_total, out_total = up_total[:, :side], up_total[:, side:]
        down_total = join_step(overlap_join(blocks_step(down_flow), side))
    else:
        qkv_grad = jnp.concatenate(
            [both_halves(keeps[n][kind], gives[n][kind]) for kind in range(3) for n in range(2)], axis=1
        )
        up_total, down_total, out_total, qkv_total = (
            scatter_plain(g)
            for g in (
                both_halves(up_keep, up_give),
                both_halves(down_keep, down_give),
                both_halves(out_keep, out_give),
                qkv_grad,
            )
        )
    d_act_exact = d_act_all.astype(jnp.float32)
    attn_gain_grad = jnp.sum(d_act_exact * norm_all, axis=0)
    attn_shift_grad = jnp.sum(d_act_exact, axis=0)
    norm_own, pace_own = normalise(jnp.concatenate([own_prompt, branch], axis=0).astype(jnp.float32))
    d_act_own = jnp.concatenate([shared, d_act_all[prompt_len:]], axis=0)
    rows_part = norm_back(d_act_own, norm_own, pace_own, attn_gain)
    prompt_resid = d_resid[:shard]
    if halved:
        home = back_home(prompt_resid.astype(jnp.bfloat16)).astype(jnp.float32)
        kept = jnp.where(is_long, prompt_resid[:block], home[:block]), jnp.where(
            is_long, home[block:], prompt_resid[:block]
        )
        prompt_resid = jnp.concatenate(kept, axis=0)
    d_rows = jnp.concatenate([prompt_resid, d_resid[shard:]], axis=0) + rows_part
    prompt_grad = d_rows[:shard].reshape(groups, shard, width)
    continuation_grad = d_rows[shard:].reshape(1, length, width)
    vectors = (
        attn_gain_grad,
        attn_shift_grad,
        query_bias_grad,
        value_bias_grad,
        out_bias_grad,
        mlp_gain_grad,
        mlp_shift_grad,
        up_bias_grad.reshape(-1),
        down_bias_grad,
    )
    joined = total_over(jnp.concatenate(vectors), ("dp", "gy", "gx"))
    totals = []
    at = 0
    for vector in vectors:
        totals.append(joined[at : at + vector.shape[0]])
        at += vector.shape[0]
    return (
        prompt_out,
        continuation_out,
        prompt_grad,
        continuation_grad,
        totals[0],
        totals[1],
        qkv_total,
        totals[2],
        totals[3],
        out_total,
        totals[4],
        totals[5],
        totals[6],
        up_total,
        totals[7],
        down_total.T,
        totals[8],
    )


def solution(mesh):
    placed = (
        P(("dp", "gx"), "gy", None),
        P(("dp", "gx", "gy"), None, None),
        P(("dp", "gx", "gy")),
        P(),
        P(),
        P("gx", "gy"),
        P(),
        P(),
        P("gx", "gy"),
        P(),
        P(),
        P(),
        P("gx", "gy"),
        P(),
        P("gy", "gx"),
        P(),
        P(("dp", "gx"), "gy", None),
        P(("dp", "gx", "gy"), None, None),
    )
    return jax.shard_map(
        local,
        mesh=mesh,
        in_specs=placed,
        out_specs=(
            P(("dp", "gx"), "gy", None),
            P(("dp", "gx", "gy"), None, None),
            P(("dp", "gx"), "gy", None),
            P(("dp", "gx", "gy"), None, None),
            P(),
            P(),
            P("gx", "gy"),
            P(),
            P(),
            P("gx", "gy"),
            P(),
            P(),
            P(),
            P("gx", "gy"),
            P(),
            P("gy", "gx"),
            P(),
        ),
        check_vma=False,
    )
```

```python
import functools
import jax
import jax.numpy as jnp
from jax import lax
from jax.sharding import PartitionSpec as P
from jax.experimental import pallas as pl
from jax.experimental.pallas import tpu as pltpu

HEAD_DIM = 64
LOG2E = 1.4426950408889634
NEG = -1e30
BK = 512
GROUP = 512
epsilon = 1e-05


def nt(a, b):
    return lax.dot_general(a, b, (((1,), (1,)), ((), ())), preferred_element_type=jnp.float32)


def nn(a, b):
    return jnp.dot(a, b, preferred_element_type=jnp.float32)


def tn(a, b):
    return lax.dot_general(a, b, (((0,), (0,)), ((), ())), preferred_element_type=jnp.float32)


def halves(pair, total):
    lane = lax.broadcasted_iota(jnp.int32, (1, 128), 1)
    left = jnp.minimum(total - pair * 128, 128)
    return lane < 64, jnp.logical_and(lane >= 64, lane < left), lane < left


def norm_bounds(ref, valid, spread):
    part = jnp.where(valid, ref[...], jnp.zeros((), jnp.bfloat16))
    return jnp.max(nn(part * part, spread), axis=0, keepdims=True)


def query_rows(pos, number, size, span, is_branch):
    if is_branch:
        return pl.ds(span, size)
    return pl.ds(pl.multiple_of(pos[number], size), size)


def forward_kernel(pos, q, k, v, *rest, block, branch, width):
    o, lse, va, vc, vab, vcb, tops, accs = rest[-8:]
    pair = pl.program_id(0)
    scale = HEAD_DIM ** (-0.5) * LOG2E
    low, high, valid = halves(pair, width)
    zero = jnp.zeros((), jnp.bfloat16)
    one = jnp.ones((), jnp.bfloat16)
    span = k.shape[0] - branch
    for part, first, second in ((slice(0, span), va, vc), (slice(span, None), vab, vcb)):
        whole = v[part, :]
        first[...] = jnp.where(low, whole, one)
        second[...] = jnp.where(low, one, jnp.where(high, whole, zero))
    spread = (
        (lax.broadcasted_iota(jnp.int32, (128, 128), 0) < 64)
        == (lax.broadcasted_iota(jnp.int32, (128, 128), 1) < 64)
    ).astype(jnp.bfloat16)
    bound = jnp.max(norm_bounds(k, valid, spread) * norm_bounds(q, valid, spread)) * (scale * scale)
    plain = bound < 90.0 * 90.0
    rows = o.shape[0]
    blocks = [(start, block, False) for start in range(0, rows - branch, block)]
    blocks.append((rows - branch, branch, True))

    def finish(start, size, acc_a, acc_b, top):
        total = pltpu.roll(jnp.where(low, acc_b, acc_a), 64, 1)
        o[start : start + size, :] = (jnp.where(low, acc_a, acc_b) / total).astype(o.dtype)
        turned = (top + jnp.log2(total)).T
        lse[0, 0:1, start : start + size] = turned[0:1, :]
        lse[0, 1:2, start : start + size] = turned[64:65, :]

    def setup(number, start, size, is_branch):
        at = pos[number]
        query = q[query_rows(pos, number, size, span, is_branch), :]
        queries = (jnp.where(low, query, zero), jnp.where(high, query, zero))
        row = lax.broadcasted_iota(jnp.int32, (size, BK), 0)
        column = lax.broadcasted_iota(jnp.int32, (size, BK), 1)
        triangle = lax.broadcasted_iota(jnp.int32, (size, size), 1) <= lax.broadcasted_iota(
            jnp.int32, (size, size), 0
        )
        whole_blocks = at // BK

        def allowed(index):
            if is_branch:
                return column + index * BK < at
            return column + index * BK <= row + at

        end = (at + BK - 1) // BK if is_branch else whole_blocks + 1
        return queries, triangle, whole_blocks, allowed, end

    def read(index):
        rows_at = pl.ds(pl.multiple_of(index * BK, BK), BK)
        return jnp.where(valid, k[rows_at, :], zero), va[rows_at, :], vc[rows_at, :]

    def own():
        return jnp.where(valid, k[span:, :], zero), vab[...], vcb[...]

    @pl.when(plain)
    def _():
        for number, (start, size, is_branch) in enumerate(blocks):
            queries, triangle, whole_blocks, allowed, end = setup(number, start, size, is_branch)

            def step(key, first, second, carry, mask):
                out = []
                for query_h, value_h, acc in zip(queries, (first, second), carry):
                    probs = jnp.exp2(nt(query_h, key) * scale)
                    if mask is not None:
                        probs = jnp.where(mask, probs, 0.0)
                    out.append(acc + nn(probs.astype(jnp.bfloat16), value_h))
                return tuple(out)

            carry = (jnp.zeros((size, 128), jnp.float32),) * 2
            carry = lax.fori_loop(0, whole_blocks, lambda i, c: step(*read(i), c, None), carry)
            if is_branch:
                carry = lax.fori_loop(
                    whole_blocks, end, lambda i, c: step(*read(i), c, allowed(i)), carry
                )
                carry = step(*own(), carry, triangle)
            else:
                carry = step(*read(whole_blocks), carry, allowed(whole_blocks))
            finish(start, size, *carry, 0.0)

    @pl.when(jnp.logical_not(plain))
    def _():
        for number, (start, size, is_branch) in enumerate(blocks):
            queries, triangle, whole_blocks, allowed, end = setup(number, start, size, is_branch)

            def step(key, first, second, mask):
                for head, value_h in enumerate((first, second)):
                    top = tops[head, 0:size, :]
                    scores = jnp.where(mask, nt(queries[head], key), NEG)
                    new_top = jnp.maximum(top, jnp.max(scores, axis=1, keepdims=True))
                    probs = jnp.exp2((scores - new_top[:, 0:1]) * scale).astype(jnp.bfloat16)
                    fade = jnp.exp2((top - new_top) * scale)
                    accs[head, 0:size, :] = accs[head, 0:size, :] * fade + nn(probs, value_h)
                    tops[head, 0:size, :] = new_top

            accs[:, 0:size, :] = jnp.zeros((2, size, 128), jnp.float32)
            tops[:, 0:size, :] = jnp.full((2, size, 128), NEG, jnp.float32)

            @pl.loop(0, end)
            def _(index):
                step(*read(index), allowed(index))

            if is_branch:
                step(*own(), triangle)
            top = jnp.where(low, tops[0, 0:size, :], tops[1, 0:size, :]) * scale
            finish(start, size, accs[0, 0:size, :], accs[1, 0:size, :], top)


def busy(microseconds):
    return pl.CostEstimate(
        flops=int(microseconds * 1.0e9), bytes_accessed=int(microseconds * 1.0e6), transcendentals=0
    )


def attention_forward(pos, q, k, v, block, branch, after=()):
    total, width = q.shape
    span = total - branch
    rows = block * (pos.shape[0] - 1) + branch
    pairs = pl.cdiv(width, 128)

    def col(n):
        return pl.BlockSpec((n, 128), lambda p, pos: (0, p))

    return pl.pallas_call(
        functools.partial(forward_kernel, block=block, branch=branch, width=width),
        grid_spec=pltpu.PrefetchScalarGridSpec(
            num_scalar_prefetch=1,
            grid=(pairs,),
            in_specs=[col(total)] * 3 + [pl.BlockSpec(memory_space=pl.ANY)] * len(after),
            out_specs=[col(rows), pl.BlockSpec((1, 8, rows), lambda p, pos: (p, 0, 0))],
            scratch_shapes=[
                pltpu.VMEM((span, 128), jnp.bfloat16),
                pltpu.VMEM((span, 128), jnp.bfloat16),
                pltpu.VMEM((branch, 128), jnp.bfloat16),
                pltpu.VMEM((branch, 128), jnp.bfloat16),
                pltpu.VMEM((2, max(block, branch), 128), jnp.float32),
                pltpu.VMEM((2, max(block, branch), 128), jnp.float32),
            ],
        ),
        out_shape=[
            jax.ShapeDtypeStruct((rows, width), jnp.bfloat16),
            jax.ShapeDtypeStruct((pairs, 8, rows), jnp.float32),
        ],
        compiler_params=pltpu.CompilerParams(
            dimension_semantics=("arbitrary",), vmem_limit_bytes=32 * 2**20
        ),
        cost_estimate=busy(7 * pairs),
        name="attention_forward",
    )(pos, q, k, v, *after)


def backward_kernel(pos, q, k, v, o, do, lse, *rest, block, branch, width):
    dq, dk, dv = rest[-13:-10]
    kta, ktc, kam, vm, ktab, ktcb, kbm, vbm, dks, dvs = rest[-10:]
    pair = pl.program_id(0)
    scale = HEAD_DIM ** (-0.5)
    low, high, valid = halves(pair, width)
    zero = jnp.zeros((), jnp.bfloat16)
    span = k.shape[0] - branch
    prompt_part, branch_part = slice(0, span), slice(span, None)
    for part, whole_ref, turn_a, turn_b in ((prompt_part, kam, kta, ktc), (branch_part, kbm, ktab, ktcb)):
        whole = jnp.where(valid, k[part, :], zero)
        whole_ref[...] = whole
        turned = whole.T
        turn_a[...] = turned[0:64, :]
        turn_b[...] = turned[64:128, :]
    vm[...] = jnp.where(valid, v[prompt_part, :], zero)
    vbm[...] = jnp.where(valid, v[branch_part, :], zero)
    dq[...] = jnp.zeros_like(dq)
    dks[...] = jnp.zeros_like(dks)
    dvs[...] = jnp.zeros_like(dvs)
    rows = o.shape[0]
    blocks = [(start, block, False) for start in range(0, rows - branch, block)]
    blocks.append((rows - branch, branch, True))
    ones_a = jnp.broadcast_to(low, (8, 128)).astype(jnp.bfloat16)
    ones_b = jnp.broadcast_to(high, (8, 128)).astype(jnp.bfloat16)
    for number, (start, size, is_branch) in enumerate(blocks):
        at = pos[number]
        here = slice(start, start + size)
        query_at = query_rows(pos, number, size, span, is_branch)
        query = q[query_at, :]
        grad = do[here, :]
        queries = (jnp.where(low, query, zero), jnp.where(high, query, zero))
        grads = (jnp.where(low, grad, zero), jnp.where(high, grad, zero))
        product = jnp.where(valid, grad.astype(jnp.float32) * o[here, :].astype(jnp.float32), 0.0)
        upper = product.astype(jnp.bfloat16)
        lower = (product - upper.astype(jnp.float32)).astype(jnp.bfloat16)
        deltas = tuple((nt(m, upper) + nt(m, lower))[0:1, :] for m in (ones_a, ones_b))
        stats = (lse[0, 0:1, here], lse[0, 1:2, here])
        queries_cat = jnp.concatenate(queries, axis=0)
        grads_cat = jnp.concatenate(grads, axis=0)

        def step(key, value, first, second, mask):
            probs, dscores = [], []
            for query_h, grad_h, delta, stat in zip(queries, grads, deltas, stats):
                scores = nt(key, query_h)
                prob = jnp.exp2(scores * (scale * LOG2E) - stat)
                if mask is not None:
                    prob = jnp.where(mask, prob, 0.0)
                dprob = nt(value, grad_h)
                probs.append(prob.astype(jnp.bfloat16))
                dscores.append((prob * (dprob - delta)).astype(jnp.bfloat16))
            dscores_cat = jnp.concatenate(dscores, axis=1)
            dvalue = nn(jnp.concatenate(probs, axis=1), grads_cat)
            dkey = nn(dscores_cat, queries_cat)
            dquery = jnp.concatenate([nn(first, dscores[0]), nn(second, dscores[1])], axis=0)
            return dquery, dkey, dvalue

        def read(base):
            rows_at = pl.ds(pl.multiple_of(base, BK), BK)
            return kam[rows_at, :], vm[rows_at, :], kta[:, rows_at], ktc[:, rows_at]

        def accumulate(index, carry, mask):
            rows_at = pl.ds(pl.multiple_of(index * BK, BK), BK)
            dquery, dkey, dvalue = step(*read(index * BK), mask)
            dks[rows_at, :] += dkey
            dvs[rows_at, :] += dvalue
            return carry + dquery

        carry = jnp.zeros((128, size), jnp.float32)
        whole_blocks = at // BK
        carry = lax.fori_loop(0, whole_blocks, lambda i, c: accumulate(i, c, None), carry)
        row = lax.broadcasted_iota(jnp.int32, (BK, size), 0)
        column = lax.broadcasted_iota(jnp.int32, (BK, size), 1)
        if is_branch:
            carry = lax.fori_loop(
                whole_blocks,
                (at + BK - 1) // BK,
                lambda i, c: accumulate(i, c, row + i * BK < at),
                carry,
            )
            triangle = lax.broadcasted_iota(jnp.int32, (size, size), 0) <= lax.broadcasted_iota(
                jnp.int32, (size, size), 1
            )
            dquery, dkey, dvalue = step(kbm[...], vbm[...], ktab[...], ktcb[...], triangle)
            carry = carry + dquery
            dk[branch_part, :] = (dkey * scale).astype(dk.dtype)
            dv[branch_part, :] = dvalue.astype(dv.dtype)
        else:
            carry = accumulate(whole_blocks, carry, row + whole_blocks * BK <= column + at)
        dq[query_at, :] = (carry.T * scale).astype(dq.dtype)
    dk[prompt_part, :] = (dks[...] * scale).astype(dk.dtype)
    dv[prompt_part, :] = dvs[...].astype(dv.dtype)


def attention_backward(pos, q, k, v, o, do, lse, block, branch, after=()):
    total, width = q.shape
    span = total - branch
    rows = o.shape[0]
    pairs = pl.cdiv(width, 128)

    def col(n):
        return pl.BlockSpec((n, 128), lambda p, pos: (0, p))

    def scratch(n):
        wide = pltpu.VMEM((64, n), jnp.bfloat16)
        tall = pltpu.VMEM((n, 128), jnp.bfloat16)
        return [wide, wide, tall, tall]

    return pl.pallas_call(
        functools.partial(backward_kernel, block=block, branch=branch, width=width),
        grid_spec=pltpu.PrefetchScalarGridSpec(
            num_scalar_prefetch=1,
            grid=(pairs,),
            in_specs=[col(total)] * 3
            + [col(rows)] * 2
            + [pl.BlockSpec((1, 8, rows), lambda p, pos: (p, 0, 0))]
            + [pl.BlockSpec(memory_space=pl.ANY)] * len(after),
            out_specs=[col(total)] * 3,
            scratch_shapes=scratch(span)
            + scratch(branch)
            + [pltpu.VMEM((span, 128), jnp.float32), pltpu.VMEM((span, 128), jnp.float32)],
        ),
        out_shape=[jax.ShapeDtypeStruct((total, width), jnp.bfloat16)] * 3,
        compiler_params=pltpu.CompilerParams(
            dimension_semantics=("arbitrary",), vmem_limit_bytes=40 * 2**20
        ),
        cost_estimate=busy(10 * pairs),
        name="attention_backward",
    )(pos, q, k, v, o, do, lse, *after)


TILE = 256


def row_chunks(rows, size=256):
    return [slice(at, min(at + size, rows)) for at in range(0, rows, size)]


def fixed(shape):
    return pl.BlockSpec(shape, lambda *_: (0,) * len(shape), pipeline_mode=pl.Buffered(1))


def steady(shape):
    return pl.BlockSpec(shape, lambda *_: (0,) * len(shape))


def store_halves(value, half, keep, give):
    count, size = keep.shape[0], keep.shape[1]
    for block in range(count):
        first = value[2 * block * size : (2 * block + 1) * size, :]
        second = value[(2 * block + 1) * size : (2 * block + 2) * size, :]
        keep[block, :, :] = jnp.where(half == 0, first, second).astype(keep.dtype)
        give[block, :, :] = jnp.where(half == 0, second, first).astype(give.dtype)


def mlp_forward_kernel(
    mixed_a, mixed_b, tokens, out_w, out_bias, gain, shift, up, up_bias, down, down_bias, *rest
):
    hidden, slope, result, act_turned, norm, pace, act, acc = rest[-8:]
    step = pl.program_id(0)
    rows = tokens.shape[0]
    first = mixed_a.shape[1]

    @pl.when(step == 0)
    def _():
        for here in row_chunks(rows):
            resid = (
                tokens[here, :].astype(jnp.float32)
                + nn(mixed_a[here, :], out_w[:first, :])
                + nn(mixed_b[here, :], out_w[first:, :])
                + out_bias[...]
            )
            centred = resid - jnp.mean(resid, axis=1, keepdims=True)
            speed = lax.rsqrt(jnp.mean(centred * centred, axis=1, keepdims=True) + epsilon)
            normed = centred * speed
            acting = (normed * gain[...] + shift[...]).astype(jnp.bfloat16)
            act[here, :] = acting
            act_turned[:, here] = acting.T
            norm[here, :] = normed.astype(norm.dtype)
            pace[here, :] = jnp.broadcast_to(speed, (speed.shape[0], 128))
            acc[here, :] = resid + down_bias[...]

    for here in row_chunks(rows):
        pre = nn(act[here, :], up[...]) + up_bias[...]
        bell = jnp.exp2(pre * pre * (-0.5 * LOG2E))
        base = 1.0 + (0.3275911 * 0.7071067811865476) * jnp.abs(pre)
        t = pl.reciprocal(base, approx=True)
        t = t * (2.0 - base * t)
        series = t * (
            0.127414796 + t * (-0.142248368 + t * (0.7107068705 + t * (-0.7265760135 + t * 0.5307027145)))
        )
        tail = series * bell
        below = jnp.where(pre >= 0.0, 1.0 - tail, tail)
        exact = (pre * below).astype(jnp.bfloat16)
        hidden[here, :] = exact
        slope[here, :] = (below + pre * bell * 0.3989422804014327).astype(jnp.bfloat16)
        acc[here, :] += nt(exact, down[...])

    @pl.when(step == pl.num_programs(0) - 1)
    def _():
        result[...] = acc[...].astype(result.dtype)


def mlp_forward(
    mixed, tokens, out_w, out_bias, gain, shift, up, up_bias, down, down_bias, after=()
):
    rows, width = tokens.shape
    inner = up.shape[1]
    column = pl.BlockSpec((width, TILE), lambda j: (0, j))
    tall = pl.BlockSpec((rows, TILE), lambda j: (0, j))
    line = fixed((1, width))
    like = jax.ShapeDtypeStruct
    return pl.pallas_call(
        mlp_forward_kernel,
        grid=(inner // TILE,),
        in_specs=[
            fixed(mixed[0].shape),
            fixed(mixed[1].shape),
            fixed((rows, width)),
            fixed((width, width)),
            line,
            line,
            line,
            column,
            pl.BlockSpec((1, TILE), lambda j: (0, j)),
            column,
            line,
        ]
        + [pl.BlockSpec(memory_space=pl.ANY)] * len(after),
        out_specs=[
            tall,
            tall,
            steady((rows, width)),
            steady((width, rows)),
            steady((rows, width)),
            steady((rows, 128)),
        ],
        out_shape=[
            like((rows, inner), jnp.bfloat16),
            like((rows, inner), jnp.bfloat16),
            like((rows, width), jnp.bfloat16),
            like((width, rows), jnp.bfloat16),
            like((rows, width), jnp.bfloat16),
            like((rows, 128), jnp.float32),
        ],
        scratch_shapes=[pltpu.VMEM((rows, width), jnp.bfloat16), pltpu.VMEM((rows, width), jnp.float32)],
        compiler_params=pltpu.CompilerParams(
            dimension_semantics=("arbitrary",), vmem_limit_bytes=52 * 2**20
        ),
        cost_estimate=busy(50),
        name="mlp_forward",
    )(
        *mixed,
        tokens,
        out_w,
        *(v.reshape(1, width) for v in (out_bias, gain, shift)),
        up,
        up_bias.reshape(1, inner),
        down,
        down_bias.reshape(1, width),
        *after,
    )


def down_back_kernel(half, cot_turned, hidden, keep, give):
    store_halves(nn(cot_turned[...], hidden[...]), half[0], keep, give)


def down_back(half, count, cot_turned, hidden):
    width, rows = cot_turned.shape
    inner = hidden.shape[1]
    block = width // count // 2
    split = pl.BlockSpec((count, block, TILE), lambda j, half: (0, 0, j))
    return pl.pallas_call(
        down_back_kernel,
        grid_spec=pltpu.PrefetchScalarGridSpec(
            num_scalar_prefetch=1,
            grid=(inner // TILE,),
            in_specs=[fixed((width, rows)), pl.BlockSpec((rows, TILE), lambda j, half: (0, j))],
            out_specs=[split, split],
        ),
        out_shape=[jax.ShapeDtypeStruct((count, block, inner), jnp.bfloat16)] * 2,
        compiler_params=pltpu.CompilerParams(
            dimension_semantics=("arbitrary",), vmem_limit_bytes=32 * 2**20
        ),
        cost_estimate=busy(15),
        name="down_back",
    )(half, cot_turned, hidden)


def up_back_step(half, act_turned, cot, slope, up, down, total, keep, give, bias_grad):
    bias = jnp.zeros((1, TILE), jnp.float32)
    pieces = []
    for here in row_chunks(cot.shape[0]):
        d_pre = (nn(cot[here, :], down[...]) * slope[here, :].astype(jnp.float32)).astype(jnp.bfloat16)
        bias = bias + jnp.sum(d_pre.astype(jnp.float32), axis=0, keepdims=True)
        total[here, :] += nt(d_pre, up[...])
        pieces.append(d_pre)
    bias_grad[...] = bias
    store_halves(nn(act_turned[...], jnp.concatenate(pieces, axis=0)), half[0], keep, give)


def up_back_first_kernel(half, act_turned, cot, slope, up, down, total, keep, give, bias_grad):
    @pl.when(pl.program_id(0) == 0)
    def _():
        total[...] = jnp.zeros_like(total)

    up_back_step(half, act_turned, cot, slope, up, down, total, keep, give, bias_grad)


def up_back_last_kernel(
    half, act_turned, cot, slope, up, down, so_far, norm, pace, gain, mixed_a, mixed_b, out_w, *rest
):
    d_resid, d_mixed_a, d_mixed_b, keep, give, out_keep, out_give, bias_grad, lines = rest[-11:-2]
    d_branch, piece = rest[-2:]
    step = pl.program_id(0)
    rows, width = cot.shape
    first = mixed_a.shape[1]

    @pl.when(step == 0)
    def _():
        d_resid[...] = so_far[...]

    up_back_step(half, act_turned, cot, slope, up, down, d_resid, keep, give, bias_grad)

    @pl.when(step == pl.num_programs(0) - 1)
    def _():
        sums = [jnp.zeros((1, width), jnp.float32)] * 4
        for here in row_chunks(rows):
            grad = d_resid[here, :]
            normed = norm[here, :].astype(jnp.float32)
            scaled = grad * gain[...]
            inner = (
                scaled
                - jnp.mean(scaled, axis=1, keepdims=True)
                - normed * jnp.mean(scaled * normed, axis=1, keepdims=True)
            )
            exact = cot[here, :].astype(jnp.float32)
            total = exact + pace[here, 0:1] * inner
            d_resid[here, :] = total
            rounded = total.astype(jnp.bfloat16)
            d_branch[here, :] = rounded
            d_mixed_a[here, :] = nt(rounded, out_w[:first, :]).astype(d_mixed_a.dtype)
            d_mixed_b[here, :] = nt(rounded, out_w[first:, :]).astype(d_mixed_b.dtype)
            for n, term in enumerate((grad * normed, grad, rounded.astype(jnp.float32), exact)):
                sums[n] = sums[n] + jnp.sum(term, axis=0, keepdims=True)
        for n in range(4):
            lines[n : n + 1, :] = sums[n]
        for columns in row_chunks(width):
            size = columns.stop - columns.start
            piece[:first, :size] = tn(mixed_a[...], d_branch[:, columns])
            piece[first:, :size] = tn(mixed_b[...], d_branch[:, columns])
            value = piece[:, :size]
            store_halves(value, half[0], out_keep.at[:, :, columns], out_give.at[:, :, columns])


def up_back(half, count, tiles, act_turned, cot, slope, up, down, final=None, after=()):
    rows, width = cot.shape
    block = width // count // 2
    low, high = tiles
    inner = (high - low) * TILE
    split = pl.BlockSpec((count, block, TILE), lambda j, half: (0, 0, j))
    column = pl.BlockSpec((width, TILE), lambda j, half: (0, j + low))
    like = jax.ShapeDtypeStruct
    in_specs = [
        fixed((width, rows)),
        fixed((rows, width)),
        pl.BlockSpec((rows, TILE), lambda j, half: (0, j + low)),
        column,
        column,
    ]
    operands = [half, act_turned, cot, slope, up, down]
    out_specs = [steady((rows, width))]
    out_shape = [like((rows, width), jnp.float32)]
    scratch = []
    if final is not None:
        so_far, norm, pace, gain, mixed, out_w = final
        in_specs += [
            fixed((rows, width)),
            fixed((rows, width)),
            fixed((rows, 128)),
            fixed((1, width)),
            fixed(mixed[0].shape),
            fixed(mixed[1].shape),
            fixed((width, width)),
        ]
        operands += [so_far, norm, pace, gain.reshape(1, width), *mixed, out_w]
        out_specs += [steady(m.shape) for m in mixed]
        out_shape += [like(m.shape, jnp.bfloat16) for m in mixed]
        scratch = [pltpu.VMEM((rows, width), jnp.bfloat16), pltpu.VMEM((width, TILE), jnp.float32)]
    out_specs += [split] * 2
    out_shape += [like((count, block, inner), jnp.bfloat16)] * 2
    if final is not None:
        out_specs += [steady((count, block, width))] * 2
        out_shape += [like((count, block, width), jnp.bfloat16)] * 2
    out_specs += [pl.BlockSpec((1, TILE), lambda j, half: (0, j))]
    out_shape += [like((1, inner), jnp.float32)]
    if final is not None:
        out_specs += [steady((8, width))]
        out_shape += [like((8, width), jnp.float32)]
        in_specs += [pl.BlockSpec(memory_space=pl.ANY)] * len(after)
        operands += after
    return pl.pallas_call(
        up_back_first_kernel if final is None else up_back_last_kernel,
        grid_spec=pltpu.PrefetchScalarGridSpec(
            num_scalar_prefetch=1,
            grid=(high - low,),
            in_specs=in_specs,
            out_specs=out_specs,
            scratch_shapes=scratch,
        ),
        out_shape=out_shape,
        compiler_params=pltpu.CompilerParams(
            dimension_semantics=("arbitrary",), vmem_limit_bytes=58 * 2**20
        ),
        cost_estimate=busy(30 if final is None else 50),
        name="up_back_first" if final is None else "up_back_last",
    )(*operands)


def projection_tiles(widths):
    first, second = (pl.cdiv(w, TILE) for w in widths)
    return first, second, [
        lambda t, *_: jnp.minimum(t, first - 1),
        lambda t, *_: jnp.maximum(t - first, 0),
    ]


def tile_of(ref, place, width):
    value = ref[...]
    if width % TILE == 0:
        return value
    lane = lax.broadcasted_iota(jnp.int32, (1, TILE), 1)
    return jnp.where(lane < width - place * TILE, value, jnp.zeros((), value.dtype))


def tokens_back_kernel(*refs, widths):
    grads, weights = (refs[0:3], refs[3:6]), (refs[6:9], refs[9:12])
    out, acc = refs[-2:]
    step = pl.program_id(0)
    first, second, _ = projection_tiles(widths)

    @pl.when(step == 0)
    def _():
        acc[...] = jnp.zeros_like(acc)

    for group in range(2):

        @pl.when(step < first if group == 0 else step >= first)
        def _():
            place = step if group == 0 else step - first
            weight = jnp.concatenate([tile_of(w, place, widths[group]) for w in weights[group]], axis=1)
            lane = lax.broadcasted_iota(jnp.int32, (1, TILE), 1)
            for here in row_chunks(acc.shape[0]):
                parts = []
                for ref in grads[group]:
                    part = ref[here, :]
                    if widths[group] % TILE:
                        part = jnp.where(lane < widths[group] - place * TILE, part, jnp.zeros((), part.dtype))
                    parts.append(part)
                acc[here, :] += nt(jnp.concatenate(parts, axis=1), weight)

    @pl.when(step == pl.num_programs(0) - 1)
    def _():
        out[...] = acc[...].astype(out.dtype)


def tokens_back(grads, weights, after=()):
    total = grads[0][0].shape[0]
    width = weights[0][0].shape[0]
    widths = [group[0].shape[1] for group in grads]
    first, second, places = projection_tiles(widths)

    def tiles(rows):
        return [pl.BlockSpec((rows, TILE), lambda t, at=at: (0, at(t))) for at in places for _ in range(3)]

    return pl.pallas_call(
        functools.partial(tokens_back_kernel, widths=widths),
        grid=(first + second,),
        in_specs=tiles(total) + tiles(width) + [pl.BlockSpec(memory_space=pl.ANY)] * len(after),
        out_specs=steady((total, width)),
        out_shape=jax.ShapeDtypeStruct((total, width), jnp.bfloat16),
        scratch_shapes=[pltpu.VMEM((total, width), jnp.float32)],
        compiler_params=pltpu.CompilerParams(
            dimension_semantics=("arbitrary",), vmem_limit_bytes=52 * 2**20
        ),
        cost_estimate=busy(20),
        name="tokens_back",
    )(*grads[0], *grads[1], *weights[0], *weights[1], *after)


def weights_back_kernel(half, turned, *refs, tiles):
    outs = refs[-6:]
    step = pl.program_id(0)
    for group in range(2):
        keep, give, bias = outs[group * 3 : group * 3 + 3]
        start, size = group * 3 * tiles[0], tiles[group]
        for kind in range(3):
            grad = refs[group * 3 + kind]

            @pl.when(jnp.logical_and(step >= start + kind * size, step < start + (kind + 1) * size))
            def _():
                part = grad[...]
                store_halves(nn(turned[...], part), half[0], keep, give)
                bias[...] = jnp.sum(part.astype(jnp.float32), axis=0, keepdims=True)


def weights_back(half, count, turned, grads, after=()):
    width, total = turned.shape
    tiles = [pl.cdiv(group[0].shape[1], TILE) for group in grads]
    block = width // count // 2
    like = jax.ShapeDtypeStruct
    in_specs, out_specs, out_shape = [], [], []
    for group in range(2):
        start, size = group * 3 * tiles[0], tiles[group]
        for kind in range(3):
            at = start + kind * size
            in_specs.append(
                pl.BlockSpec(
                    (total, TILE), lambda t, half, at=at, size=size: (0, jnp.clip(t - at, 0, size - 1))
                )
            )

        def place(t, start=start, size=size):
            return jnp.clip(t - start, 0, 3 * size - 1)

        out_specs += [
            pl.BlockSpec((count, block, TILE), lambda t, half, place=place: (0, 0, place(t)))
        ] * 2 + [pl.BlockSpec((1, TILE), lambda t, half, place=place: (0, place(t)))]
        columns = 3 * size * TILE
        out_shape += [like((count, block, columns), jnp.bfloat16)] * 2 + [like((1, columns), jnp.float32)]
    return pl.pallas_call(
        functools.partial(weights_back_kernel, tiles=tiles),
        grid_spec=pltpu.PrefetchScalarGridSpec(
            num_scalar_prefetch=1,
            grid=(3 * sum(tiles),),
            in_specs=[fixed((width, total))]
            + in_specs
            + [pl.BlockSpec(memory_space=pl.ANY)] * len(after),
            out_specs=out_specs,
        ),
        out_shape=out_shape,
        compiler_params=pltpu.CompilerParams(
            dimension_semantics=("arbitrary",), vmem_limit_bytes=52 * 2**20
        ),
        cost_estimate=busy(25),
        name="weights_back",
    )(half, turned, *grads[0], *grads[1], *after)


def rows_back_kernel(others, own, rows, resid, gain, prompt_out, branch_out):
    step = pl.program_id(0)
    last = pl.num_programs(0) - 1
    values = rows[...].astype(jnp.float32)
    centred = values - jnp.mean(values, axis=1, keepdims=True)
    pace = lax.rsqrt(jnp.mean(centred * centred, axis=1, keepdims=True) + epsilon)
    normed = centred * pace
    grad = own[...].astype(jnp.float32) + jnp.where(step == last, 0.0, others[...].astype(jnp.float32))
    scaled = grad * gain[...]
    inner = (
        scaled
        - jnp.mean(scaled, axis=1, keepdims=True)
        - normed * jnp.mean(scaled * normed, axis=1, keepdims=True)
    )
    turned = (resid[...] + pace * inner).T

    @pl.when(step < last)
    def _():
        prompt_out[...] = turned

    @pl.when(step == last)
    def _():
        branch_out[...] = turned


def rows_back(others, own, rows, resid, gain, branch):
    total, width = own.shape
    shard = total - branch
    steps = shard // branch
    tall = pl.BlockSpec((branch, width), lambda t: (t, 0))
    return pl.pallas_call(
        rows_back_kernel,
        grid=(steps + 1,),
        in_specs=[
            pl.BlockSpec((branch, width), lambda t: (jnp.minimum(t, steps - 1), 0)),
            tall,
            tall,
            tall,
            fixed((1, width)),
        ],
        out_specs=[
            pl.BlockSpec((width, branch), lambda t: (0, jnp.minimum(t, steps - 1))),
            pl.BlockSpec((width, branch), lambda t: (0, 0)),
        ],
        out_shape=[
            jax.ShapeDtypeStruct((width, shard), jnp.float32),
            jax.ShapeDtypeStruct((width, branch), jnp.float32),
        ],
        compiler_params=pltpu.CompilerParams(
            dimension_semantics=("arbitrary",), vmem_limit_bytes=40 * 2**20
        ),
        cost_estimate=busy(10),
        name="rows_back",
    )(others, own, rows, resid, gain.reshape(1, width))


def gate_kernel(*refs):
    pass


def gate(value, after):
    if not after:
        return value
    anywhere = pl.BlockSpec(memory_space=pl.ANY)
    return pl.pallas_call(
        gate_kernel,
        in_specs=[anywhere] * (1 + len(after)),
        out_specs=anywhere,
        out_shape=jax.ShapeDtypeStruct(value.shape, value.dtype),
        input_output_aliases={0: 0},
        cost_estimate=busy(1),
        name="gate",
    )(value, *after)


def normalise(values_in):
    centre = jnp.mean(values_in, axis=-1, keepdims=True)
    centred = values_in - centre
    spread = jnp.mean(centred * centred, axis=-1, keepdims=True)
    pace = lax.rsqrt(spread + epsilon)
    return centred * pace, pace


def swap(value, axis, bit):
    count = lax.axis_size(axis)
    return lax.ppermute(value, axis, [(i, i ^ bit) for i in range(count)])


def ahead(value, axis, step):
    count = lax.axis_size(axis)
    return lax.ppermute(value, axis, [(i, (i + step) % count) for i in range(count)])


def total_over(value, axes):
    for axis in axes:
        count = lax.axis_size(axis)
        if count & (count - 1):
            value = lax.psum(value, axis)
            continue
        bit = 1
        while bit < count:
            value = value + swap(value, axis, bit)
            bit *= 2
    return value


def by_halves(half_width):
    return lax.axis_size("dp") == 4 and lax.axis_size("gy") == 2 and half_width > GROUP


def half_index():
    return lax.axis_index("dp") % 2


def pair_rows(mine, theirs):
    first = half_index() == 0
    return jnp.stack([jnp.where(first, mine, theirs), jnp.where(first, theirs, mine)], axis=-3)


def gather_plain(part):
    part = lax.all_gather(part, "gy", axis=1, tiled=True)
    return lax.all_gather(part, "gx", axis=0, tiled=True)


def gather_quarters(part):
    rows, columns = part.shape
    copies, gx, gy = (lax.axis_size(axis) for axis in ("dp", "gx", "gy"))
    size = columns // copies
    mine = lax.dynamic_slice_in_dim(part, lax.axis_index("dp") * size, size, 1)
    raw = lax.all_gather(mine, ("dp", "gx", "gy"))
    got = raw.reshape(copies, gx, gy, rows, size)
    return raw, [
        [got[quarter, :, side].reshape(gx * rows, size) for quarter in range(copies)]
        for side in range(gy)
    ]


def gather_projections(qkv_part, out_part, width):
    rows = qkv_part.shape[0]
    half = width // 2
    first_side = lax.axis_index("gy") == 0
    key_at = width - half
    here = jnp.where(
        first_side,
        qkv_part[:, :GROUP],
        qkv_part[:, half : half + GROUP],
    )
    keys_here = jnp.where(first_side, qkv_part[:, width : width + GROUP], qkv_part[:, :GROUP])
    raw, one = gather_quarters(jnp.concatenate([here, keys_here], axis=1))
    rest = width - GROUP
    spare = half - GROUP
    queries_rest = jnp.where(first_side, qkv_part[:, GROUP:width], qkv_part[:, half + GROUP :])
    keys_rest = jnp.where(first_side, qkv_part[:, width + GROUP :], qkv_part[:, GROUP:half])

    def pad(value, size):
        return jnp.pad(value, ((0, 0), (0, size - value.shape[1])))

    outer = pl.cdiv(rest + spare, 128) * 128
    out_size = pl.cdiv(half, 128) * 128
    total = pl.cdiv(outer + out_size, 512) * 512
    packed = pad(jnp.concatenate([queries_rest, keys_rest], axis=1), outer)
    packed = pad(jnp.concatenate([packed, pad(out_part, out_size)], axis=1), total)
    two = [jnp.concatenate(side, axis=1) for side in gather_quarters(packed)[1]]
    first = [
        jnp.concatenate(one[0][:2], axis=1),
        jnp.concatenate(one[0][2:], axis=1),
        jnp.concatenate(one[1][:2], axis=1),
    ]
    second = [
        two[0][:, :rest],
        jnp.concatenate(
            [two[0][:, rest : rest + spare]] + one[1][2:] + [two[1][:, rest : rest + spare]], axis=1
        ),
        two[1][:, :rest],
    ]
    out_full = jnp.concatenate([side[:, outer : outer + half] for side in two], axis=1)
    return [first, second], out_full, raw


def gather_feed_forward(up_part, down_part, after):
    columns = up_part.shape[1]
    shared = columns // 2 // 512 * 512
    _, quarters = gather_quarters(jnp.concatenate([up_part[:, :shared], down_part[:, :shared]], axis=1))
    first_half = half_index() == 0
    first_side = lax.axis_index("gy") == 0
    mine = gate(jnp.where(first_half, up_part[:, shared:], down_part[:, shared:]), after)
    rows, size = mine.shape
    count = lax.axis_size("gx")
    here = lax.axis_index("gx")
    blocks = jnp.zeros((count, rows, size), mine.dtype)
    for step in range(count):
        got = mine if step == 0 else ahead(mine, "gx", step)
        blocks = lax.dynamic_update_index_in_dim(blocks, got, (here - step) % count, 0)
    own = blocks.reshape(count * rows, size)
    theirs = swap(own, "gy", 1)
    sides = (jnp.where(first_side, own, theirs), jnp.where(first_side, theirs, own))
    others = [swap(side, "dp", 1) for side in sides]
    ups = [jnp.where(first_half, a, b) for a, b in zip(sides, others)]
    downs = [jnp.where(first_half, b, a) for a, b in zip(sides, others)]
    wholes = []
    for pieces, rest in ((slice(0, 2), ups), (slice(2, 4), downs)):
        wholes.append(
            jnp.concatenate([p for side in range(2) for p in quarters[side][pieces] + [rest[side]]], axis=1)
        )
    return wholes, own


def core_step(keep, give):
    return add(keep, swap(give, "dp", 1))


def both_halves(keep, give):
    count, size, columns = keep.shape
    return jnp.stack([keep, give], axis=1).reshape(2 * count * size, columns)


def add(a, b):
    return (a.astype(jnp.float32) + b.astype(jnp.float32)).astype(jnp.bfloat16)


def chips_step(sides):
    columns = sides[0].shape[-1]
    size = pl.cdiv(columns // 128, 2) * 128
    own_first = lax.axis_index("dp") // 2 == 0
    first, second = (
        jnp.concatenate([side[..., at : at + size] for side in sides], axis=-1) for at in (0, columns - size)
    )
    return add(jnp.where(own_first, first, second), swap(jnp.where(own_first, second, first), "dp", 2))


def two(value):
    size = value.shape[-1] // 2
    return value[..., :size], value[..., size:]


def overlap_join(value, columns):
    size = value.shape[-1]
    other = swap(value, "dp", 2)
    own_first = lax.axis_index("dp") // 2 == 0
    first, second = jnp.where(own_first, value, other), jnp.where(own_first, other, value)
    return jnp.concatenate([first, second[..., 2 * size - columns :]], axis=-1)


def blocks_step(value):
    count = lax.axis_size("gx")
    here = lax.axis_index("gx")
    total = lax.dynamic_index_in_dim(value, here, 0, False).astype(jnp.float32)
    for step in range(1, count):
        give = lax.dynamic_index_in_dim(value, (here + step) % count, 0, False)
        total = total + ahead(give, "gx", step).astype(jnp.float32)
    return total.astype(jnp.bfloat16)


def copies_step(value):
    bit = 2
    while bit < lax.axis_size("dp"):
        value = add(value, swap(value, "dp", bit))
        bit *= 2
    return value


def join_step(value):
    columns = value.shape[-1]
    return pair_rows(value, swap(value, "dp", 1)).reshape(-1, columns).astype(jnp.float32)


def side_exchange(first, second):
    first_side = lax.axis_index("gy") == 0
    keep = jnp.where(first_side, first, second)
    return add(keep, swap(jnp.where(first_side, second, first), "gy", 1))


def projection_sides(first, rest):
    query, key, value = (first[..., n * GROUP : (n + 1) * GROUP] for n in range(3))
    size = rest.shape[-1] // 3
    query_rest, key_rest, value_rest = (rest[..., n * size : n * size + GROUP + 128] for n in range(3))
    return (
        jnp.concatenate([query, key, query_rest, key_rest[..., :128]], axis=-1),
        jnp.concatenate([value, key_rest, value_rest], axis=-1),
    )


def join_projections(whole, width):
    rest = width - GROUP
    spare = width // 2 - GROUP
    wide = GROUP + 128
    query, key = whole[:, :GROUP], whole[:, GROUP : 2 * GROUP]
    query_rest = whole[:, 2 * GROUP : 2 * GROUP + rest]
    key_spare = whole[:, 2 * GROUP + wide : 2 * GROUP + wide + spare]
    value = whole[:, :GROUP]
    key_rest = whole[:, GROUP + spare : GROUP + rest]
    value_rest = whole[:, GROUP + wide : GROUP + wide + rest]
    return jnp.where(
        lax.axis_index("gy") == 0,
        jnp.concatenate([query, query_rest, key, key_spare], axis=1),
        jnp.concatenate([key_rest, value, value_rest], axis=1),
    )


def scatter_plain(whole):
    part = lax.psum_scatter(whole, "gy", scatter_dimension=1, tiled=True)
    part = lax.psum_scatter(part, "gx", scatter_dimension=0, tiled=True)
    return lax.psum(part, "dp").astype(jnp.float32)


def all_tokens(own):
    count = lax.axis_size("gy")
    here = lax.axis_index("gy")
    if count != 2:
        return lax.all_gather(own, "gy", axis=0, tiled=True)
    other = swap(own, "gy", 1)
    first = here == 0
    return jnp.concatenate([jnp.where(first, own, other), jnp.where(first, other, own)], axis=0)


def others_tokens(whole):
    count = lax.axis_size("gy")
    here = lax.axis_index("gy")
    rows = whole.shape[0] // count
    if count != 2:
        keep = lax.dynamic_slice_in_dim(whole, here * rows, rows, 0)
        total = lax.psum_scatter(whole, "gy", scatter_dimension=0, tiled=True)
        return (total.astype(jnp.float32) - keep.astype(jnp.float32)).astype(jnp.bfloat16)
    return swap(lax.dynamic_slice_in_dim(whole, (1 - here) * rows, rows, 0), "gy", 1)


def dot(a, b):
    return jnp.dot(a, b, preferred_element_type=jnp.float32)


def local(
    prompt,
    continuations,
    prefix_len,
    attn_gain,
    attn_shift,
    qkv_weight,
    query_bias,
    value_bias,
    out_weight,
    out_bias,
    mlp_gain,
    mlp_shift,
    up_weight,
    up_bias,
    down_weight,
    down_bias,
    grad_prompt,
    grad_continuations,
):
    groups, shard, width = prompt.shape
    length = continuations.shape[1]
    first_pos = lax.axis_index("gy") * shard
    prompt_len = shard * lax.axis_size("gy")
    block = shard // 2
    halved = by_halves(width // 2)
    spans = [slice(0, GROUP), slice(GROUP, width)]

    if halved:
        limit, other_limit = prefix_len[0], swap(prefix_len, "gy", 1)[0]
        is_first = first_pos == 0
        is_long = jnp.logical_or(limit > other_limit, jnp.logical_and(limit == other_limit, is_first))
        kept_at = jnp.where(is_long, 0, block)
        places = [first_pos + kept_at, shard - first_pos + kept_at, limit]
    else:
        places = [first_pos, first_pos + block, prefix_len[0]]
    places = jnp.stack(places).astype(jnp.int32)

    def kept_rows(own):
        return lax.dynamic_slice_in_dim(own, kept_at, block, 0)

    def given_rows(own):
        return lax.dynamic_slice_in_dim(own, block - kept_at, block, 0)

    def back_home(done):
        if not halved:
            return done
        kept, home = done[:block], swap(done[block:], "gy", 1)
        return jnp.concatenate([jnp.where(is_long, kept, home), jnp.where(is_long, home, kept)], axis=0)

    own_prompt = prompt.reshape(shard, width)
    branch = continuations.reshape(length, width)
    own_cot = grad_prompt.reshape(shard, width)
    branch_cot = grad_continuations.reshape(length, width)
    whole_prompt = all_tokens(own_prompt)
    if halved:
        weights, out_full, raw = gather_projections(qkv_weight, out_weight, width)
        (up_full, down_full), fetched = gather_feed_forward(up_weight, down_weight.T, (raw,))
        fetched = (fetched,)
        other_cot = swap(gate(given_rows(own_cot), (raw,)), "gy", 1)
        cotangent = jnp.concatenate([kept_rows(own_cot), other_cot, branch_cot], axis=0)
    else:
        qkv = gather_plain(qkv_weight)
        weights = [[qkv[:, c.start + s : c.stop + s] for s in (0, width, 2 * width)] for c in spans]
        out_full, up_full, down_full = (gather_plain(w) for w in (out_weight, up_weight, down_weight.T))
        fetched = ()
        cotangent = jnp.concatenate([own_cot, branch_cot], axis=0)

    all_rows = jnp.concatenate([whole_prompt, branch], axis=0)
    norm_all, _ = normalise(all_rows.astype(jnp.float32))
    act_all = (norm_all * attn_gain + attn_shift).astype(jnp.bfloat16)
    projected, mixed, stats = [], [], []
    for number, (cols, (w_query, w_key, w_value)) in enumerate(zip(spans, weights)):
        projected.append(
            (
                (dot(act_all, w_query) + query_bias[cols]).astype(jnp.bfloat16),
                dot(act_all, w_key).astype(jnp.bfloat16),
                (dot(act_all, w_value) + value_bias[cols]).astype(jnp.bfloat16),
            )
        )
        got, stat = attention_forward(
            places, *projected[-1], block, length, fetched if number == 1 else ()
        )
        mixed.append(got)
        stats.append(stat)

    tokens = jnp.concatenate(
        [lax.dynamic_slice_in_dim(whole_prompt, places[n], block, 0) for n in range(2)] + [branch], axis=0
    )
    hidden, slope, result, act_turned, norm_two, pace_two = mlp_forward(
        mixed, tokens, out_full, out_bias, mlp_gain, mlp_shift, up_full, up_bias, down_full, down_bias
    )
    prompt_out = back_home(result[:shard]).reshape(groups, shard, width)
    continuation_out = result[shard:].reshape(1, length, width)

    count = lax.axis_size("gx")
    half = jnp.reshape(half_index() if halved else 0, (1,)).astype(jnp.int32)
    tiles = up_full.shape[1] // TILE
    part = tiles // 2
    down_keep, down_give = down_back(half, count, cotangent.T, hidden)
    after = ()
    if halved:
        down_flow = core_step(down_keep, down_give)
        after = (down_flow,)
    so_far, up_keep, up_give, up_bias_grad = up_back(
        half, count, (0, part), act_turned, cotangent, slope, up_full, down_full
    )
    d_resid, *d_mixed, keep_rest, give_rest, out_keep, out_give, bias_rest, lines = up_back(
        half,
        count,
        (part, tiles),
        act_turned,
        cotangent,
        slope,
        up_full,
        down_full,
        (so_far, norm_two, pace_two, mlp_gain, mixed, out_full),
        after,
    )
    up_bias_grad = jnp.concatenate([up_bias_grad, bias_rest], axis=1)
    mlp_gain_grad, mlp_shift_grad, out_bias_grad, down_bias_grad = (lines[n] for n in range(4))
    if halved:
        side = up_weight.shape[1]
        down_flow = chips_step((down_flow[..., :side], down_flow[..., side:]))
        up_flow = jnp.concatenate([core_step(up_keep, up_give), core_step(keep_rest, give_rest)], axis=-1)
        out_flow = core_step(out_keep, out_give)
        after = (down_flow, up_flow, out_flow)
    d_parts = [None, None]
    for number in (1, 0):
        d_parts[number] = attention_backward(
            places, *projected[number], mixed[number], d_mixed[number], stats[number], block, length, after
        )
        if halved and number == 1:
            up_flow = side_exchange(
                jnp.concatenate([up_flow[..., :side], out_flow[..., : width // 2]], axis=-1),
                jnp.concatenate([up_flow[..., side:], out_flow[..., width // 2 :]], axis=-1),
            )
            down_flow = blocks_step(down_flow)
            after = (up_flow, down_flow)
        if halved and number == 0:
            up_flow, down_flow = blocks_step(up_flow), side_exchange(*two(down_flow))
            after = (up_flow, down_flow)
    keep_a, give_a, bias_a, keep_b, give_b, bias_b = weights_back(half, count, act_all.T, d_parts, after)
    d_act_all = tokens_back(d_parts, weights, (keep_a,))
    others = others_tokens(d_act_all[:prompt_len])
    size = bias_b.shape[1] // 3
    query_bias_grad, value_bias_grad = (
        jnp.concatenate(
            [bias_a[0, n * GROUP : (n + 1) * GROUP], bias_b[0, n * size : n * size + width - GROUP]]
        )
        for n in (0, 2)
    )
    if halved:
        sides = projection_sides(core_step(keep_a, give_a), core_step(keep_b, give_b))
        qkv_flow = blocks_step(side_exchange(*two(chips_step(sides))))
        qkv_total = join_projections(join_step(overlap_join(qkv_flow, sides[0].shape[-1])), width)
        up_total = join_step(copies_step(up_flow))
        up_total, out_total = up_total[:, :side], up_total[:, side:]
        down_total = join_step(overlap_join(down_flow, side))
    else:
        whole_a, whole_b = both_halves(keep_a, give_a), both_halves(keep_b, give_b)
        qkv_grad = jnp.concatenate(
            [
                piece
                for n in range(3)
                for piece in (
                    whole_a[:, n * GROUP : (n + 1) * GROUP],
                    whole_b[:, n * size : n * size + width - GROUP],
                )
            ],
            axis=1,
        )
        up_total, down_total, out_total, qkv_total = (
            scatter_plain(g)
            for g in (
                jnp.concatenate([both_halves(up_keep, up_give), both_halves(keep_rest, give_rest)], axis=1),
                both_halves(down_keep, down_give),
                both_halves(out_keep, out_give),
                qkv_grad,
            )
        )
    d_act_exact = d_act_all.astype(jnp.float32)
    attn_gain_grad = jnp.sum(d_act_exact * norm_all, axis=0)
    attn_shift_grad = jnp.sum(d_act_exact, axis=0)
    prompt_resid = d_resid[:shard]
    if halved:
        home = back_home(prompt_resid.astype(jnp.bfloat16)).astype(jnp.float32)
        kept = jnp.where(is_long, prompt_resid[:block], home[:block]), jnp.where(
            is_long, home[block:], prompt_resid[:block]
        )
        prompt_resid = jnp.concatenate(kept, axis=0)
    own_rows = jnp.concatenate([own_prompt, branch], axis=0)
    own_grad = jnp.concatenate(
        [lax.dynamic_slice_in_dim(d_act_all, first_pos, shard, 0), d_act_all[prompt_len:]], axis=0
    )
    resid_rows = jnp.concatenate([prompt_resid, d_resid[shard:]], axis=0)
    prompt_grad, branch_grad = rows_back(others, own_grad, own_rows, resid_rows, attn_gain, length)
    prompt_grad = prompt_grad.T.reshape(groups, shard, width)
    continuation_grad = branch_grad.T.reshape(1, length, width)
    vectors = (
        attn_gain_grad,
        attn_shift_grad,
        query_bias_grad,
        value_bias_grad,
        out_bias_grad,
        mlp_gain_grad,
        mlp_shift_grad,
        up_bias_grad.reshape(-1),
        down_bias_grad,
    )
    joined = total_over(jnp.concatenate(vectors), ("dp", "gy", "gx"))
    totals = []
    at = 0
    for vector in vectors:
        totals.append(joined[at : at + vector.shape[0]])
        at += vector.shape[0]
    return (
        prompt_out,
        continuation_out,
        prompt_grad,
        continuation_grad,
        totals[0],
        totals[1],
        qkv_total,
        totals[2],
        totals[3],
        out_total,
        totals[4],
        totals[5],
        totals[6],
        up_total,
        totals[7],
        down_total.T,
        totals[8],
    )


def solution(mesh):
    placed = (
        P(("dp", "gx"), "gy", None),
        P(("dp", "gx", "gy"), None, None),
        P(("dp", "gx", "gy")),
        P(),
        P(),
        P("gx", "gy"),
        P(),
        P(),
        P("gx", "gy"),
        P(),
        P(),
        P(),
        P("gx", "gy"),
        P(),
        P("gy", "gx"),
        P(),
        P(("dp", "gx"), "gy", None),
        P(("dp", "gx", "gy"), None, None),
    )
    return jax.shard_map(
        local,
        mesh=mesh,
        in_specs=placed,
        out_specs=(
            P(("dp", "gx"), "gy", None),
            P(("dp", "gx", "gy"), None, None),
            P(("dp", "gx"), "gy", None),
            P(("dp", "gx", "gy"), None, None),
            P(),
            P(),
            P("gx", "gy"),
            P(),
            P(),
            P("gx", "gy"),
            P(),
            P(),
            P(),
            P("gx", "gy"),
            P(),
            P("gy", "gx"),
            P(),
        ),
        check_vma=False,
    )
```

```python
import functools
import jax
import jax.numpy as jnp
from jax import lax
from jax.sharding import PartitionSpec as P
from jax.experimental import pallas as pl
from jax.experimental.pallas import tpu as pltpu

HEAD_DIM = 64
LOG2E = 1.4426950408889634
NEG = -1e30
BK = 512
GROUP = 512
epsilon = 1e-05


def nt(a, b):
    return lax.dot_general(a, b, (((1,), (1,)), ((), ())), preferred_element_type=jnp.float32)


def nn(a, b):
    return jnp.dot(a, b, preferred_element_type=jnp.float32)


def tn(a, b):
    return lax.dot_general(a, b, (((0,), (0,)), ((), ())), preferred_element_type=jnp.float32)


def halves(pair, total):
    lane = lax.broadcasted_iota(jnp.int32, (1, 128), 1)
    left = jnp.minimum(total - pair * 128, 128)
    return lane < 64, jnp.logical_and(lane >= 64, lane < left), lane < left


def norm_bounds(ref, valid, spread):
    part = jnp.where(valid, ref[...], jnp.zeros((), jnp.bfloat16))
    return jnp.max(nn(part * part, spread), axis=0, keepdims=True)


def query_rows(pos, number, size, span, is_branch):
    if is_branch:
        return pl.ds(span, size)
    return pl.ds(pl.multiple_of(pos[number], size), size)


def forward_kernel(pos, q, k, v, *rest, block, branch, width):
    o, lse, va, vc, vab, vcb, tops, accs = rest[-8:]
    pair = pl.program_id(0)
    scale = HEAD_DIM ** (-0.5) * LOG2E
    low, high, valid = halves(pair, width)
    zero = jnp.zeros((), jnp.bfloat16)
    one = jnp.ones((), jnp.bfloat16)
    span = k.shape[0] - branch
    for part, first, second in ((slice(0, span), va, vc), (slice(span, None), vab, vcb)):
        whole = v[part, :]
        first[...] = jnp.where(low, whole, one)
        second[...] = jnp.where(low, one, jnp.where(high, whole, zero))
    spread = (
        (lax.broadcasted_iota(jnp.int32, (128, 128), 0) < 64)
        == (lax.broadcasted_iota(jnp.int32, (128, 128), 1) < 64)
    ).astype(jnp.bfloat16)
    bound = jnp.max(norm_bounds(k, valid, spread) * norm_bounds(q, valid, spread)) * (scale * scale)
    plain = bound < 90.0 * 90.0
    rows = o.shape[0]
    blocks = [(start, block, False) for start in range(0, rows - branch, block)]
    blocks.append((rows - branch, branch, True))

    def finish(start, size, acc_a, acc_b, top):
        total = pltpu.roll(jnp.where(low, acc_b, acc_a), 64, 1)
        o[start : start + size, :] = (jnp.where(low, acc_a, acc_b) / total).astype(o.dtype)
        turned = (top + jnp.log2(total)).T
        lse[0, 0:1, start : start + size] = turned[0:1, :]
        lse[0, 1:2, start : start + size] = turned[64:65, :]

    def setup(number, start, size, is_branch):
        at = pos[number]
        query = q[query_rows(pos, number, size, span, is_branch), :]
        queries = (jnp.where(low, query, zero), jnp.where(high, query, zero))
        row = lax.broadcasted_iota(jnp.int32, (size, BK), 0)
        column = lax.broadcasted_iota(jnp.int32, (size, BK), 1)
        triangle = lax.broadcasted_iota(jnp.int32, (size, size), 1) <= lax.broadcasted_iota(
            jnp.int32, (size, size), 0
        )
        whole_blocks = at // BK

        def allowed(index):
            if is_branch:
                return column + index * BK < at
            return column + index * BK <= row + at

        end = (at + BK - 1) // BK if is_branch else whole_blocks + 1
        return queries, triangle, whole_blocks, allowed, end

    def read(index):
        rows_at = pl.ds(pl.multiple_of(index * BK, BK), BK)
        return jnp.where(valid, k[rows_at, :], zero), va[rows_at, :], vc[rows_at, :]

    def own():
        return jnp.where(valid, k[span:, :], zero), vab[...], vcb[...]

    @pl.when(plain)
    def _():
        for number, (start, size, is_branch) in enumerate(blocks):
            queries, triangle, whole_blocks, allowed, end = setup(number, start, size, is_branch)

            def step(key, first, second, carry, mask):
                out = []
                for query_h, value_h, acc in zip(queries, (first, second), carry):
                    probs = jnp.exp2(nt(query_h, key) * scale)
                    if mask is not None:
                        probs = jnp.where(mask, probs, 0.0)
                    out.append(acc + nn(probs.astype(jnp.bfloat16), value_h))
                return tuple(out)

            carry = (jnp.zeros((size, 128), jnp.float32),) * 2
            carry = lax.fori_loop(0, whole_blocks, lambda i, c: step(*read(i), c, None), carry)
            if is_branch:
                carry = lax.fori_loop(
                    whole_blocks, end, lambda i, c: step(*read(i), c, allowed(i)), carry
                )
                carry = step(*own(), carry, triangle)
            else:
                carry = step(*read(whole_blocks), carry, allowed(whole_blocks))
            finish(start, size, *carry, 0.0)

    @pl.when(jnp.logical_not(plain))
    def _():
        for number, (start, size, is_branch) in enumerate(blocks):
            queries, triangle, whole_blocks, allowed, end = setup(number, start, size, is_branch)

            def step(key, first, second, mask):
                for head, value_h in enumerate((first, second)):
                    top = tops[head, 0:size, :]
                    scores = jnp.where(mask, nt(queries[head], key), NEG)
                    new_top = jnp.maximum(top, jnp.max(scores, axis=1, keepdims=True))
                    probs = jnp.exp2((scores - new_top[:, 0:1]) * scale).astype(jnp.bfloat16)
                    fade = jnp.exp2((top - new_top) * scale)
                    accs[head, 0:size, :] = accs[head, 0:size, :] * fade + nn(probs, value_h)
                    tops[head, 0:size, :] = new_top

            accs[:, 0:size, :] = jnp.zeros((2, size, 128), jnp.float32)
            tops[:, 0:size, :] = jnp.full((2, size, 128), NEG, jnp.float32)

            @pl.loop(0, end)
            def _(index):
                step(*read(index), allowed(index))

            if is_branch:
                step(*own(), triangle)
            top = jnp.where(low, tops[0, 0:size, :], tops[1, 0:size, :]) * scale
            finish(start, size, accs[0, 0:size, :], accs[1, 0:size, :], top)


def busy(microseconds):
    return pl.CostEstimate(
        flops=int(microseconds * 1.0e9), bytes_accessed=int(microseconds * 1.0e6), transcendentals=0
    )


def attention_forward(pos, q, k, v, block, branch, after=()):
    total, width = q.shape
    span = total - branch
    rows = block * (pos.shape[0] - 1) + branch
    pairs = pl.cdiv(width, 128)

    def col(n):
        return pl.BlockSpec((n, 128), lambda p, pos: (0, p))

    return pl.pallas_call(
        functools.partial(forward_kernel, block=block, branch=branch, width=width),
        grid_spec=pltpu.PrefetchScalarGridSpec(
            num_scalar_prefetch=1,
            grid=(pairs,),
            in_specs=[col(total)] * 3 + [pl.BlockSpec(memory_space=pl.ANY)] * len(after),
            out_specs=[col(rows), pl.BlockSpec((1, 8, rows), lambda p, pos: (p, 0, 0))],
            scratch_shapes=[
                pltpu.VMEM((span, 128), jnp.bfloat16),
                pltpu.VMEM((span, 128), jnp.bfloat16),
                pltpu.VMEM((branch, 128), jnp.bfloat16),
                pltpu.VMEM((branch, 128), jnp.bfloat16),
                pltpu.VMEM((2, max(block, branch), 128), jnp.float32),
                pltpu.VMEM((2, max(block, branch), 128), jnp.float32),
            ],
        ),
        out_shape=[
            jax.ShapeDtypeStruct((rows, width), jnp.bfloat16),
            jax.ShapeDtypeStruct((pairs, 8, rows), jnp.float32),
        ],
        compiler_params=pltpu.CompilerParams(
            dimension_semantics=("arbitrary",), vmem_limit_bytes=32 * 2**20
        ),
        cost_estimate=busy(7 * pairs),
        name="attention_forward",
    )(pos, q, k, v, *after)


def backward_kernel(pos, q, k, v, o, do, lse, *rest, block, branch, width):
    dq, dk, dv = rest[-13:-10]
    kta, ktc, kam, vm, ktab, ktcb, kbm, vbm, dks, dvs = rest[-10:]
    pair = pl.program_id(0)
    scale = HEAD_DIM ** (-0.5)
    low, high, valid = halves(pair, width)
    zero = jnp.zeros((), jnp.bfloat16)
    span = k.shape[0] - branch
    prompt_part, branch_part = slice(0, span), slice(span, None)
    for part, whole_ref, turn_a, turn_b in ((prompt_part, kam, kta, ktc), (branch_part, kbm, ktab, ktcb)):
        whole = jnp.where(valid, k[part, :], zero)
        whole_ref[...] = whole
        turned = whole.T
        turn_a[...] = turned[0:64, :]
        turn_b[...] = turned[64:128, :]
    vm[...] = jnp.where(valid, v[prompt_part, :], zero)
    vbm[...] = jnp.where(valid, v[branch_part, :], zero)
    dq[...] = jnp.zeros_like(dq)
    dks[...] = jnp.zeros_like(dks)
    dvs[...] = jnp.zeros_like(dvs)
    rows = o.shape[0]
    blocks = [(start, block, False) for start in range(0, rows - branch, block)]
    blocks.append((rows - branch, branch, True))
    ones_a = jnp.broadcast_to(low, (8, 128)).astype(jnp.bfloat16)
    ones_b = jnp.broadcast_to(high, (8, 128)).astype(jnp.bfloat16)
    for number, (start, size, is_branch) in enumerate(blocks):
        at = pos[number]
        here = slice(start, start + size)
        query_at = query_rows(pos, number, size, span, is_branch)
        query = q[query_at, :]
        grad = do[here, :]
        queries = (jnp.where(low, query, zero), jnp.where(high, query, zero))
        grads = (jnp.where(low, grad, zero), jnp.where(high, grad, zero))
        product = jnp.where(valid, grad.astype(jnp.float32) * o[here, :].astype(jnp.float32), 0.0)
        upper = product.astype(jnp.bfloat16)
        lower = (product - upper.astype(jnp.float32)).astype(jnp.bfloat16)
        deltas = tuple((nt(m, upper) + nt(m, lower))[0:1, :] for m in (ones_a, ones_b))
        stats = (lse[0, 0:1, here], lse[0, 1:2, here])
        queries_cat = jnp.concatenate(queries, axis=0)
        grads_cat = jnp.concatenate(grads, axis=0)

        def step(key, value, first, second, mask):
            probs, dscores = [], []
            for query_h, grad_h, delta, stat in zip(queries, grads, deltas, stats):
                scores = nt(key, query_h)
                prob = jnp.exp2(scores * (scale * LOG2E) - stat)
                if mask is not None:
                    prob = jnp.where(mask, prob, 0.0)
                dprob = nt(value, grad_h)
                probs.append(prob.astype(jnp.bfloat16))
                dscores.append((prob * (dprob - delta)).astype(jnp.bfloat16))
            dscores_cat = jnp.concatenate(dscores, axis=1)
            dvalue = nn(jnp.concatenate(probs, axis=1), grads_cat)
            dkey = nn(dscores_cat, queries_cat)
            dquery = jnp.concatenate([nn(first, dscores[0]), nn(second, dscores[1])], axis=0)
            return dquery, dkey, dvalue

        def read(base):
            rows_at = pl.ds(pl.multiple_of(base, BK), BK)
            return kam[rows_at, :], vm[rows_at, :], kta[:, rows_at], ktc[:, rows_at]

        def accumulate(index, carry, mask):
            rows_at = pl.ds(pl.multiple_of(index * BK, BK), BK)
            dquery, dkey, dvalue = step(*read(index * BK), mask)
            dks[rows_at, :] += dkey
            dvs[rows_at, :] += dvalue
            return carry + dquery

        carry = jnp.zeros((128, size), jnp.float32)
        whole_blocks = at // BK
        carry = lax.fori_loop(0, whole_blocks, lambda i, c: accumulate(i, c, None), carry)
        row = lax.broadcasted_iota(jnp.int32, (BK, size), 0)
        column = lax.broadcasted_iota(jnp.int32, (BK, size), 1)
        if is_branch:
            carry = lax.fori_loop(
                whole_blocks,
                (at + BK - 1) // BK,
                lambda i, c: accumulate(i, c, row + i * BK < at),
                carry,
            )
            triangle = lax.broadcasted_iota(jnp.int32, (size, size), 0) <= lax.broadcasted_iota(
                jnp.int32, (size, size), 1
            )
            dquery, dkey, dvalue = step(kbm[...], vbm[...], ktab[...], ktcb[...], triangle)
            carry = carry + dquery
            dk[branch_part, :] = (dkey * scale).astype(dk.dtype)
            dv[branch_part, :] = dvalue.astype(dv.dtype)
        else:
            carry = accumulate(whole_blocks, carry, row + whole_blocks * BK <= column + at)
        dq[query_at, :] = (carry.T * scale).astype(dq.dtype)
    dk[prompt_part, :] = (dks[...] * scale).astype(dk.dtype)
    dv[prompt_part, :] = dvs[...].astype(dv.dtype)


def attention_backward(pos, q, k, v, o, do, lse, block, branch, after=()):
    total, width = q.shape
    span = total - branch
    rows = o.shape[0]
    pairs = pl.cdiv(width, 128)

    def col(n):
        return pl.BlockSpec((n, 128), lambda p, pos: (0, p))

    def scratch(n):
        wide = pltpu.VMEM((64, n), jnp.bfloat16)
        tall = pltpu.VMEM((n, 128), jnp.bfloat16)
        return [wide, wide, tall, tall]

    return pl.pallas_call(
        functools.partial(backward_kernel, block=block, branch=branch, width=width),
        grid_spec=pltpu.PrefetchScalarGridSpec(
            num_scalar_prefetch=1,
            grid=(pairs,),
            in_specs=[col(total)] * 3
            + [col(rows)] * 2
            + [pl.BlockSpec((1, 8, rows), lambda p, pos: (p, 0, 0))]
            + [pl.BlockSpec(memory_space=pl.ANY)] * len(after),
            out_specs=[col(total)] * 3,
            scratch_shapes=scratch(span)
            + scratch(branch)
            + [pltpu.VMEM((span, 128), jnp.float32), pltpu.VMEM((span, 128), jnp.float32)],
        ),
        out_shape=[jax.ShapeDtypeStruct((total, width), jnp.bfloat16)] * 3,
        compiler_params=pltpu.CompilerParams(
            dimension_semantics=("arbitrary",), vmem_limit_bytes=40 * 2**20
        ),
        cost_estimate=busy(10 * pairs),
        name="attention_backward",
    )(pos, q, k, v, o, do, lse, *after)


TILE = 256


def row_chunks(rows, size=256):
    return [slice(at, min(at + size, rows)) for at in range(0, rows, size)]


def fixed(shape):
    return pl.BlockSpec(shape, lambda *_: (0,) * len(shape), pipeline_mode=pl.Buffered(1))


def steady(shape):
    return pl.BlockSpec(shape, lambda *_: (0,) * len(shape))


def store_halves(value, half, keep, give):
    count, size = keep.shape[0], keep.shape[1]
    for block in range(count):
        first = value[2 * block * size : (2 * block + 1) * size, :]
        second = value[(2 * block + 1) * size : (2 * block + 2) * size, :]
        keep[block, :, :] = jnp.where(half == 0, first, second).astype(keep.dtype)
        give[block, :, :] = jnp.where(half == 0, second, first).astype(give.dtype)


def mlp_forward_kernel(
    mixed_a, mixed_b, tokens, out_w, out_bias, gain, shift, up, up_bias, down, down_bias, *rest
):
    hidden, slope, result, act_turned, norm, pace, act, acc = rest[-8:]
    step = pl.program_id(0)
    rows = tokens.shape[0]
    first = mixed_a.shape[1]

    @pl.when(step == 0)
    def _():
        for here in row_chunks(rows):
            resid = (
                tokens[here, :].astype(jnp.float32)
                + nn(mixed_a[here, :], out_w[:first, :])
                + nn(mixed_b[here, :], out_w[first:, :])
                + out_bias[...]
            )
            centred = resid - jnp.mean(resid, axis=1, keepdims=True)
            speed = lax.rsqrt(jnp.mean(centred * centred, axis=1, keepdims=True) + epsilon)
            normed = centred * speed
            acting = (normed * gain[...] + shift[...]).astype(jnp.bfloat16)
            act[here, :] = acting
            act_turned[:, here] = acting.T
            norm[here, :] = normed.astype(norm.dtype)
            pace[here, :] = jnp.broadcast_to(speed, (speed.shape[0], 128))
            acc[here, :] = resid + down_bias[...]

    for here in row_chunks(rows):
        pre = nn(act[here, :], up[...]) + up_bias[...]
        bell = jnp.exp2(pre * pre * (-0.5 * LOG2E))
        base = 1.0 + (0.3275911 * 0.7071067811865476) * jnp.abs(pre)
        t = pl.reciprocal(base, approx=True)
        t = t * (2.0 - base * t)
        series = t * (
            0.127414796 + t * (-0.142248368 + t * (0.7107068705 + t * (-0.7265760135 + t * 0.5307027145)))
        )
        tail = series * bell
        below = jnp.where(pre >= 0.0, 1.0 - tail, tail)
        exact = (pre * below).astype(jnp.bfloat16)
        hidden[here, :] = exact
        slope[here, :] = (below + pre * bell * 0.3989422804014327).astype(jnp.bfloat16)
        acc[here, :] += nt(exact, down[...])

    @pl.when(step == pl.num_programs(0) - 1)
    def _():
        result[...] = acc[...].astype(result.dtype)


def mlp_forward(
    mixed, tokens, out_w, out_bias, gain, shift, up, up_bias, down, down_bias, after=()
):
    rows, width = tokens.shape
    inner = up.shape[1]
    column = pl.BlockSpec((width, TILE), lambda j: (0, j))
    tall = pl.BlockSpec((rows, TILE), lambda j: (0, j))
    line = fixed((1, width))
    like = jax.ShapeDtypeStruct
    return pl.pallas_call(
        mlp_forward_kernel,
        grid=(inner // TILE,),
        in_specs=[
            fixed(mixed[0].shape),
            fixed(mixed[1].shape),
            fixed((rows, width)),
            fixed((width, width)),
            line,
            line,
            line,
            column,
            pl.BlockSpec((1, TILE), lambda j: (0, j)),
            column,
            line,
        ]
        + [pl.BlockSpec(memory_space=pl.ANY)] * len(after),
        out_specs=[
            tall,
            tall,
            steady((rows, width)),
            steady((width, rows)),
            steady((rows, width)),
            steady((rows, 128)),
        ],
        out_shape=[
            like((rows, inner), jnp.bfloat16),
            like((rows, inner), jnp.bfloat16),
            like((rows, width), jnp.bfloat16),
            like((width, rows), jnp.bfloat16),
            like((rows, width), jnp.bfloat16),
            like((rows, 128), jnp.float32),
        ],
        scratch_shapes=[pltpu.VMEM((rows, width), jnp.bfloat16), pltpu.VMEM((rows, width), jnp.float32)],
        compiler_params=pltpu.CompilerParams(
            dimension_semantics=("arbitrary",), vmem_limit_bytes=52 * 2**20
        ),
        cost_estimate=busy(50),
        name="mlp_forward",
    )(
        *mixed,
        tokens,
        out_w,
        *(v.reshape(1, width) for v in (out_bias, gain, shift)),
        up,
        up_bias.reshape(1, inner),
        down,
        down_bias.reshape(1, width),
        *after,
    )


def down_back_kernel(half, cot_turned, hidden, keep, give):
    store_halves(nn(cot_turned[...], hidden[...]), half[0], keep, give)


def down_back(half, count, cot_turned, hidden):
    width, rows = cot_turned.shape
    inner = hidden.shape[1]
    block = width // count // 2
    split = pl.BlockSpec((count, block, TILE), lambda j, half: (0, 0, j))
    return pl.pallas_call(
        down_back_kernel,
        grid_spec=pltpu.PrefetchScalarGridSpec(
            num_scalar_prefetch=1,
            grid=(inner // TILE,),
            in_specs=[fixed((width, rows)), pl.BlockSpec((rows, TILE), lambda j, half: (0, j))],
            out_specs=[split, split],
        ),
        out_shape=[jax.ShapeDtypeStruct((count, block, inner), jnp.bfloat16)] * 2,
        compiler_params=pltpu.CompilerParams(
            dimension_semantics=("arbitrary",), vmem_limit_bytes=32 * 2**20
        ),
        cost_estimate=busy(15),
        name="down_back",
    )(half, cot_turned, hidden)


def up_back_step(half, act_turned, cot, slope, up, down, total, keep, give, bias_grad):
    bias = jnp.zeros((1, TILE), jnp.float32)
    pieces = []
    for here in row_chunks(cot.shape[0]):
        d_pre = (nn(cot[here, :], down[...]) * slope[here, :].astype(jnp.float32)).astype(jnp.bfloat16)
        bias = bias + jnp.sum(d_pre.astype(jnp.float32), axis=0, keepdims=True)
        total[here, :] += nt(d_pre, up[...])
        pieces.append(d_pre)
    bias_grad[...] = bias
    store_halves(nn(act_turned[...], jnp.concatenate(pieces, axis=0)), half[0], keep, give)


def up_back_first_kernel(half, act_turned, cot, slope, up, down, total, keep, give, bias_grad):
    @pl.when(pl.program_id(0) == 0)
    def _():
        total[...] = jnp.zeros_like(total)

    up_back_step(half, act_turned, cot, slope, up, down, total, keep, give, bias_grad)


def up_back_last_kernel(
    half, act_turned, cot, slope, up, down, so_far, norm, pace, gain, mixed_a, mixed_b, out_w, *rest
):
    d_resid, d_mixed_a, d_mixed_b, keep, give, out_keep, out_give, bias_grad, lines = rest[-11:-2]
    d_branch, piece = rest[-2:]
    step = pl.program_id(0)
    rows, width = cot.shape
    first = mixed_a.shape[1]

    @pl.when(step == 0)
    def _():
        d_resid[...] = so_far[...]

    up_back_step(half, act_turned, cot, slope, up, down, d_resid, keep, give, bias_grad)

    @pl.when(step == pl.num_programs(0) - 1)
    def _():
        sums = [jnp.zeros((1, width), jnp.float32)] * 4
        for here in row_chunks(rows):
            grad = d_resid[here, :]
            normed = norm[here, :].astype(jnp.float32)
            scaled = grad * gain[...]
            inner = (
                scaled
                - jnp.mean(scaled, axis=1, keepdims=True)
                - normed * jnp.mean(scaled * normed, axis=1, keepdims=True)
            )
            exact = cot[here, :].astype(jnp.float32)
            total = exact + pace[here, 0:1] * inner
            d_resid[here, :] = total
            rounded = total.astype(jnp.bfloat16)
            d_branch[here, :] = rounded
            d_mixed_a[here, :] = nt(rounded, out_w[:first, :]).astype(d_mixed_a.dtype)
            d_mixed_b[here, :] = nt(rounded, out_w[first:, :]).astype(d_mixed_b.dtype)
            for n, term in enumerate((grad * normed, grad, rounded.astype(jnp.float32), exact)):
                sums[n] = sums[n] + jnp.sum(term, axis=0, keepdims=True)
        for n in range(4):
            lines[n : n + 1, :] = sums[n]
        for columns in row_chunks(width):
            size = columns.stop - columns.start
            piece[:first, :size] = tn(mixed_a[...], d_branch[:, columns])
            piece[first:, :size] = tn(mixed_b[...], d_branch[:, columns])
            value = piece[:, :size]
            store_halves(value, half[0], out_keep.at[:, :, columns], out_give.at[:, :, columns])


def up_back(half, count, tiles, act_turned, cot, slope, up, down, final=None, after=()):
    rows, width = cot.shape
    block = width // count // 2
    low, high = tiles
    inner = (high - low) * TILE
    split = pl.BlockSpec((count, block, TILE), lambda j, half: (0, 0, j))
    column = pl.BlockSpec((width, TILE), lambda j, half: (0, j + low))
    like = jax.ShapeDtypeStruct
    in_specs = [
        fixed((width, rows)),
        fixed((rows, width)),
        pl.BlockSpec((rows, TILE), lambda j, half: (0, j + low)),
        column,
        column,
    ]
    operands = [half, act_turned, cot, slope, up, down]
    out_specs = [steady((rows, width))]
    out_shape = [like((rows, width), jnp.float32)]
    scratch = []
    if final is not None:
        so_far, norm, pace, gain, mixed, out_w = final
        in_specs += [
            fixed((rows, width)),
            fixed((rows, width)),
            fixed((rows, 128)),
            fixed((1, width)),
            fixed(mixed[0].shape),
            fixed(mixed[1].shape),
            fixed((width, width)),
        ]
        operands += [so_far, norm, pace, gain.reshape(1, width), *mixed, out_w]
        out_specs += [steady(m.shape) for m in mixed]
        out_shape += [like(m.shape, jnp.bfloat16) for m in mixed]
        scratch = [pltpu.VMEM((rows, width), jnp.bfloat16), pltpu.VMEM((width, TILE), jnp.float32)]
    out_specs += [split] * 2
    out_shape += [like((count, block, inner), jnp.bfloat16)] * 2
    if final is not None:
        out_specs += [steady((count, block, width))] * 2
        out_shape += [like((count, block, width), jnp.bfloat16)] * 2
    out_specs += [pl.BlockSpec((1, TILE), lambda j, half: (0, j))]
    out_shape += [like((1, inner), jnp.float32)]
    if final is not None:
        out_specs += [steady((8, width))]
        out_shape += [like((8, width), jnp.float32)]
        in_specs += [pl.BlockSpec(memory_space=pl.ANY)] * len(after)
        operands += after
    return pl.pallas_call(
        up_back_first_kernel if final is None else up_back_last_kernel,
        grid_spec=pltpu.PrefetchScalarGridSpec(
            num_scalar_prefetch=1,
            grid=(high - low,),
            in_specs=in_specs,
            out_specs=out_specs,
            scratch_shapes=scratch,
        ),
        out_shape=out_shape,
        compiler_params=pltpu.CompilerParams(
            dimension_semantics=("arbitrary",), vmem_limit_bytes=58 * 2**20
        ),
        cost_estimate=busy(30 if final is None else 50),
        name="up_back_first" if final is None else "up_back_last",
    )(*operands)


def tokens_back_kernel(*refs):
    grads, weights, norm = refs[0:6], refs[6:12], refs[12]
    out, lines = refs[-2:]
    total = sum(nt(grad[...], weight[...]) for grad, weight in zip(grads, weights))
    out[...] = total.astype(out.dtype)

    @pl.when(pl.program_id(0) == 0)
    def _():
        lines[...] = jnp.zeros_like(lines)

    lines[0:1, :] += jnp.sum(total * norm[...].astype(jnp.float32), axis=0, keepdims=True)
    lines[1:2, :] += jnp.sum(total, axis=0, keepdims=True)


def tokens_back(grads, weights, norm, size, after=()):
    total, width = norm.shape
    flat_grads, flat_weights = [g for group in grads for g in group], [w for group in weights for w in group]
    tall = pl.BlockSpec((size, width), lambda t: (t, 0))
    return pl.pallas_call(
        tokens_back_kernel,
        grid=(total // size,),
        in_specs=[pl.BlockSpec((size, g.shape[1]), lambda t: (t, 0)) for g in flat_grads]
        + [fixed(w.shape) for w in flat_weights]
        + [tall]
        + [pl.BlockSpec(memory_space=pl.ANY)] * len(after),
        out_specs=[tall, steady((8, width))],
        out_shape=[
            jax.ShapeDtypeStruct((total, width), jnp.bfloat16),
            jax.ShapeDtypeStruct((8, width), jnp.float32),
        ],
        compiler_params=pltpu.CompilerParams(
            dimension_semantics=("arbitrary",), vmem_limit_bytes=40 * 2**20
        ),
        cost_estimate=busy(20),
        name="tokens_back",
    )(*flat_grads, *flat_weights, norm, *after)


def weights_back_kernel(half, turned, *refs, tiles):
    outs = refs[-6:]
    step = pl.program_id(0)
    for group in range(2):
        keep, give, bias = outs[group * 3 : group * 3 + 3]
        start, size = group * 3 * tiles[0], tiles[group]
        for kind in range(3):
            grad = refs[group * 3 + kind]

            @pl.when(jnp.logical_and(step >= start + kind * size, step < start + (kind + 1) * size))
            def _():
                part = grad[...]
                store_halves(nn(turned[...], part), half[0], keep, give)
                bias[...] = jnp.sum(part.astype(jnp.float32), axis=0, keepdims=True)


def weights_back(half, count, turned, grads, after=()):
    width, total = turned.shape
    tiles = [pl.cdiv(group[0].shape[1], TILE) for group in grads]
    block = width // count // 2
    like = jax.ShapeDtypeStruct
    in_specs, out_specs, out_shape = [], [], []
    for group in range(2):
        start, size = group * 3 * tiles[0], tiles[group]
        for kind in range(3):
            at = start + kind * size
            in_specs.append(
                pl.BlockSpec(
                    (total, TILE), lambda t, half, at=at, size=size: (0, jnp.clip(t - at, 0, size - 1))
                )
            )

        def place(t, start=start, size=size):
            return jnp.clip(t - start, 0, 3 * size - 1)

        out_specs += [
            pl.BlockSpec((count, block, TILE), lambda t, half, place=place: (0, 0, place(t)))
        ] * 2 + [pl.BlockSpec((1, TILE), lambda t, half, place=place: (0, place(t)))]
        columns = 3 * size * TILE
        out_shape += [like((count, block, columns), jnp.bfloat16)] * 2 + [like((1, columns), jnp.float32)]
    return pl.pallas_call(
        functools.partial(weights_back_kernel, tiles=tiles),
        grid_spec=pltpu.PrefetchScalarGridSpec(
            num_scalar_prefetch=1,
            grid=(3 * sum(tiles),),
            in_specs=[fixed((width, total))]
            + in_specs
            + [pl.BlockSpec(memory_space=pl.ANY)] * len(after),
            out_specs=out_specs,
        ),
        out_shape=out_shape,
        compiler_params=pltpu.CompilerParams(
            dimension_semantics=("arbitrary",), vmem_limit_bytes=52 * 2**20
        ),
        cost_estimate=busy(25),
        name="weights_back",
    )(half, turned, *grads[0], *grads[1], *after)


def rows_back_kernel(others, own, rows, resid, gain, prompt_out, branch_out):
    step = pl.program_id(0)
    last = pl.num_programs(0) - 1
    values = rows[...].astype(jnp.float32)
    centred = values - jnp.mean(values, axis=1, keepdims=True)
    pace = lax.rsqrt(jnp.mean(centred * centred, axis=1, keepdims=True) + epsilon)
    normed = centred * pace
    grad = own[...].astype(jnp.float32) + jnp.where(step == last, 0.0, others[...].astype(jnp.float32))
    scaled = grad * gain[...]
    inner = (
        scaled
        - jnp.mean(scaled, axis=1, keepdims=True)
        - normed * jnp.mean(scaled * normed, axis=1, keepdims=True)
    )
    turned = (resid[...] + pace * inner).T

    @pl.when(step < last)
    def _():
        prompt_out[...] = turned

    @pl.when(step == last)
    def _():
        branch_out[...] = turned


def rows_back(others, own, rows, resid, gain, branch):
    total, width = own.shape
    shard = total - branch
    steps = shard // branch
    tall = pl.BlockSpec((branch, width), lambda t: (t, 0))
    return pl.pallas_call(
        rows_back_kernel,
        grid=(steps + 1,),
        in_specs=[
            pl.BlockSpec((branch, width), lambda t: (jnp.minimum(t, steps - 1), 0)),
            tall,
            tall,
            tall,
            fixed((1, width)),
        ],
        out_specs=[
            pl.BlockSpec((width, branch), lambda t: (0, jnp.minimum(t, steps - 1))),
            pl.BlockSpec((width, branch), lambda t: (0, 0)),
        ],
        out_shape=[
            jax.ShapeDtypeStruct((width, shard), jnp.float32),
            jax.ShapeDtypeStruct((width, branch), jnp.float32),
        ],
        compiler_params=pltpu.CompilerParams(
            dimension_semantics=("arbitrary",), vmem_limit_bytes=40 * 2**20
        ),
        cost_estimate=busy(10),
        name="rows_back",
    )(others, own, rows, resid, gain.reshape(1, width))


def gate_kernel(*refs):
    pass


def gate(value, after):
    if not after:
        return value
    anywhere = pl.BlockSpec(memory_space=pl.ANY)
    return pl.pallas_call(
        gate_kernel,
        in_specs=[anywhere] * (1 + len(after)),
        out_specs=anywhere,
        out_shape=jax.ShapeDtypeStruct(value.shape, value.dtype),
        input_output_aliases={0: 0},
        cost_estimate=busy(1),
        name="gate",
    )(value, *after)


def normalise(values_in):
    centre = jnp.mean(values_in, axis=-1, keepdims=True)
    centred = values_in - centre
    spread = jnp.mean(centred * centred, axis=-1, keepdims=True)
    pace = lax.rsqrt(spread + epsilon)
    return centred * pace, pace


def swap(value, axis, bit):
    count = lax.axis_size(axis)
    return lax.ppermute(value, axis, [(i, i ^ bit) for i in range(count)])


def ahead(value, axis, step):
    count = lax.axis_size(axis)
    return lax.ppermute(value, axis, [(i, (i + step) % count) for i in range(count)])


def total_over(value, axes):
    for axis in axes:
        count = lax.axis_size(axis)
        if count & (count - 1):
            value = lax.psum(value, axis)
            continue
        bit = 1
        while bit < count:
            value = value + swap(value, axis, bit)
            bit *= 2
    return value


def by_halves(half_width):
    return lax.axis_size("dp") == 4 and lax.axis_size("gy") == 2 and half_width > GROUP


def half_index():
    return lax.axis_index("dp") % 2


def pair_rows(mine, theirs):
    first = half_index() == 0
    return jnp.stack([jnp.where(first, mine, theirs), jnp.where(first, theirs, mine)], axis=-3)


def gather_plain(part):
    part = lax.all_gather(part, "gy", axis=1, tiled=True)
    return lax.all_gather(part, "gx", axis=0, tiled=True)


def gather_quarters(part):
    rows, columns = part.shape
    copies, gx, gy = (lax.axis_size(axis) for axis in ("dp", "gx", "gy"))
    size = columns // copies
    mine = lax.dynamic_slice_in_dim(part, lax.axis_index("dp") * size, size, 1)
    raw = lax.all_gather(mine, ("dp", "gx", "gy"))
    got = raw.reshape(copies, gx, gy, rows, size)
    return raw, [
        [got[quarter, :, side].reshape(gx * rows, size) for quarter in range(copies)]
        for side in range(gy)
    ]


def gather_projections(qkv_part, out_part, width):
    rows = qkv_part.shape[0]
    half = width // 2
    first_side = lax.axis_index("gy") == 0
    key_at = width - half
    here = jnp.where(
        first_side,
        qkv_part[:, :GROUP],
        qkv_part[:, half : half + GROUP],
    )
    keys_here = jnp.where(first_side, qkv_part[:, width : width + GROUP], qkv_part[:, :GROUP])
    raw, one = gather_quarters(jnp.concatenate([here, keys_here], axis=1))
    rest = width - GROUP
    spare = half - GROUP
    queries_rest = jnp.where(first_side, qkv_part[:, GROUP:width], qkv_part[:, half + GROUP :])
    keys_rest = jnp.where(first_side, qkv_part[:, width + GROUP :], qkv_part[:, GROUP:half])

    def pad(value, size):
        return jnp.pad(value, ((0, 0), (0, size - value.shape[1])))

    outer = pl.cdiv(rest + spare, 128) * 128
    out_size = pl.cdiv(half, 128) * 128
    total = pl.cdiv(outer + out_size, 512) * 512
    packed = pad(jnp.concatenate([queries_rest, keys_rest], axis=1), outer)
    packed = pad(jnp.concatenate([packed, pad(out_part, out_size)], axis=1), total)
    two = [jnp.concatenate(side, axis=1) for side in gather_quarters(packed)[1]]
    first = [
        jnp.concatenate(one[0][:2], axis=1),
        jnp.concatenate(one[0][2:], axis=1),
        jnp.concatenate(one[1][:2], axis=1),
    ]
    second = [
        two[0][:, :rest],
        jnp.concatenate(
            [two[0][:, rest : rest + spare]] + one[1][2:] + [two[1][:, rest : rest + spare]], axis=1
        ),
        two[1][:, :rest],
    ]
    out_full = jnp.concatenate([side[:, outer : outer + half] for side in two], axis=1)
    return [first, second], out_full, raw


def gather_feed_forward(up_part, down_part, after):
    columns = up_part.shape[1]
    shared = columns // 2 // 512 * 512
    _, quarters = gather_quarters(jnp.concatenate([up_part[:, :shared], down_part[:, :shared]], axis=1))
    first_half = half_index() == 0
    mine = gate(jnp.where(first_half, up_part[:, shared:], down_part[:, shared:]), after)
    rows, size = mine.shape
    count = lax.axis_size("gx")
    here = lax.axis_index("gx")
    blocks = jnp.zeros((count, rows, size), mine.dtype)
    for step in range(count):
        got = mine if step == 0 else ahead(mine, "gx", step)
        blocks = lax.dynamic_update_index_in_dim(blocks, got, (here - step) % count, 0)
    return quarters, blocks.reshape(count * rows, size)


def finish_feed_forward(quarters, own, theirs):
    first_half = half_index() == 0
    first_side = lax.axis_index("gy") == 0
    sides = (jnp.where(first_side, own, theirs), jnp.where(first_side, theirs, own))
    others = [swap(side, "dp", 1) for side in sides]
    ups = [jnp.where(first_half, a, b) for a, b in zip(sides, others)]
    downs = [jnp.where(first_half, b, a) for a, b in zip(sides, others)]
    wholes = []
    for pieces, rest in ((slice(0, 2), ups), (slice(2, 4), downs)):
        wholes.append(
            jnp.concatenate([p for side in range(2) for p in quarters[side][pieces] + [rest[side]]], axis=1)
        )
    return wholes


def core_step(keep, give):
    return add(keep, swap(give, "dp", 1))


def both_halves(keep, give):
    count, size, columns = keep.shape
    return jnp.stack([keep, give], axis=1).reshape(2 * count * size, columns)


def add(a, b):
    return (a.astype(jnp.float32) + b.astype(jnp.float32)).astype(jnp.bfloat16)


def chips_parts(sides):
    columns = sides[0].shape[-1]
    size = pl.cdiv(columns // 128, 2) * 128
    own_first = lax.axis_index("dp") // 2 == 0
    first, second = (
        jnp.concatenate([side[..., at : at + size] for side in sides], axis=-1) for at in (0, columns - size)
    )
    return jnp.where(own_first, first, second), jnp.where(own_first, second, first)


def chips_step(parts, end=()):
    keep, give = parts
    return add(keep, gate(swap(give, "dp", 2), end))


def two(value):
    size = value.shape[-1] // 2
    return value[..., :size], value[..., size:]


def overlap_join(value, columns):
    size = value.shape[-1]
    other = swap(value, "dp", 2)
    own_first = lax.axis_index("dp") // 2 == 0
    first, second = jnp.where(own_first, value, other), jnp.where(own_first, other, value)
    return jnp.concatenate([first, second[..., 2 * size - columns :]], axis=-1)


def blocks_step(value, begin=()):
    value = gate(value, begin)
    count = lax.axis_size("gx")
    here = lax.axis_index("gx")
    total = lax.dynamic_index_in_dim(value, here, 0, False).astype(jnp.float32)
    for step in range(1, count):
        give = lax.dynamic_index_in_dim(value, (here + step) % count, 0, False)
        total = total + ahead(give, "gx", step).astype(jnp.float32)
    return total.astype(jnp.bfloat16)


def copies_step(value):
    bit = 2
    while bit < lax.axis_size("dp"):
        value = add(value, swap(value, "dp", bit))
        bit *= 2
    return value


def join_step(value):
    columns = value.shape[-1]
    return pair_rows(value, swap(value, "dp", 1)).reshape(-1, columns).astype(jnp.float32)


def side_exchange(first, second, begin=()):
    first_side = lax.axis_index("gy") == 0
    keep = jnp.where(first_side, first, second)
    return add(keep, swap(gate(jnp.where(first_side, second, first), begin), "gy", 1))


def projection_sides(first, rest):
    query, key, value = (first[..., n * GROUP : (n + 1) * GROUP] for n in range(3))
    size = rest.shape[-1] // 3
    query_rest, key_rest, value_rest = (rest[..., n * size : n * size + GROUP + 128] for n in range(3))
    return (
        jnp.concatenate([query, key, query_rest, key_rest[..., :128]], axis=-1),
        jnp.concatenate([value, key_rest, value_rest], axis=-1),
    )


def join_projections(whole, width):
    rest = width - GROUP
    spare = width // 2 - GROUP
    wide = GROUP + 128
    query, key = whole[:, :GROUP], whole[:, GROUP : 2 * GROUP]
    query_rest = whole[:, 2 * GROUP : 2 * GROUP + rest]
    key_spare = whole[:, 2 * GROUP + wide : 2 * GROUP + wide + spare]
    value = whole[:, :GROUP]
    key_rest = whole[:, GROUP + spare : GROUP + rest]
    value_rest = whole[:, GROUP + wide : GROUP + wide + rest]
    return jnp.where(
        lax.axis_index("gy") == 0,
        jnp.concatenate([query, query_rest, key, key_spare], axis=1),
        jnp.concatenate([key_rest, value, value_rest], axis=1),
    )


def scatter_plain(whole):
    part = lax.psum_scatter(whole, "gy", scatter_dimension=1, tiled=True)
    part = lax.psum_scatter(part, "gx", scatter_dimension=0, tiled=True)
    return lax.psum(part, "dp").astype(jnp.float32)


def all_tokens(own):
    count = lax.axis_size("gy")
    here = lax.axis_index("gy")
    if count != 2:
        return lax.all_gather(own, "gy", axis=0, tiled=True)
    other = swap(own, "gy", 1)
    first = here == 0
    return jnp.concatenate([jnp.where(first, own, other), jnp.where(first, other, own)], axis=0)


def others_tokens(whole):
    count = lax.axis_size("gy")
    here = lax.axis_index("gy")
    rows = whole.shape[0] // count
    if count != 2:
        keep = lax.dynamic_slice_in_dim(whole, here * rows, rows, 0)
        total = lax.psum_scatter(whole, "gy", scatter_dimension=0, tiled=True)
        return (total.astype(jnp.float32) - keep.astype(jnp.float32)).astype(jnp.bfloat16)
    return swap(lax.dynamic_slice_in_dim(whole, (1 - here) * rows, rows, 0), "gy", 1)


def dot(a, b):
    return jnp.dot(a, b, preferred_element_type=jnp.float32)


def local(
    prompt,
    continuations,
    prefix_len,
    attn_gain,
    attn_shift,
    qkv_weight,
    query_bias,
    value_bias,
    out_weight,
    out_bias,
    mlp_gain,
    mlp_shift,
    up_weight,
    up_bias,
    down_weight,
    down_bias,
    grad_prompt,
    grad_continuations,
):
    groups, shard, width = prompt.shape
    length = continuations.shape[1]
    first_pos = lax.axis_index("gy") * shard
    prompt_len = shard * lax.axis_size("gy")
    block = shard // 2
    halved = by_halves(width // 2)
    spans = [slice(0, GROUP), slice(GROUP, width)]

    if halved:
        limit, other_limit = prefix_len[0], swap(prefix_len, "gy", 1)[0]
        is_first = first_pos == 0
        is_long = jnp.logical_or(limit > other_limit, jnp.logical_and(limit == other_limit, is_first))
        kept_at = jnp.where(is_long, 0, block)
        places = [first_pos + kept_at, shard - first_pos + kept_at, limit]
    else:
        places = [first_pos, first_pos + block, prefix_len[0]]
    places = jnp.stack(places).astype(jnp.int32)

    def kept_rows(own):
        return lax.dynamic_slice_in_dim(own, kept_at, block, 0)

    def given_rows(own):
        return lax.dynamic_slice_in_dim(own, block - kept_at, block, 0)

    def back_home(done, end=()):
        if not halved:
            return done
        kept, home = done[:block], gate(swap(done[block:], "gy", 1), end)
        return jnp.concatenate([jnp.where(is_long, kept, home), jnp.where(is_long, home, kept)], axis=0)

    own_prompt = prompt.reshape(shard, width)
    branch = continuations.reshape(length, width)
    own_cot = grad_prompt.reshape(shard, width)
    branch_cot = grad_continuations.reshape(length, width)
    whole_prompt = all_tokens(own_prompt)
    if halved:
        weights, out_full, raw = gather_projections(qkv_weight, out_weight, width)
        quarters, fetched = gather_feed_forward(up_weight, down_weight.T, (raw,))
        other_cot = swap(gate(given_rows(own_cot), (raw,)), "gy", 1)
        cotangent = jnp.concatenate([kept_rows(own_cot), other_cot, branch_cot], axis=0)
    else:
        qkv = gather_plain(qkv_weight)
        weights = [[qkv[:, c.start + s : c.stop + s] for s in (0, width, 2 * width)] for c in spans]
        out_full, up_full, down_full = (gather_plain(w) for w in (out_weight, up_weight, down_weight.T))
        cotangent = jnp.concatenate([own_cot, branch_cot], axis=0)

    all_rows = jnp.concatenate([whole_prompt, branch], axis=0)
    norm_all, _ = normalise(all_rows.astype(jnp.float32))
    act_all = (norm_all * attn_gain + attn_shift).astype(jnp.bfloat16)
    projected, mixed, stats = [], [], []
    for number, (cols, (w_query, w_key, w_value)) in enumerate(zip(spans, weights)):
        projected.append(
            (
                (dot(act_all, w_query) + query_bias[cols]).astype(jnp.bfloat16),
                dot(act_all, w_key).astype(jnp.bfloat16),
                (dot(act_all, w_value) + value_bias[cols]).astype(jnp.bfloat16),
            )
        )
        got, stat = attention_forward(places, *projected[-1], block, length)
        if halved and number == 0:
            fetched = gate(fetched, (got, cotangent))
            theirs = swap(fetched, "gy", 1)
        if halved and number == 1:
            up_full, down_full = finish_feed_forward(quarters, fetched, gate(theirs, (got,)))
        mixed.append(got)
        stats.append(stat)

    tokens = jnp.concatenate(
        [lax.dynamic_slice_in_dim(whole_prompt, places[n], block, 0) for n in range(2)] + [branch], axis=0
    )
    hidden, slope, result, act_turned, norm_two, pace_two = mlp_forward(
        mixed, tokens, out_full, out_bias, mlp_gain, mlp_shift, up_full, up_bias, down_full, down_bias
    )
    count = lax.axis_size("gx")
    half = jnp.reshape(half_index() if halved else 0, (1,)).astype(jnp.int32)
    tiles = up_full.shape[1] // TILE
    part = tiles // 2
    prompt_out = back_home(result[:shard]).reshape(groups, shard, width)
    continuation_out = result[shard:].reshape(1, length, width)
    down_keep, down_give = down_back(half, count, cotangent.T, hidden)
    after = ()
    if halved:
        down_flow = core_step(down_keep, down_give)
        after = (down_flow, prompt_out)
    so_far, up_keep, up_give, up_bias_grad = up_back(
        half, count, (0, part), act_turned, cotangent, slope, up_full, down_full
    )
    d_resid, *d_mixed, keep_rest, give_rest, out_keep, out_give, bias_rest, lines = up_back(
        half,
        count,
        (part, tiles),
        act_turned,
        cotangent,
        slope,
        up_full,
        down_full,
        (so_far, norm_two, pace_two, mlp_gain, mixed, out_full),
        after,
    )
    up_bias_grad = jnp.concatenate([up_bias_grad, bias_rest], axis=1)
    mlp_gain_grad, mlp_shift_grad, out_bias_grad, down_bias_grad = (lines[n] for n in range(4))
    if halved:
        side = up_weight.shape[1]
        up_flow = core_step(up_keep, gate(up_give, (down_flow,)))
        keep, give = chips_parts((down_flow[..., :side], down_flow[..., side:]))
        down_flow = chips_step((keep, gate(give, (so_far,))))
        ready = (down_flow, up_flow)
        rest_flow, out_flow = core_step(keep_rest, gate(give_rest, ready)), core_step(out_keep, gate(out_give, ready))
        ready = (rest_flow, out_flow)
        up_flow = jnp.concatenate([up_flow, rest_flow], axis=-1)
        down_flow = gate(down_flow, ready)
        after = (down_flow, up_flow, out_flow)
    d_parts = [None, None]
    for number in (1, 0):
        d_parts[number] = attention_backward(
            places, *projected[number], mixed[number], d_mixed[number], stats[number], block, length, after
        )
        if halved and number == 1:
            up_flow = side_exchange(
                jnp.concatenate([up_flow[..., :side], out_flow[..., : width // 2]], axis=-1),
                jnp.concatenate([up_flow[..., side:], out_flow[..., width // 2 :]], axis=-1),
            )
            down_flow = blocks_step(down_flow)
            d_home = gate(d_resid.astype(jnp.bfloat16), (d_parts[1][0],))
            after = (up_flow, down_flow, d_home)
        if halved and number == 0:
            up_flow = blocks_step(up_flow)
            home = back_home(d_home[:shard], (d_parts[0][0],)).astype(jnp.float32)
            after = (up_flow,)
    keep_a, give_a, bias_a, keep_b, give_b, bias_b = weights_back(half, count, act_all.T, d_parts, after)
    if halved:
        sides = projection_sides(core_step(keep_a, give_a), core_step(keep_b, give_b))
        parts = chips_parts(sides)
        after = parts
    else:
        after = (keep_a,)
    d_act_all, act_lines = tokens_back(d_parts, weights, norm_all.astype(jnp.bfloat16), length, after)
    attn_gain_grad, attn_shift_grad = act_lines[0], act_lines[1]
    others = others_tokens(d_act_all[:prompt_len])
    if halved:
        qkv_flow = chips_step(parts, (d_act_all,))
        down_flow = side_exchange(*two(down_flow), (qkv_flow,))
        qkv_flow = blocks_step(qkv_flow)
        others = gate(others, (qkv_flow,))
        summed = qkv_flow
        up_flow = gate(up_flow, (summed,))
    size = bias_b.shape[1] // 3
    query_bias_grad, value_bias_grad = (
        jnp.concatenate(
            [bias_a[0, n * GROUP : (n + 1) * GROUP], bias_b[0, n * size : n * size + width - GROUP]]
        )
        for n in (0, 2)
    )
    if halved:
        qkv_flow = side_exchange(*two(qkv_flow))
        qkv_total = join_projections(join_step(overlap_join(qkv_flow, sides[0].shape[-1])), width)
        up_total = join_step(copies_step(up_flow))
        up_total, out_total = up_total[:, :side], up_total[:, side:]
        down_total = join_step(overlap_join(down_flow, side))
    else:
        whole_a, whole_b = both_halves(keep_a, give_a), both_halves(keep_b, give_b)
        qkv_grad = jnp.concatenate(
            [
                piece
                for n in range(3)
                for piece in (
                    whole_a[:, n * GROUP : (n + 1) * GROUP],
                    whole_b[:, n * size : n * size + width - GROUP],
                )
            ],
            axis=1,
        )
        up_total, down_total, out_total, qkv_total = (
            scatter_plain(g)
            for g in (
                jnp.concatenate([both_halves(up_keep, up_give), both_halves(keep_rest, give_rest)], axis=1),
                both_halves(down_keep, down_give),
                both_halves(out_keep, out_give),
                qkv_grad,
            )
        )
    prompt_resid = d_resid[:shard]
    if halved:
        kept = jnp.where(is_long, prompt_resid[:block], home[:block]), jnp.where(
            is_long, home[block:], prompt_resid[:block]
        )
        prompt_resid = jnp.concatenate(kept, axis=0)
    own_rows = jnp.concatenate([own_prompt, branch], axis=0)
    own_grad = jnp.concatenate(
        [lax.dynamic_slice_in_dim(d_act_all, first_pos, shard, 0), d_act_all[prompt_len:]], axis=0
    )
    resid_rows = jnp.concatenate([prompt_resid, d_resid[shard:]], axis=0)
    prompt_grad, branch_grad = rows_back(others, own_grad, own_rows, resid_rows, attn_gain, length)
    prompt_grad = prompt_grad.T.reshape(groups, shard, width)
    continuation_grad = branch_grad.T.reshape(1, length, width)
    vectors = (
        attn_gain_grad,
        attn_shift_grad,
        query_bias_grad,
        value_bias_grad,
        out_bias_grad,
        mlp_gain_grad,
        mlp_shift_grad,
        up_bias_grad.reshape(-1),
        down_bias_grad,
    )
    joined = gate(jnp.concatenate(vectors), (summed,) if halved else ())
    joined = total_over(joined, ("dp", "gy", "gx"))
    totals = []
    at = 0
    for vector in vectors:
        totals.append(joined[at : at + vector.shape[0]])
        at += vector.shape[0]
    return (
        prompt_out,
        continuation_out,
        prompt_grad,
        continuation_grad,
        totals[0],
        totals[1],
        qkv_total,
        totals[2],
        totals[3],
        out_total,
        totals[4],
        totals[5],
        totals[6],
        up_total,
        totals[7],
        down_total.T,
        totals[8],
    )


def solution(mesh):
    placed = (
        P(("dp", "gx"), "gy", None),
        P(("dp", "gx", "gy"), None, None),
        P(("dp", "gx", "gy")),
        P(),
        P(),
        P("gx", "gy"),
        P(),
        P(),
        P("gx", "gy"),
        P(),
        P(),
        P(),
        P("gx", "gy"),
        P(),
        P("gy", "gx"),
        P(),
        P(("dp", "gx"), "gy", None),
        P(("dp", "gx", "gy"), None, None),
    )
    return jax.shard_map(
        local,
        mesh=mesh,
        in_specs=placed,
        out_specs=(
            P(("dp", "gx"), "gy", None),
            P(("dp", "gx", "gy"), None, None),
            P(("dp", "gx"), "gy", None),
            P(("dp", "gx", "gy"), None, None),
            P(),
            P(),
            P("gx", "gy"),
            P(),
            P(),
            P("gx", "gy"),
            P(),
            P(),
            P(),
            P("gx", "gy"),
            P(),
            P("gy", "gx"),
            P(),
        ),
        check_vma=False,
    )
```

```python
import functools
import jax
import jax.numpy as jnp
from jax import lax
from jax.sharding import PartitionSpec as P
from jax.experimental import pallas as pl
from jax.experimental.pallas import tpu as pltpu

HEAD_DIM = 64
LOG2E = 1.4426950408889634
NEG = -1e30
BK = 512
GROUP = 512
epsilon = 1e-05


def nt(a, b):
    return lax.dot_general(a, b, (((1,), (1,)), ((), ())), preferred_element_type=jnp.float32)


def nn(a, b):
    return jnp.dot(a, b, preferred_element_type=jnp.float32)


def tn(a, b):
    return lax.dot_general(a, b, (((0,), (0,)), ((), ())), preferred_element_type=jnp.float32)


def halves(pair, total):
    lane = lax.broadcasted_iota(jnp.int32, (1, 128), 1)
    left = jnp.minimum(total - pair * 128, 128)
    return lane < 64, jnp.logical_and(lane >= 64, lane < left), lane < left


def norm_bounds(ref, valid, spread):
    part = jnp.where(valid, ref[...], jnp.zeros((), jnp.bfloat16))
    return jnp.max(nn(part * part, spread), axis=0, keepdims=True)


def query_rows(pos, number, size, span, is_branch):
    if is_branch:
        return pl.ds(span, size)
    return pl.ds(pl.multiple_of(pos[number], size), size)


def forward_kernel(pos, q, k, v, *rest, block, branch, width):
    o, lse, va, vc, vab, vcb, tops, accs = rest[-8:]
    pair = pl.program_id(0)
    scale = HEAD_DIM ** (-0.5) * LOG2E
    low, high, valid = halves(pair, width)
    zero = jnp.zeros((), jnp.bfloat16)
    one = jnp.ones((), jnp.bfloat16)
    span = k.shape[0] - branch
    for part, first, second in ((slice(0, span), va, vc), (slice(span, None), vab, vcb)):
        whole = v[part, :]
        first[...] = jnp.where(low, whole, one)
        second[...] = jnp.where(low, one, jnp.where(high, whole, zero))
    spread = (
        (lax.broadcasted_iota(jnp.int32, (128, 128), 0) < 64)
        == (lax.broadcasted_iota(jnp.int32, (128, 128), 1) < 64)
    ).astype(jnp.bfloat16)
    bound = jnp.max(norm_bounds(k, valid, spread) * norm_bounds(q, valid, spread)) * (scale * scale)
    plain = bound < 90.0 * 90.0
    rows = o.shape[0]
    blocks = [(start, block, False) for start in range(0, rows - branch, block)]
    blocks.append((rows - branch, branch, True))

    def finish(start, size, acc_a, acc_b, top):
        total = pltpu.roll(jnp.where(low, acc_b, acc_a), 64, 1)
        o[start : start + size, :] = (jnp.where(low, acc_a, acc_b) / total).astype(o.dtype)
        turned = (top + jnp.log2(total)).T
        lse[0, 0:1, start : start + size] = turned[0:1, :]
        lse[0, 1:2, start : start + size] = turned[64:65, :]

    def setup(number, start, size, is_branch):
        at = pos[number]
        query = q[query_rows(pos, number, size, span, is_branch), :]
        queries = (jnp.where(low, query, zero), jnp.where(high, query, zero))
        row = lax.broadcasted_iota(jnp.int32, (size, BK), 0)
        column = lax.broadcasted_iota(jnp.int32, (size, BK), 1)
        triangle = lax.broadcasted_iota(jnp.int32, (size, size), 1) <= lax.broadcasted_iota(
            jnp.int32, (size, size), 0
        )
        whole_blocks = at // BK

        def allowed(index):
            if is_branch:
                return column + index * BK < at
            return column + index * BK <= row + at

        end = (at + BK - 1) // BK if is_branch else whole_blocks + 1
        return queries, triangle, whole_blocks, allowed, end

    def read(index):
        rows_at = pl.ds(pl.multiple_of(index * BK, BK), BK)
        return jnp.where(valid, k[rows_at, :], zero), va[rows_at, :], vc[rows_at, :]

    def own():
        return jnp.where(valid, k[span:, :], zero), vab[...], vcb[...]

    @pl.when(plain)
    def _():
        for number, (start, size, is_branch) in enumerate(blocks):
            queries, triangle, whole_blocks, allowed, end = setup(number, start, size, is_branch)

            def step(key, first, second, carry, mask):
                out = []
                for query_h, value_h, acc in zip(queries, (first, second), carry):
                    probs = jnp.exp2(nt(query_h, key) * scale)
                    if mask is not None:
                        probs = jnp.where(mask, probs, 0.0)
                    out.append(acc + nn(probs.astype(jnp.bfloat16), value_h))
                return tuple(out)

            carry = (jnp.zeros((size, 128), jnp.float32),) * 2
            carry = lax.fori_loop(0, whole_blocks, lambda i, c: step(*read(i), c, None), carry)
            if is_branch:
                carry = lax.fori_loop(
                    whole_blocks, end, lambda i, c: step(*read(i), c, allowed(i)), carry
                )
                carry = step(*own(), carry, triangle)
            else:
                carry = step(*read(whole_blocks), carry, allowed(whole_blocks))
            finish(start, size, *carry, 0.0)

    @pl.when(jnp.logical_not(plain))
    def _():
        for number, (start, size, is_branch) in enumerate(blocks):
            queries, triangle, whole_blocks, allowed, end = setup(number, start, size, is_branch)

            def step(key, first, second, mask):
                for head, value_h in enumerate((first, second)):
                    top = tops[head, 0:size, :]
                    scores = jnp.where(mask, nt(queries[head], key), NEG)
                    new_top = jnp.maximum(top, jnp.max(scores, axis=1, keepdims=True))
                    probs = jnp.exp2((scores - new_top[:, 0:1]) * scale).astype(jnp.bfloat16)
                    fade = jnp.exp2((top - new_top) * scale)
                    accs[head, 0:size, :] = accs[head, 0:size, :] * fade + nn(probs, value_h)
                    tops[head, 0:size, :] = new_top

            accs[:, 0:size, :] = jnp.zeros((2, size, 128), jnp.float32)
            tops[:, 0:size, :] = jnp.full((2, size, 128), NEG, jnp.float32)

            @pl.loop(0, end)
            def _(index):
                step(*read(index), allowed(index))

            if is_branch:
                step(*own(), triangle)
            top = jnp.where(low, tops[0, 0:size, :], tops[1, 0:size, :]) * scale
            finish(start, size, accs[0, 0:size, :], accs[1, 0:size, :], top)


def busy(microseconds):
    return pl.CostEstimate(
        flops=int(microseconds * 1.0e9), bytes_accessed=int(microseconds * 1.0e6), transcendentals=0
    )


def attention_forward(pos, q, k, v, block, branch, after=()):
    total, width = q.shape
    span = total - branch
    rows = block * (pos.shape[0] - 1) + branch
    pairs = pl.cdiv(width, 128)

    def col(n):
        return pl.BlockSpec((n, 128), lambda p, pos: (0, p))

    return pl.pallas_call(
        functools.partial(forward_kernel, block=block, branch=branch, width=width),
        grid_spec=pltpu.PrefetchScalarGridSpec(
            num_scalar_prefetch=1,
            grid=(pairs,),
            in_specs=[col(total)] * 3 + [pl.BlockSpec(memory_space=pl.ANY)] * len(after),
            out_specs=[col(rows), pl.BlockSpec((1, 8, rows), lambda p, pos: (p, 0, 0))],
            scratch_shapes=[
                pltpu.VMEM((span, 128), jnp.bfloat16),
                pltpu.VMEM((span, 128), jnp.bfloat16),
                pltpu.VMEM((branch, 128), jnp.bfloat16),
                pltpu.VMEM((branch, 128), jnp.bfloat16),
                pltpu.VMEM((2, max(block, branch), 128), jnp.float32),
                pltpu.VMEM((2, max(block, branch), 128), jnp.float32),
            ],
        ),
        out_shape=[
            jax.ShapeDtypeStruct((rows, width), jnp.bfloat16),
            jax.ShapeDtypeStruct((pairs, 8, rows), jnp.float32),
        ],
        compiler_params=pltpu.CompilerParams(
            dimension_semantics=("arbitrary",), vmem_limit_bytes=32 * 2**20
        ),
        cost_estimate=busy(7 * pairs),
        name="attention_forward",
    )(pos, q, k, v, *after)


def backward_kernel(pos, q, k, v, o, do, lse, *rest, block, branch, width):
    dq, dk, dv = rest[-13:-10]
    kta, ktc, kam, vm, ktab, ktcb, kbm, vbm, dks, dvs = rest[-10:]
    pair = pl.program_id(0)
    scale = HEAD_DIM ** (-0.5)
    low, high, valid = halves(pair, width)
    zero = jnp.zeros((), jnp.bfloat16)
    span = k.shape[0] - branch
    prompt_part, branch_part = slice(0, span), slice(span, None)
    for part, whole_ref, turn_a, turn_b in ((prompt_part, kam, kta, ktc), (branch_part, kbm, ktab, ktcb)):
        whole = jnp.where(valid, k[part, :], zero)
        whole_ref[...] = whole
        turned = whole.T
        turn_a[...] = turned[0:64, :]
        turn_b[...] = turned[64:128, :]
    vm[...] = jnp.where(valid, v[prompt_part, :], zero)
    vbm[...] = jnp.where(valid, v[branch_part, :], zero)
    dq[...] = jnp.zeros_like(dq)
    dks[...] = jnp.zeros_like(dks)
    dvs[...] = jnp.zeros_like(dvs)
    rows = o.shape[0]
    blocks = [(start, block, False) for start in range(0, rows - branch, block)]
    blocks.append((rows - branch, branch, True))
    ones_a = jnp.broadcast_to(low, (8, 128)).astype(jnp.bfloat16)
    ones_b = jnp.broadcast_to(high, (8, 128)).astype(jnp.bfloat16)
    for number, (start, size, is_branch) in enumerate(blocks):
        at = pos[number]
        here = slice(start, start + size)
        query_at = query_rows(pos, number, size, span, is_branch)
        query = q[query_at, :]
        grad = do[here, :]
        queries = (jnp.where(low, query, zero), jnp.where(high, query, zero))
        grads = (jnp.where(low, grad, zero), jnp.where(high, grad, zero))
        product = jnp.where(valid, grad.astype(jnp.float32) * o[here, :].astype(jnp.float32), 0.0)
        upper = product.astype(jnp.bfloat16)
        lower = (product - upper.astype(jnp.float32)).astype(jnp.bfloat16)
        deltas = tuple((nt(m, upper) + nt(m, lower))[0:1, :] for m in (ones_a, ones_b))
        stats = (lse[0, 0:1, here], lse[0, 1:2, here])
        queries_cat = jnp.concatenate(queries, axis=0)
        grads_cat = jnp.concatenate(grads, axis=0)

        def step(key, value, first, second, mask):
            probs, dscores = [], []
            for query_h, grad_h, delta, stat in zip(queries, grads, deltas, stats):
                scores = nt(key, query_h)
                prob = jnp.exp2(scores * (scale * LOG2E) - stat)
                if mask is not None:
                    prob = jnp.where(mask, prob, 0.0)
                dprob = nt(value, grad_h)
                probs.append(prob.astype(jnp.bfloat16))
                dscores.append((prob * (dprob - delta)).astype(jnp.bfloat16))
            dscores_cat = jnp.concatenate(dscores, axis=1)
            dvalue = nn(jnp.concatenate(probs, axis=1), grads_cat)
            dkey = nn(dscores_cat, queries_cat)
            dquery = jnp.concatenate([nn(first, dscores[0]), nn(second, dscores[1])], axis=0)
            return dquery, dkey, dvalue

        def read(base):
            rows_at = pl.ds(pl.multiple_of(base, BK), BK)
            return kam[rows_at, :], vm[rows_at, :], kta[:, rows_at], ktc[:, rows_at]

        def accumulate(index, carry, mask):
            rows_at = pl.ds(pl.multiple_of(index * BK, BK), BK)
            dquery, dkey, dvalue = step(*read(index * BK), mask)
            dks[rows_at, :] += dkey
            dvs[rows_at, :] += dvalue
            return carry + dquery

        carry = jnp.zeros((128, size), jnp.float32)
        whole_blocks = at // BK
        carry = lax.fori_loop(0, whole_blocks, lambda i, c: accumulate(i, c, None), carry)
        row = lax.broadcasted_iota(jnp.int32, (BK, size), 0)
        column = lax.broadcasted_iota(jnp.int32, (BK, size), 1)
        if is_branch:
            carry = lax.fori_loop(
                whole_blocks,
                (at + BK - 1) // BK,
                lambda i, c: accumulate(i, c, row + i * BK < at),
                carry,
            )
            triangle = lax.broadcasted_iota(jnp.int32, (size, size), 0) <= lax.broadcasted_iota(
                jnp.int32, (size, size), 1
            )
            dquery, dkey, dvalue = step(kbm[...], vbm[...], ktab[...], ktcb[...], triangle)
            carry = carry + dquery
            dk[branch_part, :] = (dkey * scale).astype(dk.dtype)
            dv[branch_part, :] = dvalue.astype(dv.dtype)
        else:
            carry = accumulate(whole_blocks, carry, row + whole_blocks * BK <= column + at)
        dq[query_at, :] = (carry.T * scale).astype(dq.dtype)
    dk[prompt_part, :] = (dks[...] * scale).astype(dk.dtype)
    dv[prompt_part, :] = dvs[...].astype(dv.dtype)


def attention_backward(pos, q, k, v, o, do, lse, block, branch, after=()):
    total, width = q.shape
    span = total - branch
    rows = o.shape[0]
    pairs = pl.cdiv(width, 128)

    def col(n):
        return pl.BlockSpec((n, 128), lambda p, pos: (0, p))

    def scratch(n):
        wide = pltpu.VMEM((64, n), jnp.bfloat16)
        tall = pltpu.VMEM((n, 128), jnp.bfloat16)
        return [wide, wide, tall, tall]

    return pl.pallas_call(
        functools.partial(backward_kernel, block=block, branch=branch, width=width),
        grid_spec=pltpu.PrefetchScalarGridSpec(
            num_scalar_prefetch=1,
            grid=(pairs,),
            in_specs=[col(total)] * 3
            + [col(rows)] * 2
            + [pl.BlockSpec((1, 8, rows), lambda p, pos: (p, 0, 0))]
            + [pl.BlockSpec(memory_space=pl.ANY)] * len(after),
            out_specs=[col(total)] * 3,
            scratch_shapes=scratch(span)
            + scratch(branch)
            + [pltpu.VMEM((span, 128), jnp.float32), pltpu.VMEM((span, 128), jnp.float32)],
        ),
        out_shape=[jax.ShapeDtypeStruct((total, width), jnp.bfloat16)] * 3,
        compiler_params=pltpu.CompilerParams(
            dimension_semantics=("arbitrary",), vmem_limit_bytes=40 * 2**20
        ),
        cost_estimate=busy(10 * pairs),
        name="attention_backward",
    )(pos, q, k, v, o, do, lse, *after)


TILE = 256


def row_chunks(rows, size=256):
    return [slice(at, min(at + size, rows)) for at in range(0, rows, size)]


def fixed(shape):
    return pl.BlockSpec(shape, lambda *_: (0,) * len(shape), pipeline_mode=pl.Buffered(1))


def steady(shape):
    return pl.BlockSpec(shape, lambda *_: (0,) * len(shape))


def store_halves(value, half, keep, give):
    count, size = keep.shape[0], keep.shape[1]
    for block in range(count):
        first = value[2 * block * size : (2 * block + 1) * size, :]
        second = value[(2 * block + 1) * size : (2 * block + 2) * size, :]
        keep[block, :, :] = jnp.where(half == 0, first, second).astype(keep.dtype)
        give[block, :, :] = jnp.where(half == 0, second, first).astype(give.dtype)


def mlp_forward_kernel(
    mixed_a, mixed_b, tokens, out_w, out_bias, gain, shift, up, up_bias, down, down_bias, *rest
):
    hidden, slope, result, act_turned, norm, pace, act, acc = rest[-8:]
    step = pl.program_id(0)
    rows = tokens.shape[0]
    first = mixed_a.shape[1]

    @pl.when(step == 0)
    def _():
        for here in row_chunks(rows):
            resid = (
                tokens[here, :].astype(jnp.float32)
                + nn(mixed_a[here, :], out_w[:first, :])
                + nn(mixed_b[here, :], out_w[first:, :])
                + out_bias[...]
            )
            centred = resid - jnp.mean(resid, axis=1, keepdims=True)
            speed = lax.rsqrt(jnp.mean(centred * centred, axis=1, keepdims=True) + epsilon)
            normed = centred * speed
            acting = (normed * gain[...] + shift[...]).astype(jnp.bfloat16)
            act[here, :] = acting
            act_turned[:, here] = acting.T
            norm[here, :] = normed.astype(norm.dtype)
            pace[here, :] = jnp.broadcast_to(speed, (speed.shape[0], 128))
            acc[here, :] = resid + down_bias[...]

    for here in row_chunks(rows):
        pre = nn(act[here, :], up[...]) + up_bias[...]
        bell = jnp.exp2(pre * pre * (-0.5 * LOG2E))
        base = 1.0 + (0.3275911 * 0.7071067811865476) * jnp.abs(pre)
        t = pl.reciprocal(base, approx=True)
        t = t * (2.0 - base * t)
        series = t * (
            0.127414796 + t * (-0.142248368 + t * (0.7107068705 + t * (-0.7265760135 + t * 0.5307027145)))
        )
        tail = series * bell
        below = jnp.where(pre >= 0.0, 1.0 - tail, tail)
        exact = (pre * below).astype(jnp.bfloat16)
        hidden[here, :] = exact
        slope[here, :] = (below + pre * bell * 0.3989422804014327).astype(jnp.bfloat16)
        acc[here, :] += nt(exact, down[...])

    @pl.when(step == pl.num_programs(0) - 1)
    def _():
        result[...] = acc[...].astype(result.dtype)


def mlp_forward(
    mixed, tokens, out_w, out_bias, gain, shift, up, up_bias, down, down_bias, after=()
):
    rows, width = tokens.shape
    inner = up.shape[1]
    column = pl.BlockSpec((width, TILE), lambda j: (0, j))
    tall = pl.BlockSpec((rows, TILE), lambda j: (0, j))
    line = fixed((1, width))
    like = jax.ShapeDtypeStruct
    return pl.pallas_call(
        mlp_forward_kernel,
        grid=(inner // TILE,),
        in_specs=[
            fixed(mixed[0].shape),
            fixed(mixed[1].shape),
            fixed((rows, width)),
            fixed((width, width)),
            line,
            line,
            line,
            column,
            pl.BlockSpec((1, TILE), lambda j: (0, j)),
            column,
            line,
        ]
        + [pl.BlockSpec(memory_space=pl.ANY)] * len(after),
        out_specs=[
            tall,
            tall,
            steady((rows, width)),
            steady((width, rows)),
            steady((rows, width)),
            steady((rows, 128)),
        ],
        out_shape=[
            like((rows, inner), jnp.bfloat16),
            like((rows, inner), jnp.bfloat16),
            like((rows, width), jnp.bfloat16),
            like((width, rows), jnp.bfloat16),
            like((rows, width), jnp.bfloat16),
            like((rows, 128), jnp.float32),
        ],
        scratch_shapes=[pltpu.VMEM((rows, width), jnp.bfloat16), pltpu.VMEM((rows, width), jnp.float32)],
        compiler_params=pltpu.CompilerParams(
            dimension_semantics=("arbitrary",), vmem_limit_bytes=52 * 2**20
        ),
        cost_estimate=busy(50),
        name="mlp_forward",
    )(
        *mixed,
        tokens,
        out_w,
        *(v.reshape(1, width) for v in (out_bias, gain, shift)),
        up,
        up_bias.reshape(1, inner),
        down,
        down_bias.reshape(1, width),
        *after,
    )


def down_back_kernel(half, cot_turned, hidden, keep, give):
    store_halves(nn(cot_turned[...], hidden[...]), half[0], keep, give)


def down_back(half, count, cot_turned, hidden):
    width, rows = cot_turned.shape
    inner = hidden.shape[1]
    block = width // count // 2
    split = pl.BlockSpec((count, block, TILE), lambda j, half: (0, 0, j))
    return pl.pallas_call(
        down_back_kernel,
        grid_spec=pltpu.PrefetchScalarGridSpec(
            num_scalar_prefetch=1,
            grid=(inner // TILE,),
            in_specs=[fixed((width, rows)), pl.BlockSpec((rows, TILE), lambda j, half: (0, j))],
            out_specs=[split, split],
        ),
        out_shape=[jax.ShapeDtypeStruct((count, block, inner), jnp.bfloat16)] * 2,
        compiler_params=pltpu.CompilerParams(
            dimension_semantics=("arbitrary",), vmem_limit_bytes=32 * 2**20
        ),
        cost_estimate=busy(15),
        name="down_back",
    )(half, cot_turned, hidden)


def up_back_step(half, act_turned, cot, slope, up, down, total, keep, give, bias_grad):
    bias = jnp.zeros((1, TILE), jnp.float32)
    pieces = []
    for here in row_chunks(cot.shape[0]):
        d_pre = (nn(cot[here, :], down[...]) * slope[here, :].astype(jnp.float32)).astype(jnp.bfloat16)
        bias = bias + jnp.sum(d_pre.astype(jnp.float32), axis=0, keepdims=True)
        total[here, :] += nt(d_pre, up[...])
        pieces.append(d_pre)
    bias_grad[...] = bias
    store_halves(nn(act_turned[...], jnp.concatenate(pieces, axis=0)), half[0], keep, give)


def up_back_first_kernel(half, act_turned, cot, slope, up, down, total, keep, give, bias_grad):
    @pl.when(pl.program_id(0) == 0)
    def _():
        total[...] = jnp.zeros_like(total)

    up_back_step(half, act_turned, cot, slope, up, down, total, keep, give, bias_grad)


def up_back_last_kernel(
    half, act_turned, cot, slope, up, down, so_far, norm, pace, gain, mixed_a, mixed_b, out_w, *rest
):
    d_resid, d_branch, d_mixed_a, d_mixed_b, keep, give, out_keep, out_give, bias_grad, lines, piece = rest[-11:]
    step = pl.program_id(0)
    rows, width = cot.shape
    first = mixed_a.shape[1]

    @pl.when(step == 0)
    def _():
        d_resid[...] = so_far[...]

    up_back_step(half, act_turned, cot, slope, up, down, d_resid, keep, give, bias_grad)

    @pl.when(step == pl.num_programs(0) - 1)
    def _():
        sums = [jnp.zeros((1, width), jnp.float32)] * 4
        for here in row_chunks(rows):
            grad = d_resid[here, :]
            normed = norm[here, :].astype(jnp.float32)
            scaled = grad * gain[...]
            inner = (
                scaled
                - jnp.mean(scaled, axis=1, keepdims=True)
                - normed * jnp.mean(scaled * normed, axis=1, keepdims=True)
            )
            exact = cot[here, :].astype(jnp.float32)
            total = exact + pace[here, 0:1] * inner
            d_resid[here, :] = total
            rounded = total.astype(jnp.bfloat16)
            d_branch[here, :] = rounded
            d_mixed_a[here, :] = nt(rounded, out_w[:first, :]).astype(d_mixed_a.dtype)
            d_mixed_b[here, :] = nt(rounded, out_w[first:, :]).astype(d_mixed_b.dtype)
            for n, term in enumerate((grad * normed, grad, rounded.astype(jnp.float32), exact)):
                sums[n] = sums[n] + jnp.sum(term, axis=0, keepdims=True)
        for n in range(4):
            lines[n : n + 1, :] = sums[n]
        for columns in row_chunks(width):
            size = columns.stop - columns.start
            piece[:first, :size] = tn(mixed_a[...], d_branch[:, columns])
            piece[first:, :size] = tn(mixed_b[...], d_branch[:, columns])
            value = piece[:, :size]
            store_halves(value, half[0], out_keep.at[:, :, columns], out_give.at[:, :, columns])


def up_back(half, count, tiles, act_turned, cot, slope, up, down, final=None, after=()):
    rows, width = cot.shape
    block = width // count // 2
    low, high = tiles
    inner = (high - low) * TILE
    split = pl.BlockSpec((count, block, TILE), lambda j, half: (0, 0, j))
    column = pl.BlockSpec((width, TILE), lambda j, half: (0, j + low))
    like = jax.ShapeDtypeStruct
    in_specs = [
        fixed((width, rows)),
        fixed((rows, width)),
        pl.BlockSpec((rows, TILE), lambda j, half: (0, j + low)),
        column,
        column,
    ]
    operands = [half, act_turned, cot, slope, up, down]
    out_specs = [steady((rows, width))]
    out_shape = [like((rows, width), jnp.float32)]
    scratch = []
    if final is not None:
        so_far, norm, pace, gain, mixed, out_w = final
        in_specs += [
            fixed((rows, width)),
            fixed((rows, width)),
            fixed((rows, 128)),
            fixed((1, width)),
            fixed(mixed[0].shape),
            fixed(mixed[1].shape),
            fixed((width, width)),
        ]
        operands += [so_far, norm, pace, gain.reshape(1, width), *mixed, out_w]
        out_specs += [steady((rows, width))] + [steady(m.shape) for m in mixed]
        out_shape += [like((rows, width), jnp.bfloat16)] + [like(m.shape, jnp.bfloat16) for m in mixed]
        scratch = [pltpu.VMEM((width, TILE), jnp.float32)]
    out_specs += [split] * 2
    out_shape += [like((count, block, inner), jnp.bfloat16)] * 2
    if final is not None:
        out_specs += [steady((count, block, width))] * 2
        out_shape += [like((count, block, width), jnp.bfloat16)] * 2
    out_specs += [pl.BlockSpec((1, TILE), lambda j, half: (0, j))]
    out_shape += [like((1, inner), jnp.float32)]
    if final is not None:
        out_specs += [steady((8, width))]
        out_shape += [like((8, width), jnp.float32)]
        in_specs += [pl.BlockSpec(memory_space=pl.ANY)] * len(after)
        operands += after
    return pl.pallas_call(
        up_back_first_kernel if final is None else up_back_last_kernel,
        grid_spec=pltpu.PrefetchScalarGridSpec(
            num_scalar_prefetch=1,
            grid=(high - low,),
            in_specs=in_specs,
            out_specs=out_specs,
            scratch_shapes=scratch,
        ),
        out_shape=out_shape,
        compiler_params=pltpu.CompilerParams(
            dimension_semantics=("arbitrary",), vmem_limit_bytes=58 * 2**20
        ),
        cost_estimate=busy(30 if final is None else 50),
        name="up_back_first" if final is None else "up_back_last",
    )(*operands)


def tokens_back_kernel(*refs):
    grads, weights, rows = refs[0:6], refs[6:12], refs[12]
    out, lines = refs[-2:]
    values = rows[...].astype(jnp.float32)
    centred = values - jnp.mean(values, axis=1, keepdims=True)
    normed = centred * lax.rsqrt(jnp.mean(centred * centred, axis=1, keepdims=True) + epsilon)
    total = sum(nt(grad[...], weight[...]) for grad, weight in zip(grads, weights))
    out[...] = total.astype(out.dtype)

    @pl.when(pl.program_id(0) == 0)
    def _():
        lines[...] = jnp.zeros_like(lines)

    lines[0:1, :] += jnp.sum(total * normed, axis=0, keepdims=True)
    lines[1:2, :] += jnp.sum(total, axis=0, keepdims=True)


def tokens_back(grads, weights, rows, size, after=()):
    total, width = rows.shape
    flat_grads, flat_weights = [g for group in grads for g in group], [w for group in weights for w in group]
    tall = pl.BlockSpec((size, width), lambda t: (t, 0))
    return pl.pallas_call(
        tokens_back_kernel,
        grid=(total // size,),
        in_specs=[pl.BlockSpec((size, g.shape[1]), lambda t: (t, 0)) for g in flat_grads]
        + [fixed(w.shape) for w in flat_weights]
        + [tall]
        + [pl.BlockSpec(memory_space=pl.ANY)] * len(after),
        out_specs=[tall, steady((8, width))],
        out_shape=[
            jax.ShapeDtypeStruct((total, width), jnp.bfloat16),
            jax.ShapeDtypeStruct((8, width), jnp.float32),
        ],
        compiler_params=pltpu.CompilerParams(
            dimension_semantics=("arbitrary",), vmem_limit_bytes=40 * 2**20
        ),
        cost_estimate=busy(20),
        name="tokens_back",
    )(*flat_grads, *flat_weights, rows, *after)


def weights_back_kernel(half, turned, *refs, tiles):
    outs = refs[-6:]
    step = pl.program_id(0)
    for group in range(2):
        keep, give, bias = outs[group * 3 : group * 3 + 3]
        start, size = group * 3 * tiles[0], tiles[group]
        for kind in range(3):
            grad = refs[group * 3 + kind]

            @pl.when(jnp.logical_and(step >= start + kind * size, step < start + (kind + 1) * size))
            def _():
                part = grad[...]
                store_halves(nn(turned[...], part), half[0], keep, give)
                bias[...] = jnp.sum(part.astype(jnp.float32), axis=0, keepdims=True)


def weights_back(half, count, turned, grads, after=()):
    width, total = turned.shape
    tiles = [pl.cdiv(group[0].shape[1], TILE) for group in grads]
    block = width // count // 2
    like = jax.ShapeDtypeStruct
    in_specs, out_specs, out_shape = [], [], []
    for group in range(2):
        start, size = group * 3 * tiles[0], tiles[group]
        for kind in range(3):
            at = start + kind * size
            in_specs.append(
                pl.BlockSpec(
                    (total, TILE), lambda t, half, at=at, size=size: (0, jnp.clip(t - at, 0, size - 1))
                )
            )

        def place(t, start=start, size=size):
            return jnp.clip(t - start, 0, 3 * size - 1)

        out_specs += [
            pl.BlockSpec((count, block, TILE), lambda t, half, place=place: (0, 0, place(t)))
        ] * 2 + [pl.BlockSpec((1, TILE), lambda t, half, place=place: (0, place(t)))]
        columns = 3 * size * TILE
        out_shape += [like((count, block, columns), jnp.bfloat16)] * 2 + [like((1, columns), jnp.float32)]
    return pl.pallas_call(
        functools.partial(weights_back_kernel, tiles=tiles),
        grid_spec=pltpu.PrefetchScalarGridSpec(
            num_scalar_prefetch=1,
            grid=(3 * sum(tiles),),
            in_specs=[fixed((width, total))]
            + in_specs
            + [pl.BlockSpec(memory_space=pl.ANY)] * len(after),
            out_specs=out_specs,
        ),
        out_shape=out_shape,
        compiler_params=pltpu.CompilerParams(
            dimension_semantics=("arbitrary",), vmem_limit_bytes=52 * 2**20
        ),
        cost_estimate=busy(25),
        name="weights_back",
    )(half, turned, *grads[0], *grads[1], *after)


def rows_back_kernel(others, own, rows, resid, gain, prompt_out, branch_out):
    step = pl.program_id(0)
    last = pl.num_programs(0) - 1
    values = rows[...].astype(jnp.float32)
    centred = values - jnp.mean(values, axis=1, keepdims=True)
    pace = lax.rsqrt(jnp.mean(centred * centred, axis=1, keepdims=True) + epsilon)
    normed = centred * pace
    grad = own[...].astype(jnp.float32) + jnp.where(step == last, 0.0, others[...].astype(jnp.float32))
    scaled = grad * gain[...]
    inner = (
        scaled
        - jnp.mean(scaled, axis=1, keepdims=True)
        - normed * jnp.mean(scaled * normed, axis=1, keepdims=True)
    )
    turned = (resid[...] + pace * inner).T

    @pl.when(step < last)
    def _():
        prompt_out[...] = turned

    @pl.when(step == last)
    def _():
        branch_out[...] = turned


def rows_back(others, own, rows, resid, gain, branch):
    total, width = own.shape
    shard = total - branch
    steps = shard // branch
    tall = pl.BlockSpec((branch, width), lambda t: (t, 0))
    return pl.pallas_call(
        rows_back_kernel,
        grid=(steps + 1,),
        in_specs=[
            pl.BlockSpec((branch, width), lambda t: (jnp.minimum(t, steps - 1), 0)),
            tall,
            tall,
            tall,
            fixed((1, width)),
        ],
        out_specs=[
            pl.BlockSpec((width, branch), lambda t: (0, jnp.minimum(t, steps - 1))),
            pl.BlockSpec((width, branch), lambda t: (0, 0)),
        ],
        out_shape=[
            jax.ShapeDtypeStruct((width, shard), jnp.float32),
            jax.ShapeDtypeStruct((width, branch), jnp.float32),
        ],
        compiler_params=pltpu.CompilerParams(
            dimension_semantics=("arbitrary",), vmem_limit_bytes=40 * 2**20
        ),
        cost_estimate=busy(10),
        name="rows_back",
    )(others, own, rows, resid, gain.reshape(1, width))


def gate_kernel(*refs):
    pass


def gate(value, after):
    if not after:
        return value
    anywhere = pl.BlockSpec(memory_space=pl.ANY)
    return pl.pallas_call(
        gate_kernel,
        in_specs=[anywhere] * (1 + len(after)),
        out_specs=anywhere,
        out_shape=jax.ShapeDtypeStruct(value.shape, value.dtype),
        input_output_aliases={0: 0},
        cost_estimate=busy(1),
        name="gate",
    )(value, *after)


def normalise(values_in):
    centre = jnp.mean(values_in, axis=-1, keepdims=True)
    centred = values_in - centre
    spread = jnp.mean(centred * centred, axis=-1, keepdims=True)
    pace = lax.rsqrt(spread + epsilon)
    return centred * pace, pace


def swap(value, axis, bit):
    count = lax.axis_size(axis)
    return lax.ppermute(value, axis, [(i, i ^ bit) for i in range(count)])


def ahead(value, axis, step):
    count = lax.axis_size(axis)
    return lax.ppermute(value, axis, [(i, (i + step) % count) for i in range(count)])


def by_halves(half_width):
    return lax.axis_size("dp") == 4 and lax.axis_size("gy") == 2 and half_width > GROUP


def half_index():
    return lax.axis_index("dp") % 2


def pair_rows(mine, theirs):
    first = half_index() == 0
    return jnp.stack([jnp.where(first, mine, theirs), jnp.where(first, theirs, mine)], axis=-3)


def gather_plain(part):
    part = lax.all_gather(part, "gy", axis=1, tiled=True)
    return lax.all_gather(part, "gx", axis=0, tiled=True)


def gather_quarters(part):
    rows, columns = part.shape
    copies, gx, gy = (lax.axis_size(axis) for axis in ("dp", "gx", "gy"))
    size = columns // copies
    mine = lax.dynamic_slice_in_dim(part, lax.axis_index("dp") * size, size, 1)
    raw = lax.all_gather(mine, ("dp", "gx", "gy"))
    got = raw.reshape(copies, gx, gy, rows, size)
    return raw, [
        [got[quarter, :, side].reshape(gx * rows, size) for quarter in range(copies)]
        for side in range(gy)
    ]


def gather_projections(qkv_part, out_part, width):
    rows = qkv_part.shape[0]
    half = width // 2
    first_side = lax.axis_index("gy") == 0
    key_at = width - half
    here = jnp.where(
        first_side,
        qkv_part[:, :GROUP],
        qkv_part[:, half : half + GROUP],
    )
    keys_here = jnp.where(first_side, qkv_part[:, width : width + GROUP], qkv_part[:, :GROUP])
    raw, one = gather_quarters(jnp.concatenate([here, keys_here], axis=1))
    rest = width - GROUP
    spare = half - GROUP
    queries_rest = jnp.where(first_side, qkv_part[:, GROUP:width], qkv_part[:, half + GROUP :])
    keys_rest = jnp.where(first_side, qkv_part[:, width + GROUP :], qkv_part[:, GROUP:half])

    def pad(value, size):
        return jnp.pad(value, ((0, 0), (0, size - value.shape[1])))

    outer = pl.cdiv(rest + spare, 128) * 128
    out_size = pl.cdiv(half, 128) * 128
    total = pl.cdiv(outer + out_size, 512) * 512
    packed = pad(jnp.concatenate([queries_rest, keys_rest], axis=1), outer)
    packed = pad(jnp.concatenate([packed, pad(out_part, out_size)], axis=1), total)
    two = [jnp.concatenate(side, axis=1) for side in gather_quarters(packed)[1]]
    first = [
        jnp.concatenate(one[0][:2], axis=1),
        jnp.concatenate(one[0][2:], axis=1),
        jnp.concatenate(one[1][:2], axis=1),
    ]
    second = [
        two[0][:, :rest],
        jnp.concatenate(
            [two[0][:, rest : rest + spare]] + one[1][2:] + [two[1][:, rest : rest + spare]], axis=1
        ),
        two[1][:, :rest],
    ]
    out_full = jnp.concatenate([side[:, outer : outer + half] for side in two], axis=1)
    return [first, second], out_full, raw


def gather_feed_forward(up_part, down_part, after):
    columns = up_part.shape[1]
    shared = columns // 2 // 512 * 512
    _, quarters = gather_quarters(jnp.concatenate([up_part[:, :shared], down_part[:, :shared]], axis=1))
    first_half = half_index() == 0
    mine = gate(jnp.where(first_half, up_part[:, shared:], down_part[:, shared:]), after)
    rows, size = mine.shape
    count = lax.axis_size("gx")
    here = lax.axis_index("gx")
    blocks = jnp.zeros((count, rows, size), mine.dtype)
    for step in range(count):
        got = mine if step == 0 else ahead(mine, "gx", step)
        blocks = lax.dynamic_update_index_in_dim(blocks, got, (here - step) % count, 0)
    return quarters, blocks.reshape(count * rows, size)


def finish_feed_forward(quarters, own, theirs):
    first_half = half_index() == 0
    first_side = lax.axis_index("gy") == 0
    sides = (jnp.where(first_side, own, theirs), jnp.where(first_side, theirs, own))
    others = [swap(side, "dp", 1) for side in sides]
    ups = [jnp.where(first_half, a, b) for a, b in zip(sides, others)]
    downs = [jnp.where(first_half, b, a) for a, b in zip(sides, others)]
    wholes = []
    for pieces, rest in ((slice(0, 2), ups), (slice(2, 4), downs)):
        wholes.append(
            jnp.concatenate([p for side in range(2) for p in quarters[side][pieces] + [rest[side]]], axis=1)
        )
    return wholes


def core_step(keep, give):
    return add(keep, swap(give, "dp", 1))


def both_halves(keep, give):
    count, size, columns = keep.shape
    return jnp.stack([keep, give], axis=1).reshape(2 * count * size, columns)


def add(a, b):
    return (a.astype(jnp.float32) + b.astype(jnp.float32)).astype(jnp.bfloat16)


def chips_parts(sides):
    columns = sides[0].shape[-1]
    size = pl.cdiv(columns // 128, 2) * 128
    own_first = lax.axis_index("dp") // 2 == 0
    first, second = (
        jnp.concatenate([side[..., at : at + size] for side in sides], axis=-1) for at in (0, columns - size)
    )
    return jnp.where(own_first, first, second), jnp.where(own_first, second, first)


def chips_step(parts, end=()):
    keep, give = parts
    return add(keep, gate(swap(give, "dp", 2), end))


def two(value):
    size = value.shape[-1] // 2
    return value[..., :size], value[..., size:]


def overlap_join(value, columns, end=()):
    size = value.shape[-1]
    other = gate(swap(value, "dp", 2), end)
    own_first = lax.axis_index("dp") // 2 == 0
    first, second = jnp.where(own_first, value, other), jnp.where(own_first, other, value)
    return jnp.concatenate([first, second[..., 2 * size - columns :]], axis=-1)


def blocks_step(value, begin=()):
    value = gate(value, begin)
    count = lax.axis_size("gx")
    here = lax.axis_index("gx")
    total = lax.dynamic_index_in_dim(value, here, 0, False).astype(jnp.float32)
    for step in range(1, count):
        give = lax.dynamic_index_in_dim(value, (here + step) % count, 0, False)
        total = total + ahead(give, "gx", step).astype(jnp.float32)
    return total.astype(jnp.bfloat16)


def join_step(value, end=()):
    columns = value.shape[-1]
    return pair_rows(value, gate(swap(value, "dp", 1), end)).reshape(-1, columns).astype(jnp.float32)


def side_parts(first, second):
    first_side = lax.axis_index("gy") == 0
    return jnp.where(first_side, first, second), jnp.where(first_side, second, first)


def side_exchange(first, second):
    keep, give = side_parts(first, second)
    return add(keep, swap(give, "gy", 1))


def projection_sides(first, rest):
    query, key, value = (first[..., n * GROUP : (n + 1) * GROUP] for n in range(3))
    size = rest.shape[-1] // 3
    query_rest, key_rest, value_rest = (rest[..., n * size : n * size + GROUP + 128] for n in range(3))
    return (
        jnp.concatenate([query, key, query_rest, key_rest[..., :128]], axis=-1),
        jnp.concatenate([value, key_rest, value_rest], axis=-1),
    )


def join_projections(whole, width):
    rest = width - GROUP
    spare = width // 2 - GROUP
    wide = GROUP + 128
    query, key = whole[:, :GROUP], whole[:, GROUP : 2 * GROUP]
    query_rest = whole[:, 2 * GROUP : 2 * GROUP + rest]
    key_spare = whole[:, 2 * GROUP + wide : 2 * GROUP + wide + spare]
    value = whole[:, :GROUP]
    key_rest = whole[:, GROUP + spare : GROUP + rest]
    value_rest = whole[:, GROUP + wide : GROUP + wide + rest]
    return jnp.where(
        lax.axis_index("gy") == 0,
        jnp.concatenate([query, query_rest, key, key_spare], axis=1),
        jnp.concatenate([key_rest, value, value_rest], axis=1),
    )


def scatter_plain(whole):
    part = lax.psum_scatter(whole, "gy", scatter_dimension=1, tiled=True)
    part = lax.psum_scatter(part, "gx", scatter_dimension=0, tiled=True)
    return lax.psum(part, "dp").astype(jnp.float32)


def all_tokens(own):
    count = lax.axis_size("gy")
    here = lax.axis_index("gy")
    if count != 2:
        return lax.all_gather(own, "gy", axis=0, tiled=True)
    other = swap(own, "gy", 1)
    first = here == 0
    return jnp.concatenate([jnp.where(first, own, other), jnp.where(first, other, own)], axis=0)


def others_tokens(whole):
    count = lax.axis_size("gy")
    here = lax.axis_index("gy")
    rows = whole.shape[0] // count
    if count != 2:
        keep = lax.dynamic_slice_in_dim(whole, here * rows, rows, 0)
        total = lax.psum_scatter(whole, "gy", scatter_dimension=0, tiled=True)
        return (total.astype(jnp.float32) - keep.astype(jnp.float32)).astype(jnp.bfloat16)
    return swap(lax.dynamic_slice_in_dim(whole, (1 - here) * rows, rows, 0), "gy", 1)


def dot(a, b):
    return jnp.dot(a, b, preferred_element_type=jnp.float32)


def local(
    prompt,
    continuations,
    prefix_len,
    attn_gain,
    attn_shift,
    qkv_weight,
    query_bias,
    value_bias,
    out_weight,
    out_bias,
    mlp_gain,
    mlp_shift,
    up_weight,
    up_bias,
    down_weight,
    down_bias,
    grad_prompt,
    grad_continuations,
):
    groups, shard, width = prompt.shape
    length = continuations.shape[1]
    first_pos = lax.axis_index("gy") * shard
    prompt_len = shard * lax.axis_size("gy")
    block = shard // 2
    halved = by_halves(width // 2)
    spans = [slice(0, GROUP), slice(GROUP, width)]

    if halved:
        limit, other_limit = prefix_len[0], swap(prefix_len, "gy", 1)[0]
        is_first = first_pos == 0
        is_long = jnp.logical_or(limit > other_limit, jnp.logical_and(limit == other_limit, is_first))
        kept_at = jnp.where(is_long, 0, block)
        places = [first_pos + kept_at, shard - first_pos + kept_at, limit]
    else:
        places = [first_pos, first_pos + block, prefix_len[0]]
    places = jnp.stack(places).astype(jnp.int32)

    def kept_rows(own):
        return lax.dynamic_slice_in_dim(own, kept_at, block, 0)

    def given_rows(own):
        return lax.dynamic_slice_in_dim(own, block - kept_at, block, 0)

    def back_home(done):
        if not halved:
            return done
        kept, home = done[:block], swap(done[block:], "gy", 1)
        return jnp.concatenate([jnp.where(is_long, kept, home), jnp.where(is_long, home, kept)], axis=0)

    own_prompt = prompt.reshape(shard, width)
    branch = continuations.reshape(length, width)
    own_cot = grad_prompt.reshape(shard, width)
    branch_cot = grad_continuations.reshape(length, width)
    whole_prompt = all_tokens(own_prompt)
    if halved:
        weights, out_full, raw = gather_projections(qkv_weight, out_weight, width)
        quarters, fetched = gather_feed_forward(up_weight, down_weight.T, (raw,))
        other_cot = swap(gate(given_rows(own_cot), (raw,)), "gy", 1)
        cotangent = jnp.concatenate([kept_rows(own_cot), other_cot, branch_cot], axis=0)
    else:
        qkv = gather_plain(qkv_weight)
        weights = [[qkv[:, c.start + s : c.stop + s] for s in (0, width, 2 * width)] for c in spans]
        out_full, up_full, down_full = (gather_plain(w) for w in (out_weight, up_weight, down_weight.T))
        cotangent = jnp.concatenate([own_cot, branch_cot], axis=0)

    all_rows = jnp.concatenate([whole_prompt, branch], axis=0)
    norm_all, _ = normalise(all_rows.astype(jnp.float32))
    act_all = (norm_all * attn_gain + attn_shift).astype(jnp.bfloat16)
    projected, mixed, stats = [], [], []
    for number, (cols, (w_query, w_key, w_value)) in enumerate(zip(spans, weights)):
        projected.append(
            (
                (dot(act_all, w_query) + query_bias[cols]).astype(jnp.bfloat16),
                dot(act_all, w_key).astype(jnp.bfloat16),
                (dot(act_all, w_value) + value_bias[cols]).astype(jnp.bfloat16),
            )
        )
        got, stat = attention_forward(places, *projected[-1], block, length)
        if halved and number == 0:
            fetched = gate(fetched, (got, cotangent))
            theirs = swap(fetched, "gy", 1)
        if halved and number == 1:
            up_full, down_full = finish_feed_forward(quarters, fetched, gate(theirs, (got,)))
        mixed.append(got)
        stats.append(stat)

    tokens = jnp.concatenate(
        [lax.dynamic_slice_in_dim(whole_prompt, places[n], block, 0) for n in range(2)] + [branch], axis=0
    )
    all_turned, cotangent_turned = act_all.T, cotangent.T
    hidden, slope, result, act_turned, norm_two, pace_two = mlp_forward(
        mixed,
        tokens,
        out_full,
        out_bias,
        mlp_gain,
        mlp_shift,
        up_full,
        up_bias,
        down_full,
        down_bias,
        (all_turned, cotangent_turned),
    )
    count = lax.axis_size("gx")
    half = jnp.reshape(half_index() if halved else 0, (1,)).astype(jnp.int32)
    tiles = up_full.shape[1] // TILE
    part = tiles // 2
    prompt_out = back_home(result[:shard]).reshape(groups, shard, width)
    continuation_out = result[shard:].reshape(1, length, width)
    down_keep, down_give = down_back(half, count, cotangent_turned, hidden)
    after = ()
    if halved:
        down_flow = core_step(down_keep, down_give)
        after = (down_flow, prompt_out)
    so_far, up_keep, up_give, up_bias_grad = up_back(
        half, count, (0, part), act_turned, cotangent, slope, up_full, down_full
    )
    d_resid, d_branch, *d_mixed, keep_rest, give_rest, out_keep, out_give, bias_rest, lines = up_back(
        half,
        count,
        (part, tiles),
        act_turned,
        cotangent,
        slope,
        up_full,
        down_full,
        (so_far, norm_two, pace_two, mlp_gain, mixed, out_full),
        after,
    )
    up_bias_grad = jnp.concatenate([up_bias_grad, bias_rest], axis=1)
    mlp_gain_grad, mlp_shift_grad, out_bias_grad, down_bias_grad = (lines[n] for n in range(4))
    if halved:
        side = up_weight.shape[1]
        up_flow = core_step(up_keep, gate(up_give, (down_flow,)))
        keep, give = chips_parts((down_flow[..., :side], down_flow[..., side:]))
        down_flow = chips_step((keep, gate(give, (so_far,))))
        ready = (down_flow, up_flow)
        rest_flow, out_flow = core_step(keep_rest, gate(give_rest, ready)), core_step(out_keep, gate(out_give, ready))
        ready = (rest_flow, out_flow)
        up_flow = jnp.concatenate([up_flow, rest_flow], axis=-1)
        down_flow = gate(down_flow, ready)
        after = (down_flow, up_flow, out_flow)
    d_parts = [None, None]
    for number in (1, 0):
        d_parts[number] = attention_backward(
            places, *projected[number], mixed[number], d_mixed[number], stats[number], block, length, after
        )
        if halved and number == 1:
            up_flow = side_exchange(
                jnp.concatenate([up_flow[..., :side], out_flow[..., : width // 2]], axis=-1),
                jnp.concatenate([up_flow[..., side:], out_flow[..., width // 2 :]], axis=-1),
            )
            down_flow = blocks_step(down_flow)
            after = (up_flow, down_flow)
        if halved and number == 0:
            up_flow = blocks_step(up_flow)
            down_keep, down_give = side_parts(*two(down_flow))
            home_give = gate(d_branch[block:shard], (d_parts[0][0],))
            after = (up_flow, down_give, home_give)
    keep_a, give_a, bias_a, keep_b, give_b, bias_b = weights_back(half, count, all_turned, d_parts, after)
    if halved:
        sides = projection_sides(core_step(keep_a, give_a), core_step(keep_b, give_b))
        parts = chips_parts(sides)
        up_flow = add(up_flow, gate(swap(up_flow, "dp", 2), (keep_a,)))
        down_flow = add(down_keep, gate(swap(down_give, "gy", 1), (keep_a,)))
        home = gate(swap(home_give, "gy", 1), (keep_a,)).astype(jnp.float32)
        after = (*parts, up_flow, down_flow)
    else:
        after = (keep_a,)
    d_act_all, act_lines = tokens_back(d_parts, weights, all_rows, length, after)
    attn_gain_grad, attn_shift_grad = act_lines[0], act_lines[1]
    others = others_tokens(d_act_all[:prompt_len])
    if halved:
        qkv_flow = chips_step(parts, (d_act_all,))
        up_total = join_step(up_flow, (d_act_all,))
        down_flow = overlap_join(down_flow, side, (d_act_all,))
        qkv_flow = blocks_step(qkv_flow)
        others = gate(others, (qkv_flow,))
        down_total = join_step(gate(down_flow, (qkv_flow,)))
    size = bias_b.shape[1] // 3
    query_bias_grad, value_bias_grad = (
        jnp.concatenate(
            [bias_a[0, n * GROUP : (n + 1) * GROUP], bias_b[0, n * size : n * size + width - GROUP]]
        )
        for n in (0, 2)
    )
    if halved:
        qkv_flow = side_exchange(*two(qkv_flow))
        qkv_total = join_projections(join_step(overlap_join(qkv_flow, sides[0].shape[-1])), width)
        up_total, out_total = up_total[:, :side], up_total[:, side:]
    else:
        whole_a, whole_b = both_halves(keep_a, give_a), both_halves(keep_b, give_b)
        qkv_grad = jnp.concatenate(
            [
                piece
                for n in range(3)
                for piece in (
                    whole_a[:, n * GROUP : (n + 1) * GROUP],
                    whole_b[:, n * size : n * size + width - GROUP],
                )
            ],
            axis=1,
        )
        up_total, down_total, out_total, qkv_total = (
            scatter_plain(g)
            for g in (
                jnp.concatenate([both_halves(up_keep, up_give), both_halves(keep_rest, give_rest)], axis=1),
                both_halves(down_keep, down_give),
                both_halves(out_keep, out_give),
                qkv_grad,
            )
        )
    prompt_resid = d_resid[:shard]
    if halved:
        kept = prompt_resid[:block]
        kept = jnp.where(is_long, kept, home), jnp.where(is_long, home, kept)
        prompt_resid = jnp.concatenate(kept, axis=0)
    own_rows = jnp.concatenate([own_prompt, branch], axis=0)
    own_grad = jnp.concatenate(
        [lax.dynamic_slice_in_dim(d_act_all, first_pos, shard, 0), d_act_all[prompt_len:]], axis=0
    )
    resid_rows = jnp.concatenate([prompt_resid, d_resid[shard:]], axis=0)
    prompt_grad, branch_grad = rows_back(others, own_grad, own_rows, resid_rows, attn_gain, length)
    prompt_grad = prompt_grad.T.reshape(groups, shard, width)
    continuation_grad = branch_grad.T.reshape(1, length, width)
    vectors = (
        attn_gain_grad,
        attn_shift_grad,
        query_bias_grad,
        value_bias_grad,
        out_bias_grad,
        mlp_gain_grad,
        mlp_shift_grad,
        up_bias_grad.reshape(-1),
        down_bias_grad,
    )
    joined = jnp.sum(lax.all_gather(jnp.concatenate(vectors), ("dp", "gx", "gy")), axis=0)
    totals = []
    at = 0
    for vector in vectors:
        totals.append(joined[at : at + vector.shape[0]])
        at += vector.shape[0]
    return (
        prompt_out,
        continuation_out,
        prompt_grad,
        continuation_grad,
        totals[0],
        totals[1],
        qkv_total,
        totals[2],
        totals[3],
        out_total,
        totals[4],
        totals[5],
        totals[6],
        up_total,
        totals[7],
        down_total.T,
        totals[8],
    )


def solution(mesh):
    placed = (
        P(("dp", "gx"), "gy", None),
        P(("dp", "gx", "gy"), None, None),
        P(("dp", "gx", "gy")),
        P(),
        P(),
        P("gx", "gy"),
        P(),
        P(),
        P("gx", "gy"),
        P(),
        P(),
        P(),
        P("gx", "gy"),
        P(),
        P("gy", "gx"),
        P(),
        P(("dp", "gx"), "gy", None),
        P(("dp", "gx", "gy"), None, None),
    )
    return jax.shard_map(
        local,
        mesh=mesh,
        in_specs=placed,
        out_specs=(
            P(("dp", "gx"), "gy", None),
            P(("dp", "gx", "gy"), None, None),
            P(("dp", "gx"), "gy", None),
            P(("dp", "gx", "gy"), None, None),
            P(),
            P(),
            P("gx", "gy"),
            P(),
            P(),
            P("gx", "gy"),
            P(),
            P(),
            P(),
            P("gx", "gy"),
            P(),
            P("gy", "gx"),
            P(),
        ),
        check_vma=False,
    )
```

```python
import functools
import jax
import jax.numpy as jnp
from jax import lax
from jax.sharding import PartitionSpec as P
from jax.experimental import pallas as pl
from jax.experimental.pallas import tpu as pltpu

HEAD_DIM = 64
LOG2E = 1.4426950408889634
NEG = -1e30
BK = 512
GROUP = 512
epsilon = 1e-05


def nt(a, b):
    return lax.dot_general(a, b, (((1,), (1,)), ((), ())), preferred_element_type=jnp.float32)


def nn(a, b):
    return jnp.dot(a, b, preferred_element_type=jnp.float32)


def tn(a, b):
    return lax.dot_general(a, b, (((0,), (0,)), ((), ())), preferred_element_type=jnp.float32)


def halves(pair, total):
    lane = lax.broadcasted_iota(jnp.int32, (1, 128), 1)
    left = jnp.minimum(total - pair * 128, 128)
    return lane < 64, jnp.logical_and(lane >= 64, lane < left), lane < left


def norm_bounds(ref, valid, spread):
    part = jnp.where(valid, ref[...], jnp.zeros((), jnp.bfloat16))
    return jnp.max(nn(part * part, spread), axis=0, keepdims=True)


def query_rows(pos, number, size, span, is_branch):
    if is_branch:
        return pl.ds(span, size)
    return pl.ds(pl.multiple_of(pos[number], size), size)


def forward_kernel(pos, q, k, v, *rest, block, branch, width):
    o, lse, va, vc, vab, vcb, tops, accs = rest[-8:]
    pair = pl.program_id(0)
    scale = HEAD_DIM ** (-0.5) * LOG2E
    low, high, valid = halves(pair, width)
    zero = jnp.zeros((), jnp.bfloat16)
    one = jnp.ones((), jnp.bfloat16)
    span = k.shape[0] - branch
    for part, first, second in ((slice(0, span), va, vc), (slice(span, None), vab, vcb)):
        whole = v[part, :]
        first[...] = jnp.where(low, whole, one)
        second[...] = jnp.where(low, one, jnp.where(high, whole, zero))
    spread = (
        (lax.broadcasted_iota(jnp.int32, (128, 128), 0) < 64)
        == (lax.broadcasted_iota(jnp.int32, (128, 128), 1) < 64)
    ).astype(jnp.bfloat16)
    bound = jnp.max(norm_bounds(k, valid, spread) * norm_bounds(q, valid, spread)) * (scale * scale)
    plain = bound < 90.0 * 90.0
    rows = o.shape[0]
    blocks = [(start, block, False) for start in range(0, rows - branch, block)]
    blocks.append((rows - branch, branch, True))

    def finish(start, size, acc_a, acc_b, top):
        total = pltpu.roll(jnp.where(low, acc_b, acc_a), 64, 1)
        o[start : start + size, :] = (jnp.where(low, acc_a, acc_b) / total).astype(o.dtype)
        turned = (top + jnp.log2(total)).T
        lse[0, 0:1, start : start + size] = turned[0:1, :]
        lse[0, 1:2, start : start + size] = turned[64:65, :]

    def setup(number, start, size, is_branch):
        at = pos[number]
        query = q[query_rows(pos, number, size, span, is_branch), :]
        queries = (jnp.where(low, query, zero), jnp.where(high, query, zero))
        row = lax.broadcasted_iota(jnp.int32, (size, BK), 0)
        column = lax.broadcasted_iota(jnp.int32, (size, BK), 1)
        triangle = lax.broadcasted_iota(jnp.int32, (size, size), 1) <= lax.broadcasted_iota(
            jnp.int32, (size, size), 0
        )
        whole_blocks = at // BK

        def allowed(index):
            if is_branch:
                return column + index * BK < at
            return column + index * BK <= row + at

        end = (at + BK - 1) // BK if is_branch else whole_blocks + 1
        return queries, triangle, whole_blocks, allowed, end

    def read(index):
        rows_at = pl.ds(pl.multiple_of(index * BK, BK), BK)
        return jnp.where(valid, k[rows_at, :], zero), va[rows_at, :], vc[rows_at, :]

    def own():
        return jnp.where(valid, k[span:, :], zero), vab[...], vcb[...]

    @pl.when(plain)
    def _():
        for number, (start, size, is_branch) in enumerate(blocks):
            queries, triangle, whole_blocks, allowed, end = setup(number, start, size, is_branch)

            def step(key, first, second, carry, mask):
                out = []
                for query_h, value_h, acc in zip(queries, (first, second), carry):
                    probs = jnp.exp2(nt(query_h, key) * scale)
                    if mask is not None:
                        probs = jnp.where(mask, probs, 0.0)
                    out.append(acc + nn(probs.astype(jnp.bfloat16), value_h))
                return tuple(out)

            carry = (jnp.zeros((size, 128), jnp.float32),) * 2
            carry = lax.fori_loop(0, whole_blocks, lambda i, c: step(*read(i), c, None), carry)
            if is_branch:
                carry = lax.fori_loop(
                    whole_blocks, end, lambda i, c: step(*read(i), c, allowed(i)), carry
                )
                carry = step(*own(), carry, triangle)
            else:
                carry = step(*read(whole_blocks), carry, allowed(whole_blocks))
            finish(start, size, *carry, 0.0)

    @pl.when(jnp.logical_not(plain))
    def _():
        for number, (start, size, is_branch) in enumerate(blocks):
            queries, triangle, whole_blocks, allowed, end = setup(number, start, size, is_branch)

            def step(key, first, second, mask):
                for head, value_h in enumerate((first, second)):
                    top = tops[head, 0:size, :]
                    scores = jnp.where(mask, nt(queries[head], key), NEG)
                    new_top = jnp.maximum(top, jnp.max(scores, axis=1, keepdims=True))
                    probs = jnp.exp2((scores - new_top[:, 0:1]) * scale).astype(jnp.bfloat16)
                    fade = jnp.exp2((top - new_top) * scale)
                    accs[head, 0:size, :] = accs[head, 0:size, :] * fade + nn(probs, value_h)
                    tops[head, 0:size, :] = new_top

            accs[:, 0:size, :] = jnp.zeros((2, size, 128), jnp.float32)
            tops[:, 0:size, :] = jnp.full((2, size, 128), NEG, jnp.float32)

            @pl.loop(0, end)
            def _(index):
                step(*read(index), allowed(index))

            if is_branch:
                step(*own(), triangle)
            top = jnp.where(low, tops[0, 0:size, :], tops[1, 0:size, :]) * scale
            finish(start, size, accs[0, 0:size, :], accs[1, 0:size, :], top)


def busy(microseconds):
    return pl.CostEstimate(
        flops=int(microseconds * 1.0e9), bytes_accessed=int(microseconds * 1.0e6), transcendentals=0
    )


def attention_forward(pos, q, k, v, block, branch, after=()):
    total, width = q.shape
    span = total - branch
    rows = block * (pos.shape[0] - 1) + branch
    pairs = pl.cdiv(width, 128)

    def col(n):
        return pl.BlockSpec((n, 128), lambda p, pos: (0, p))

    return pl.pallas_call(
        functools.partial(forward_kernel, block=block, branch=branch, width=width),
        grid_spec=pltpu.PrefetchScalarGridSpec(
            num_scalar_prefetch=1,
            grid=(pairs,),
            in_specs=[col(total)] * 3 + [pl.BlockSpec(memory_space=pl.ANY)] * len(after),
            out_specs=[col(rows), pl.BlockSpec((1, 8, rows), lambda p, pos: (p, 0, 0))],
            scratch_shapes=[
                pltpu.VMEM((span, 128), jnp.bfloat16),
                pltpu.VMEM((span, 128), jnp.bfloat16),
                pltpu.VMEM((branch, 128), jnp.bfloat16),
                pltpu.VMEM((branch, 128), jnp.bfloat16),
                pltpu.VMEM((2, max(block, branch), 128), jnp.float32),
                pltpu.VMEM((2, max(block, branch), 128), jnp.float32),
            ],
        ),
        out_shape=[
            jax.ShapeDtypeStruct((rows, width), jnp.bfloat16),
            jax.ShapeDtypeStruct((pairs, 8, rows), jnp.float32),
        ],
        compiler_params=pltpu.CompilerParams(
            dimension_semantics=("arbitrary",), vmem_limit_bytes=32 * 2**20
        ),
        cost_estimate=busy(7 * pairs),
        name="attention_forward",
    )(pos, q, k, v, *after)


def backward_kernel(pos, q, k, v, o, do, lse, *rest, block, branch, width):
    dq, dk, dv = rest[-13:-10]
    kta, ktc, kam, vm, ktab, ktcb, kbm, vbm, dks, dvs = rest[-10:]
    pair = pl.program_id(0)
    scale = HEAD_DIM ** (-0.5)
    low, high, valid = halves(pair, width)
    zero = jnp.zeros((), jnp.bfloat16)
    span = k.shape[0] - branch
    prompt_part, branch_part = slice(0, span), slice(span, None)
    for part, whole_ref, turn_a, turn_b in ((prompt_part, kam, kta, ktc), (branch_part, kbm, ktab, ktcb)):
        whole = jnp.where(valid, k[part, :], zero)
        whole_ref[...] = whole
        turned = whole.T
        turn_a[...] = turned[0:64, :]
        turn_b[...] = turned[64:128, :]
    vm[...] = jnp.where(valid, v[prompt_part, :], zero)
    vbm[...] = jnp.where(valid, v[branch_part, :], zero)
    dq[...] = jnp.zeros_like(dq)
    dks[...] = jnp.zeros_like(dks)
    dvs[...] = jnp.zeros_like(dvs)
    rows = o.shape[0]
    blocks = [(start, block, False) for start in range(0, rows - branch, block)]
    blocks.append((rows - branch, branch, True))
    ones_a = jnp.broadcast_to(low, (8, 128)).astype(jnp.bfloat16)
    ones_b = jnp.broadcast_to(high, (8, 128)).astype(jnp.bfloat16)
    for number, (start, size, is_branch) in enumerate(blocks):
        at = pos[number]
        here = slice(start, start + size)
        query_at = query_rows(pos, number, size, span, is_branch)
        query = q[query_at, :]
        grad = do[here, :]
        queries = (jnp.where(low, query, zero), jnp.where(high, query, zero))
        grads = (jnp.where(low, grad, zero), jnp.where(high, grad, zero))
        product = jnp.where(valid, grad.astype(jnp.float32) * o[here, :].astype(jnp.float32), 0.0)
        upper = product.astype(jnp.bfloat16)
        lower = (product - upper.astype(jnp.float32)).astype(jnp.bfloat16)
        deltas = tuple((nt(m, upper) + nt(m, lower))[0:1, :] for m in (ones_a, ones_b))
        stats = (lse[0, 0:1, here], lse[0, 1:2, here])
        queries_cat = jnp.concatenate(queries, axis=0)
        grads_cat = jnp.concatenate(grads, axis=0)

        def step(key, value, first, second, mask):
            probs, dscores = [], []
            for query_h, grad_h, delta, stat in zip(queries, grads, deltas, stats):
                scores = nt(key, query_h)
                prob = jnp.exp2(scores * (scale * LOG2E) - stat)
                if mask is not None:
                    prob = jnp.where(mask, prob, 0.0)
                dprob = nt(value, grad_h)
                probs.append(prob.astype(jnp.bfloat16))
                dscores.append((prob * (dprob - delta)).astype(jnp.bfloat16))
            dscores_cat = jnp.concatenate(dscores, axis=1)
            dvalue = nn(jnp.concatenate(probs, axis=1), grads_cat)
            dkey = nn(dscores_cat, queries_cat)
            dquery = jnp.concatenate([nn(first, dscores[0]), nn(second, dscores[1])], axis=0)
            return dquery, dkey, dvalue

        def read(base):
            rows_at = pl.ds(pl.multiple_of(base, BK), BK)
            return kam[rows_at, :], vm[rows_at, :], kta[:, rows_at], ktc[:, rows_at]

        def accumulate(index, carry, mask):
            rows_at = pl.ds(pl.multiple_of(index * BK, BK), BK)
            dquery, dkey, dvalue = step(*read(index * BK), mask)
            dks[rows_at, :] += dkey
            dvs[rows_at, :] += dvalue
            return carry + dquery

        carry = jnp.zeros((128, size), jnp.float32)
        whole_blocks = at // BK
        carry = lax.fori_loop(0, whole_blocks, lambda i, c: accumulate(i, c, None), carry)
        row = lax.broadcasted_iota(jnp.int32, (BK, size), 0)
        column = lax.broadcasted_iota(jnp.int32, (BK, size), 1)
        if is_branch:
            carry = lax.fori_loop(
                whole_blocks,
                (at + BK - 1) // BK,
                lambda i, c: accumulate(i, c, row + i * BK < at),
                carry,
            )
            triangle = lax.broadcasted_iota(jnp.int32, (size, size), 0) <= lax.broadcasted_iota(
                jnp.int32, (size, size), 1
            )
            dquery, dkey, dvalue = step(kbm[...], vbm[...], ktab[...], ktcb[...], triangle)
            carry = carry + dquery
            dk[branch_part, :] = (dkey * scale).astype(dk.dtype)
            dv[branch_part, :] = dvalue.astype(dv.dtype)
        else:
            carry = accumulate(whole_blocks, carry, row + whole_blocks * BK <= column + at)
        dq[query_at, :] = (carry.T * scale).astype(dq.dtype)
    dk[prompt_part, :] = (dks[...] * scale).astype(dk.dtype)
    dv[prompt_part, :] = dvs[...].astype(dv.dtype)


def attention_backward(pos, q, k, v, o, do, lse, block, branch, after=()):
    total, width = q.shape
    span = total - branch
    rows = o.shape[0]
    pairs = pl.cdiv(width, 128)

    def col(n):
        return pl.BlockSpec((n, 128), lambda p, pos: (0, p))

    def scratch(n):
        wide = pltpu.VMEM((64, n), jnp.bfloat16)
        tall = pltpu.VMEM((n, 128), jnp.bfloat16)
        return [wide, wide, tall, tall]

    return pl.pallas_call(
        functools.partial(backward_kernel, block=block, branch=branch, width=width),
        grid_spec=pltpu.PrefetchScalarGridSpec(
            num_scalar_prefetch=1,
            grid=(pairs,),
            in_specs=[col(total)] * 3
            + [col(rows)] * 2
            + [pl.BlockSpec((1, 8, rows), lambda p, pos: (p, 0, 0))]
            + [pl.BlockSpec(memory_space=pl.ANY)] * len(after),
            out_specs=[col(total)] * 3,
            scratch_shapes=scratch(span)
            + scratch(branch)
            + [pltpu.VMEM((span, 128), jnp.float32), pltpu.VMEM((span, 128), jnp.float32)],
        ),
        out_shape=[jax.ShapeDtypeStruct((total, width), jnp.bfloat16)] * 3,
        compiler_params=pltpu.CompilerParams(
            dimension_semantics=("arbitrary",), vmem_limit_bytes=40 * 2**20
        ),
        cost_estimate=busy(10 * pairs),
        name="attention_backward",
    )(pos, q, k, v, o, do, lse, *after)


TILE = 256


def row_chunks(rows, size=256):
    return [slice(at, min(at + size, rows)) for at in range(0, rows, size)]


def fixed(shape):
    return pl.BlockSpec(shape, lambda *_: (0,) * len(shape), pipeline_mode=pl.Buffered(1))


def steady(shape):
    return pl.BlockSpec(shape, lambda *_: (0,) * len(shape))


def store_halves(value, half, keep, give):
    count, size = keep.shape[0], keep.shape[1]
    for block in range(count):
        first = value[2 * block * size : (2 * block + 1) * size, :]
        second = value[(2 * block + 1) * size : (2 * block + 2) * size, :]
        keep[block, :, :] = jnp.where(half == 0, first, second).astype(keep.dtype)
        give[block, :, :] = jnp.where(half == 0, second, first).astype(give.dtype)


def mlp_forward_kernel(
    mixed_a, mixed_b, tokens, out_w, out_bias, gain, shift, up, up_bias, down, down_bias, *rest
):
    hidden, slope, result, act_turned, norm, pace, act, acc = rest[-8:]
    step = pl.program_id(0)
    rows = tokens.shape[0]
    first = mixed_a.shape[1]

    @pl.when(step == 0)
    def _():
        for here in row_chunks(rows):
            resid = (
                tokens[here, :].astype(jnp.float32)
                + nn(mixed_a[here, :], out_w[:first, :])
                + nn(mixed_b[here, :], out_w[first:, :])
                + out_bias[...]
            )
            centred = resid - jnp.mean(resid, axis=1, keepdims=True)
            speed = lax.rsqrt(jnp.mean(centred * centred, axis=1, keepdims=True) + epsilon)
            normed = centred * speed
            acting = (normed * gain[...] + shift[...]).astype(jnp.bfloat16)
            act[here, :] = acting
            act_turned[:, here] = acting.T
            norm[here, :] = normed.astype(norm.dtype)
            pace[here, :] = jnp.broadcast_to(speed, (speed.shape[0], 128))
            acc[here, :] = resid + down_bias[...]

    for here in row_chunks(rows):
        pre = nn(act[here, :], up[...]) + up_bias[...]
        bell = jnp.exp2(pre * pre * (-0.5 * LOG2E))
        base = 1.0 + (0.3275911 * 0.7071067811865476) * jnp.abs(pre)
        t = pl.reciprocal(base, approx=True)
        t = t * (2.0 - base * t)
        series = t * (
            0.127414796 + t * (-0.142248368 + t * (0.7107068705 + t * (-0.7265760135 + t * 0.5307027145)))
        )
        tail = series * bell
        below = jnp.where(pre >= 0.0, 1.0 - tail, tail)
        exact = (pre * below).astype(jnp.bfloat16)
        hidden[here, :] = exact
        slope[here, :] = (below + pre * bell * 0.3989422804014327).astype(jnp.bfloat16)
        acc[here, :] += nt(exact, down[...])

    @pl.when(step == pl.num_programs(0) - 1)
    def _():
        result[...] = acc[...].astype(result.dtype)


def mlp_forward(
    mixed, tokens, out_w, out_bias, gain, shift, up, up_bias, down, down_bias, after=()
):
    rows, width = tokens.shape
    inner = up.shape[1]
    column = pl.BlockSpec((width, TILE), lambda j: (0, j))
    tall = pl.BlockSpec((rows, TILE), lambda j: (0, j))
    line = fixed((1, width))
    like = jax.ShapeDtypeStruct
    return pl.pallas_call(
        mlp_forward_kernel,
        grid=(inner // TILE,),
        in_specs=[
            fixed(mixed[0].shape),
            fixed(mixed[1].shape),
            fixed((rows, width)),
            fixed((width, width)),
            line,
            line,
            line,
            column,
            pl.BlockSpec((1, TILE), lambda j: (0, j)),
            column,
            line,
        ]
        + [pl.BlockSpec(memory_space=pl.ANY)] * len(after),
        out_specs=[
            tall,
            tall,
            steady((rows, width)),
            steady((width, rows)),
            steady((rows, width)),
            steady((rows, 128)),
        ],
        out_shape=[
            like((rows, inner), jnp.bfloat16),
            like((rows, inner), jnp.bfloat16),
            like((rows, width), jnp.bfloat16),
            like((width, rows), jnp.bfloat16),
            like((rows, width), jnp.bfloat16),
            like((rows, 128), jnp.float32),
        ],
        scratch_shapes=[pltpu.VMEM((rows, width), jnp.bfloat16), pltpu.VMEM((rows, width), jnp.float32)],
        compiler_params=pltpu.CompilerParams(
            dimension_semantics=("arbitrary",), vmem_limit_bytes=52 * 2**20
        ),
        cost_estimate=busy(50),
        name="mlp_forward",
    )(
        *mixed,
        tokens,
        out_w,
        *(v.reshape(1, width) for v in (out_bias, gain, shift)),
        up,
        up_bias.reshape(1, inner),
        down,
        down_bias.reshape(1, width),
        *after,
    )


def down_back_kernel(half, cot_turned, hidden, keep, give):
    store_halves(nn(cot_turned[...], hidden[...]), half[0], keep, give)


def down_back(half, count, cot_turned, hidden):
    width, rows = cot_turned.shape
    inner = hidden.shape[1]
    block = width // count // 2
    split = pl.BlockSpec((count, block, TILE), lambda j, half: (0, 0, j))
    return pl.pallas_call(
        down_back_kernel,
        grid_spec=pltpu.PrefetchScalarGridSpec(
            num_scalar_prefetch=1,
            grid=(inner // TILE,),
            in_specs=[fixed((width, rows)), pl.BlockSpec((rows, TILE), lambda j, half: (0, j))],
            out_specs=[split, split],
        ),
        out_shape=[jax.ShapeDtypeStruct((count, block, inner), jnp.bfloat16)] * 2,
        compiler_params=pltpu.CompilerParams(
            dimension_semantics=("arbitrary",), vmem_limit_bytes=32 * 2**20
        ),
        cost_estimate=busy(15),
        name="down_back",
    )(half, cot_turned, hidden)


def up_back_step(half, act_turned, cot, slope, up, down, total, keep, give, bias_grad):
    bias = jnp.zeros((1, TILE), jnp.float32)
    pieces = []
    for here in row_chunks(cot.shape[0]):
        d_pre = (nn(cot[here, :], down[...]) * slope[here, :].astype(jnp.float32)).astype(jnp.bfloat16)
        bias = bias + jnp.sum(d_pre.astype(jnp.float32), axis=0, keepdims=True)
        total[here, :] += nt(d_pre, up[...])
        pieces.append(d_pre)
    bias_grad[...] = bias
    store_halves(nn(act_turned[...], jnp.concatenate(pieces, axis=0)), half[0], keep, give)


def up_back_first_kernel(half, act_turned, cot, slope, up, down, total, keep, give, bias_grad):
    @pl.when(pl.program_id(0) == 0)
    def _():
        total[...] = jnp.zeros_like(total)

    up_back_step(half, act_turned, cot, slope, up, down, total, keep, give, bias_grad)


def up_back_last_kernel(
    half, act_turned, cot, slope, up, down, so_far, norm, pace, gain, mixed_a, mixed_b, out_w, *rest
):
    d_resid, d_branch, d_mixed_a, d_mixed_b, keep, give, out_keep, out_give, bias_grad, lines, piece = rest[-11:]
    step = pl.program_id(0)
    rows, width = cot.shape
    first = mixed_a.shape[1]

    @pl.when(step == 0)
    def _():
        d_resid[...] = so_far[...]

    up_back_step(half, act_turned, cot, slope, up, down, d_resid, keep, give, bias_grad)

    @pl.when(step == pl.num_programs(0) - 1)
    def _():
        sums = [jnp.zeros((1, width), jnp.float32)] * 4
        for here in row_chunks(rows):
            grad = d_resid[here, :]
            normed = norm[here, :].astype(jnp.float32)
            scaled = grad * gain[...]
            inner = (
                scaled
                - jnp.mean(scaled, axis=1, keepdims=True)
                - normed * jnp.mean(scaled * normed, axis=1, keepdims=True)
            )
            exact = cot[here, :].astype(jnp.float32)
            total = exact + pace[here, 0:1] * inner
            d_resid[here, :] = total
            rounded = total.astype(jnp.bfloat16)
            d_branch[here, :] = rounded
            d_mixed_a[here, :] = nt(rounded, out_w[:first, :]).astype(d_mixed_a.dtype)
            d_mixed_b[here, :] = nt(rounded, out_w[first:, :]).astype(d_mixed_b.dtype)
            for n, term in enumerate((grad * normed, grad, rounded.astype(jnp.float32), exact)):
                sums[n] = sums[n] + jnp.sum(term, axis=0, keepdims=True)
        for n in range(4):
            lines[n : n + 1, :] = sums[n]
        for columns in row_chunks(width):
            size = columns.stop - columns.start
            piece[:first, :size] = tn(mixed_a[...], d_branch[:, columns])
            piece[first:, :size] = tn(mixed_b[...], d_branch[:, columns])
            value = piece[:, :size]
            store_halves(value, half[0], out_keep.at[:, :, columns], out_give.at[:, :, columns])


def up_back(half, count, tiles, act_turned, cot, slope, up, down, final=None, after=()):
    rows, width = cot.shape
    block = width // count // 2
    low, high = tiles
    inner = (high - low) * TILE
    split = pl.BlockSpec((count, block, TILE), lambda j, half: (0, 0, j))
    column = pl.BlockSpec((width, TILE), lambda j, half: (0, j + low))
    like = jax.ShapeDtypeStruct
    in_specs = [
        fixed((width, rows)),
        fixed((rows, width)),
        pl.BlockSpec((rows, TILE), lambda j, half: (0, j + low)),
        column,
        column,
    ]
    operands = [half, act_turned, cot, slope, up, down]
    out_specs = [steady((rows, width))]
    out_shape = [like((rows, width), jnp.float32)]
    scratch = []
    if final is not None:
        so_far, norm, pace, gain, mixed, out_w = final
        in_specs += [
            fixed((rows, width)),
            fixed((rows, width)),
            fixed((rows, 128)),
            fixed((1, width)),
            fixed(mixed[0].shape),
            fixed(mixed[1].shape),
            fixed((width, width)),
        ]
        operands += [so_far, norm, pace, gain.reshape(1, width), *mixed, out_w]
        out_specs += [steady((rows, width))] + [steady(m.shape) for m in mixed]
        out_shape += [like((rows, width), jnp.bfloat16)] + [like(m.shape, jnp.bfloat16) for m in mixed]
        scratch = [pltpu.VMEM((width, TILE), jnp.float32)]
    out_specs += [split] * 2
    out_shape += [like((count, block, inner), jnp.bfloat16)] * 2
    if final is not None:
        out_specs += [steady((count, block, width))] * 2
        out_shape += [like((count, block, width), jnp.bfloat16)] * 2
    out_specs += [pl.BlockSpec((1, TILE), lambda j, half: (0, j))]
    out_shape += [like((1, inner), jnp.float32)]
    if final is not None:
        out_specs += [steady((8, width))]
        out_shape += [like((8, width), jnp.float32)]
        in_specs += [pl.BlockSpec(memory_space=pl.ANY)] * len(after)
        operands += after
    return pl.pallas_call(
        up_back_first_kernel if final is None else up_back_last_kernel,
        grid_spec=pltpu.PrefetchScalarGridSpec(
            num_scalar_prefetch=1,
            grid=(high - low,),
            in_specs=in_specs,
            out_specs=out_specs,
            scratch_shapes=scratch,
        ),
        out_shape=out_shape,
        compiler_params=pltpu.CompilerParams(
            dimension_semantics=("arbitrary",), vmem_limit_bytes=58 * 2**20
        ),
        cost_estimate=busy(30 if final is None else 50),
        name="up_back_first" if final is None else "up_back_last",
    )(*operands)


def tokens_back_kernel(*refs):
    grads, weights, rows = refs[0:6], refs[6:12], refs[12]
    out, lines = refs[-2:]
    values = rows[...].astype(jnp.float32)
    centred = values - jnp.mean(values, axis=1, keepdims=True)
    normed = centred * lax.rsqrt(jnp.mean(centred * centred, axis=1, keepdims=True) + epsilon)
    total = sum(nt(grad[...], weight[...]) for grad, weight in zip(grads, weights))
    width = total.shape[1]
    out[:, :width] = total.astype(out.dtype)
    out[:, width:] = jnp.zeros((out.shape[0], out.shape[1] - width), out.dtype)

    @pl.when(pl.program_id(0) == 0)
    def _():
        lines[...] = jnp.zeros_like(lines)

    lines[0:1, :] += jnp.sum(total * normed, axis=0, keepdims=True)
    lines[1:2, :] += jnp.sum(total, axis=0, keepdims=True)


def tokens_back(grads, weights, rows, size, after=()):
    total, width = rows.shape
    flat_grads, flat_weights = [g for group in grads for g in group], [w for group in weights for w in group]
    tall = pl.BlockSpec((size, width), lambda t: (t, 0))
    wide = pl.cdiv(width, 128) * 128
    return pl.pallas_call(
        tokens_back_kernel,
        grid=(total // size,),
        in_specs=[pl.BlockSpec((size, g.shape[1]), lambda t: (t, 0)) for g in flat_grads]
        + [fixed(w.shape) for w in flat_weights]
        + [tall]
        + [pl.BlockSpec(memory_space=pl.ANY)] * len(after),
        out_specs=[pl.BlockSpec((size, wide), lambda t: (t, 0)), steady((8, width))],
        out_shape=[
            jax.ShapeDtypeStruct((total, wide), jnp.bfloat16),
            jax.ShapeDtypeStruct((8, width), jnp.float32),
        ],
        compiler_params=pltpu.CompilerParams(
            dimension_semantics=("arbitrary",), vmem_limit_bytes=40 * 2**20
        ),
        cost_estimate=busy(20),
        name="tokens_back",
    )(*flat_grads, *flat_weights, rows, *after)


def weights_back_kernel(half, turned, *refs, tiles):
    outs = refs[-6:]
    step = pl.program_id(0)
    for group in range(2):
        keep, give, bias = outs[group * 3 : group * 3 + 3]
        start, size = group * 3 * tiles[0], tiles[group]
        for kind in range(3):
            grad = refs[group * 3 + kind]

            @pl.when(jnp.logical_and(step >= start + kind * size, step < start + (kind + 1) * size))
            def _():
                part = grad[...]
                store_halves(nn(turned[...], part), half[0], keep, give)
                bias[...] = jnp.sum(part.astype(jnp.float32), axis=0, keepdims=True)


def weights_back(half, count, turned, grads, after=()):
    width, total = turned.shape
    tiles = [pl.cdiv(group[0].shape[1], TILE) for group in grads]
    block = width // count // 2
    like = jax.ShapeDtypeStruct
    in_specs, out_specs, out_shape = [], [], []
    for group in range(2):
        start, size = group * 3 * tiles[0], tiles[group]
        for kind in range(3):
            at = start + kind * size
            in_specs.append(
                pl.BlockSpec(
                    (total, TILE), lambda t, half, at=at, size=size: (0, jnp.clip(t - at, 0, size - 1))
                )
            )

        def place(t, start=start, size=size):
            return jnp.clip(t - start, 0, 3 * size - 1)

        out_specs += [
            pl.BlockSpec((count, block, TILE), lambda t, half, place=place: (0, 0, place(t)))
        ] * 2 + [pl.BlockSpec((1, TILE), lambda t, half, place=place: (0, place(t)))]
        columns = 3 * size * TILE
        out_shape += [like((count, block, columns), jnp.bfloat16)] * 2 + [like((1, columns), jnp.float32)]
    return pl.pallas_call(
        functools.partial(weights_back_kernel, tiles=tiles),
        grid_spec=pltpu.PrefetchScalarGridSpec(
            num_scalar_prefetch=1,
            grid=(3 * sum(tiles),),
            in_specs=[fixed((width, total))]
            + in_specs
            + [pl.BlockSpec(memory_space=pl.ANY)] * len(after),
            out_specs=out_specs,
        ),
        out_shape=out_shape,
        compiler_params=pltpu.CompilerParams(
            dimension_semantics=("arbitrary",), vmem_limit_bytes=52 * 2**20
        ),
        cost_estimate=busy(25),
        name="weights_back",
    )(half, turned, *grads[0], *grads[1], *after)


def rows_back_kernel(others, own, rows, resid, gain, prompt_out, branch_out):
    step = pl.program_id(0)
    last = pl.num_programs(0) - 1
    values = rows[...].astype(jnp.float32)
    centred = values - jnp.mean(values, axis=1, keepdims=True)
    pace = lax.rsqrt(jnp.mean(centred * centred, axis=1, keepdims=True) + epsilon)
    normed = centred * pace
    width = values.shape[1]
    received = jnp.where(step == last, 0.0, others[:, :width].astype(jnp.float32))
    grad = own[:, :width].astype(jnp.float32) + received
    scaled = grad * gain[...]
    inner = (
        scaled
        - jnp.mean(scaled, axis=1, keepdims=True)
        - normed * jnp.mean(scaled * normed, axis=1, keepdims=True)
    )
    turned = (resid[...] + pace * inner).T

    @pl.when(step < last)
    def _():
        prompt_out[...] = turned

    @pl.when(step == last)
    def _():
        branch_out[...] = turned


def rows_back(others, own, rows, resid, gain, branch):
    total, width = rows.shape
    wide = own.shape[1]
    shard = total - branch
    steps = shard // branch
    tall = pl.BlockSpec((branch, width), lambda t: (t, 0))
    return pl.pallas_call(
        rows_back_kernel,
        grid=(steps + 1,),
        in_specs=[
            pl.BlockSpec((branch, wide), lambda t: (jnp.minimum(t, steps - 1), 0)),
            pl.BlockSpec((branch, wide), lambda t: (t, 0)),
            tall,
            tall,
            fixed((1, width)),
        ],
        out_specs=[
            pl.BlockSpec((width, branch), lambda t: (0, jnp.minimum(t, steps - 1))),
            pl.BlockSpec((width, branch), lambda t: (0, 0)),
        ],
        out_shape=[
            jax.ShapeDtypeStruct((width, shard), jnp.float32),
            jax.ShapeDtypeStruct((width, branch), jnp.float32),
        ],
        compiler_params=pltpu.CompilerParams(
            dimension_semantics=("arbitrary",), vmem_limit_bytes=40 * 2**20
        ),
        cost_estimate=busy(10),
        name="rows_back",
    )(others, own, rows, resid, gain.reshape(1, width))


def gate_kernel(*refs):
    pass


def gate(value, after):
    if not after:
        return value
    anywhere = pl.BlockSpec(memory_space=pl.ANY)
    return pl.pallas_call(
        gate_kernel,
        in_specs=[anywhere] * (1 + len(after)),
        out_specs=anywhere,
        out_shape=jax.ShapeDtypeStruct(value.shape, value.dtype),
        input_output_aliases={0: 0},
        cost_estimate=busy(1),
        name="gate",
    )(value, *after)


def normalise(values_in):
    centre = jnp.mean(values_in, axis=-1, keepdims=True)
    centred = values_in - centre
    spread = jnp.mean(centred * centred, axis=-1, keepdims=True)
    pace = lax.rsqrt(spread + epsilon)
    return centred * pace, pace


def swap(value, axis, bit):
    count = lax.axis_size(axis)
    return lax.ppermute(value, axis, [(i, i ^ bit) for i in range(count)])


def ahead(value, axis, step):
    count = lax.axis_size(axis)
    return lax.ppermute(value, axis, [(i, (i + step) % count) for i in range(count)])


def by_halves(half_width):
    return lax.axis_size("dp") == 4 and lax.axis_size("gy") == 2 and half_width > GROUP


def half_index():
    return lax.axis_index("dp") % 2


def pair_rows(mine, theirs):
    first = half_index() == 0
    return jnp.stack([jnp.where(first, mine, theirs), jnp.where(first, theirs, mine)], axis=-3)


def gather_plain(part):
    part = lax.all_gather(part, "gy", axis=1, tiled=True)
    return lax.all_gather(part, "gx", axis=0, tiled=True)


def gather_quarters(part):
    rows, columns = part.shape
    copies, gx, gy = (lax.axis_size(axis) for axis in ("dp", "gx", "gy"))
    size = columns // copies
    mine = lax.dynamic_slice_in_dim(part, lax.axis_index("dp") * size, size, 1)
    raw = lax.all_gather(mine, ("dp", "gx", "gy"))
    got = raw.reshape(copies, gx, gy, rows, size)
    return raw, [
        [got[quarter, :, side].reshape(gx * rows, size) for quarter in range(copies)]
        for side in range(gy)
    ]


def gather_projections(qkv_part, out_part, width):
    rows = qkv_part.shape[0]
    half = width // 2
    first_side = lax.axis_index("gy") == 0
    key_at = width - half
    here = jnp.where(
        first_side,
        qkv_part[:, :GROUP],
        qkv_part[:, half : half + GROUP],
    )
    keys_here = jnp.where(first_side, qkv_part[:, width : width + GROUP], qkv_part[:, :GROUP])
    raw, one = gather_quarters(jnp.concatenate([here, keys_here], axis=1))
    rest = width - GROUP
    spare = half - GROUP
    queries_rest = jnp.where(first_side, qkv_part[:, GROUP:width], qkv_part[:, half + GROUP :])
    keys_rest = jnp.where(first_side, qkv_part[:, width + GROUP :], qkv_part[:, GROUP:half])

    def pad(value, size):
        return jnp.pad(value, ((0, 0), (0, size - value.shape[1])))

    outer = pl.cdiv(rest + spare, 128) * 128
    out_size = pl.cdiv(half, 128) * 128
    total = pl.cdiv(outer + out_size, 512) * 512
    packed = pad(jnp.concatenate([queries_rest, keys_rest], axis=1), outer)
    packed = pad(jnp.concatenate([packed, pad(out_part, out_size)], axis=1), total)
    two = [jnp.concatenate(side, axis=1) for side in gather_quarters(packed)[1]]
    first = [
        jnp.concatenate(one[0][:2], axis=1),
        jnp.concatenate(one[0][2:], axis=1),
        jnp.concatenate(one[1][:2], axis=1),
    ]
    second = [
        two[0][:, :rest],
        jnp.concatenate(
            [two[0][:, rest : rest + spare]] + one[1][2:] + [two[1][:, rest : rest + spare]], axis=1
        ),
        two[1][:, :rest],
    ]
    out_full = jnp.concatenate([side[:, outer : outer + half] for side in two], axis=1)
    return [first, second], out_full, raw


def gather_feed_forward(up_part, down_part, after):
    columns = up_part.shape[1]
    shared = columns // 2 // 512 * 512
    _, quarters = gather_quarters(jnp.concatenate([up_part[:, :shared], down_part[:, :shared]], axis=1))
    first_half = half_index() == 0
    mine = gate(jnp.where(first_half, up_part[:, shared:], down_part[:, shared:]), after)
    rows, size = mine.shape
    count = lax.axis_size("gx")
    here = lax.axis_index("gx")
    blocks = jnp.zeros((count, rows, size), mine.dtype)
    for step in range(count):
        got = mine if step == 0 else ahead(mine, "gx", step)
        blocks = lax.dynamic_update_index_in_dim(blocks, got, (here - step) % count, 0)
    return quarters, blocks.reshape(count * rows, size)


def finish_feed_forward(quarters, own, theirs):
    first_half = half_index() == 0
    first_side = lax.axis_index("gy") == 0
    sides = (jnp.where(first_side, own, theirs), jnp.where(first_side, theirs, own))
    others = [swap(side, "dp", 1) for side in sides]
    ups = [jnp.where(first_half, a, b) for a, b in zip(sides, others)]
    downs = [jnp.where(first_half, b, a) for a, b in zip(sides, others)]
    wholes = []
    for pieces, rest in ((slice(0, 2), ups), (slice(2, 4), downs)):
        wholes.append(
            jnp.concatenate([p for side in range(2) for p in quarters[side][pieces] + [rest[side]]], axis=1)
        )
    return wholes


def core_step(keep, give):
    return add(keep, swap(give, "dp", 1))


def both_halves(keep, give):
    count, size, columns = keep.shape
    return jnp.stack([keep, give], axis=1).reshape(2 * count * size, columns)


def add(a, b):
    return (a.astype(jnp.float32) + b.astype(jnp.float32)).astype(jnp.bfloat16)


def chips_parts(sides):
    columns = sides[0].shape[-1]
    size = pl.cdiv(columns // 128, 2) * 128
    own_first = lax.axis_index("dp") // 2 == 0
    first, second = (
        jnp.concatenate([side[..., at : at + size] for side in sides], axis=-1) for at in (0, columns - size)
    )
    return jnp.where(own_first, first, second), jnp.where(own_first, second, first)


def chips_step(parts, end=()):
    keep, give = parts
    return add(keep, gate(swap(give, "dp", 2), end))


def two(value):
    size = value.shape[-1] // 2
    return value[..., :size], value[..., size:]


def overlap_join(value, columns, end=()):
    size = value.shape[-1]
    other = gate(swap(value, "dp", 2), end)
    own_first = lax.axis_index("dp") // 2 == 0
    first, second = jnp.where(own_first, value, other), jnp.where(own_first, other, value)
    return jnp.concatenate([first, second[..., 2 * size - columns :]], axis=-1)


def blocks_step(value, begin=()):
    value = gate(value, begin)
    count = lax.axis_size("gx")
    here = lax.axis_index("gx")
    total = lax.dynamic_index_in_dim(value, here, 0, False).astype(jnp.float32)
    for step in range(1, count):
        give = lax.dynamic_index_in_dim(value, (here + step) % count, 0, False)
        total = total + ahead(give, "gx", step).astype(jnp.float32)
    return total.astype(jnp.bfloat16)


def join_step(value, end=()):
    columns = value.shape[-1]
    return pair_rows(value, gate(swap(value, "dp", 1), end)).reshape(-1, columns).astype(jnp.float32)


def side_parts(first, second):
    first_side = lax.axis_index("gy") == 0
    return jnp.where(first_side, first, second), jnp.where(first_side, second, first)


def side_exchange(first, second):
    keep, give = side_parts(first, second)
    return add(keep, swap(give, "gy", 1))


def projection_sides(first, rest):
    query, key, value = (first[..., n * GROUP : (n + 1) * GROUP] for n in range(3))
    size = rest.shape[-1] // 3
    query_rest, key_rest, value_rest = (rest[..., n * size : n * size + GROUP + 128] for n in range(3))
    return (
        jnp.concatenate([query, key, query_rest, key_rest[..., :128]], axis=-1),
        jnp.concatenate([value, key_rest, value_rest], axis=-1),
    )


def join_projections(whole, width):
    rest = width - GROUP
    spare = width // 2 - GROUP
    wide = GROUP + 128
    query, key = whole[:, :GROUP], whole[:, GROUP : 2 * GROUP]
    query_rest = whole[:, 2 * GROUP : 2 * GROUP + rest]
    key_spare = whole[:, 2 * GROUP + wide : 2 * GROUP + wide + spare]
    value = whole[:, :GROUP]
    key_rest = whole[:, GROUP + spare : GROUP + rest]
    value_rest = whole[:, GROUP + wide : GROUP + wide + rest]
    return jnp.where(
        lax.axis_index("gy") == 0,
        jnp.concatenate([query, query_rest, key, key_spare], axis=1),
        jnp.concatenate([key_rest, value, value_rest], axis=1),
    )


def scatter_plain(whole):
    part = lax.psum_scatter(whole, "gy", scatter_dimension=1, tiled=True)
    part = lax.psum_scatter(part, "gx", scatter_dimension=0, tiled=True)
    return lax.psum(part, "dp").astype(jnp.float32)


def all_tokens(own):
    count = lax.axis_size("gy")
    here = lax.axis_index("gy")
    if count != 2:
        return lax.all_gather(own, "gy", axis=0, tiled=True)
    other = swap(own, "gy", 1)
    first = here == 0
    return jnp.concatenate([jnp.where(first, own, other), jnp.where(first, other, own)], axis=0)


def others_tokens(whole):
    count = lax.axis_size("gy")
    here = lax.axis_index("gy")
    rows = whole.shape[0] // count
    if count != 2:
        keep = lax.dynamic_slice_in_dim(whole, here * rows, rows, 0)
        total = lax.psum_scatter(whole, "gy", scatter_dimension=0, tiled=True)
        return (total.astype(jnp.float32) - keep.astype(jnp.float32)).astype(jnp.bfloat16)
    return swap(lax.dynamic_slice_in_dim(whole, (1 - here) * rows, rows, 0), "gy", 1)


def dot(a, b):
    return jnp.dot(a, b, preferred_element_type=jnp.float32)


def local(
    prompt,
    continuations,
    prefix_len,
    attn_gain,
    attn_shift,
    qkv_weight,
    query_bias,
    value_bias,
    out_weight,
    out_bias,
    mlp_gain,
    mlp_shift,
    up_weight,
    up_bias,
    down_weight,
    down_bias,
    grad_prompt,
    grad_continuations,
):
    groups, shard, width = prompt.shape
    length = continuations.shape[1]
    first_pos = lax.axis_index("gy") * shard
    prompt_len = shard * lax.axis_size("gy")
    block = shard // 2
    halved = by_halves(width // 2)
    spans = [slice(0, GROUP), slice(GROUP, width)]

    if halved:
        limit, other_limit = prefix_len[0], swap(prefix_len, "gy", 1)[0]
        is_first = first_pos == 0
        is_long = jnp.logical_or(limit > other_limit, jnp.logical_and(limit == other_limit, is_first))
        kept_at = jnp.where(is_long, 0, block)
        places = [first_pos + kept_at, shard - first_pos + kept_at, limit]
    else:
        places = [first_pos, first_pos + block, prefix_len[0]]
    places = jnp.stack(places).astype(jnp.int32)

    def kept_rows(own):
        return lax.dynamic_slice_in_dim(own, kept_at, block, 0)

    def given_rows(own):
        return lax.dynamic_slice_in_dim(own, block - kept_at, block, 0)

    def back_home(done):
        if not halved:
            return done
        kept, home = done[:block], swap(done[block:], "gy", 1)
        return jnp.concatenate([jnp.where(is_long, kept, home), jnp.where(is_long, home, kept)], axis=0)

    own_prompt = prompt.reshape(shard, width)
    branch = continuations.reshape(length, width)
    own_cot = grad_prompt.reshape(shard, width)
    branch_cot = grad_continuations.reshape(length, width)
    whole_prompt = all_tokens(own_prompt)
    if halved:
        weights, out_full, raw = gather_projections(qkv_weight, out_weight, width)
        quarters, fetched = gather_feed_forward(up_weight, down_weight.T, (raw,))
        other_cot = swap(gate(given_rows(own_cot), (raw,)), "gy", 1)
        cotangent = jnp.concatenate([kept_rows(own_cot), other_cot, branch_cot], axis=0)
    else:
        qkv = gather_plain(qkv_weight)
        weights = [[qkv[:, c.start + s : c.stop + s] for s in (0, width, 2 * width)] for c in spans]
        out_full, up_full, down_full = (gather_plain(w) for w in (out_weight, up_weight, down_weight.T))
        cotangent = jnp.concatenate([own_cot, branch_cot], axis=0)

    all_rows = jnp.concatenate([whole_prompt, branch], axis=0)
    norm_all, _ = normalise(all_rows.astype(jnp.float32))
    act_all = (norm_all * attn_gain + attn_shift).astype(jnp.bfloat16)
    projected, mixed, stats = [], [], []
    for number, (cols, (w_query, w_key, w_value)) in enumerate(zip(spans, weights)):
        projected.append(
            (
                (dot(act_all, w_query) + query_bias[cols]).astype(jnp.bfloat16),
                dot(act_all, w_key).astype(jnp.bfloat16),
                (dot(act_all, w_value) + value_bias[cols]).astype(jnp.bfloat16),
            )
        )
        got, stat = attention_forward(places, *projected[-1], block, length)
        if halved and number == 0:
            fetched = gate(fetched, (got, cotangent))
            theirs = swap(fetched, "gy", 1)
        if halved and number == 1:
            up_full, down_full = finish_feed_forward(quarters, fetched, gate(theirs, (got,)))
        mixed.append(got)
        stats.append(stat)

    tokens = jnp.concatenate(
        [lax.dynamic_slice_in_dim(whole_prompt, places[n], block, 0) for n in range(2)] + [branch], axis=0
    )
    all_turned, cotangent_turned = act_all.T, cotangent.T
    hidden, slope, result, act_turned, norm_two, pace_two = mlp_forward(
        mixed,
        tokens,
        out_full,
        out_bias,
        mlp_gain,
        mlp_shift,
        up_full,
        up_bias,
        down_full,
        down_bias,
        (all_turned, cotangent_turned),
    )
    count = lax.axis_size("gx")
    half = jnp.reshape(half_index() if halved else 0, (1,)).astype(jnp.int32)
    tiles = up_full.shape[1] // TILE
    part = tiles // 2
    prompt_out = back_home(result[:shard]).reshape(groups, shard, width)
    continuation_out = result[shard:].reshape(1, length, width)
    down_keep, down_give = down_back(half, count, cotangent_turned, hidden)
    after = ()
    if halved:
        down_flow = core_step(down_keep, down_give)
        after = (down_flow, prompt_out)
    so_far, up_keep, up_give, up_bias_grad = up_back(
        half, count, (0, part), act_turned, cotangent, slope, up_full, down_full
    )
    d_resid, d_branch, *d_mixed, keep_rest, give_rest, out_keep, out_give, bias_rest, lines = up_back(
        half,
        count,
        (part, tiles),
        act_turned,
        cotangent,
        slope,
        up_full,
        down_full,
        (so_far, norm_two, pace_two, mlp_gain, mixed, out_full),
        after,
    )
    up_bias_grad = jnp.concatenate([up_bias_grad, bias_rest], axis=1)
    mlp_gain_grad, mlp_shift_grad, out_bias_grad, down_bias_grad = (lines[n] for n in range(4))
    if halved:
        side = up_weight.shape[1]
        up_flow = core_step(up_keep, gate(up_give, (down_flow,)))
        keep, give = chips_parts((down_flow[..., :side], down_flow[..., side:]))
        down_flow = chips_step((keep, gate(give, (so_far,))))
        ready = (down_flow, up_flow)
        rest_flow, out_flow = core_step(keep_rest, gate(give_rest, ready)), core_step(out_keep, gate(out_give, ready))
        ready = (rest_flow, out_flow)
        up_flow = jnp.concatenate([up_flow, rest_flow], axis=-1)
        down_flow = gate(down_flow, ready)
        after = (down_flow, up_flow, out_flow)
    d_parts = [None, None]
    for number in (1, 0):
        d_parts[number] = attention_backward(
            places, *projected[number], mixed[number], d_mixed[number], stats[number], block, length, after
        )
        if halved and number == 1:
            up_flow = side_exchange(
                jnp.concatenate([up_flow[..., :side], out_flow[..., : width // 2]], axis=-1),
                jnp.concatenate([up_flow[..., side:], out_flow[..., width // 2 :]], axis=-1),
            )
            down_flow = blocks_step(down_flow)
            after = (up_flow, down_flow)
        if halved and number == 0:
            up_flow = blocks_step(up_flow)
            down_keep, down_give = side_parts(*two(down_flow))
            home_give = gate(d_branch[block:shard], (d_parts[0][0],))
            after = (up_flow, down_give, home_give)
    keep_a, give_a, bias_a, keep_b, give_b, bias_b = weights_back(half, count, all_turned, d_parts, after)
    if halved:
        sides = projection_sides(core_step(keep_a, give_a), core_step(keep_b, give_b))
        parts = chips_parts(sides)
        up_flow = add(up_flow, gate(swap(up_flow, "dp", 2), (keep_a,)))
        down_flow = add(down_keep, gate(swap(down_give, "gy", 1), (keep_a,)))
        home = gate(swap(home_give, "gy", 1), (keep_a,)).astype(jnp.float32)
        after = (*parts, up_flow, down_flow)
    else:
        after = (keep_a,)
    d_act_all, act_lines = tokens_back(d_parts, weights, all_rows, length, after)
    attn_gain_grad, attn_shift_grad = act_lines[0], act_lines[1]
    others = others_tokens(d_act_all[:prompt_len])
    if halved:
        qkv_flow = chips_step(parts, (d_act_all,))
        up_total = join_step(up_flow, (d_act_all,))
        down_flow = overlap_join(down_flow, side, (d_act_all,))
        qkv_flow = blocks_step(qkv_flow)
        others = gate(others, (qkv_flow,))
        down_total = join_step(gate(down_flow, (qkv_flow,)))
    size = bias_b.shape[1] // 3
    query_bias_grad, value_bias_grad = (
        jnp.concatenate(
            [bias_a[0, n * GROUP : (n + 1) * GROUP], bias_b[0, n * size : n * size + width - GROUP]]
        )
        for n in (0, 2)
    )
    if halved:
        qkv_flow = side_exchange(*two(qkv_flow))
        qkv_total = join_projections(join_step(overlap_join(qkv_flow, sides[0].shape[-1])), width)
        up_total, out_total = up_total[:, :side], up_total[:, side:]
    else:
        whole_a, whole_b = both_halves(keep_a, give_a), both_halves(keep_b, give_b)
        qkv_grad = jnp.concatenate(
            [
                piece
                for n in range(3)
                for piece in (
                    whole_a[:, n * GROUP : (n + 1) * GROUP],
                    whole_b[:, n * size : n * size + width - GROUP],
                )
            ],
            axis=1,
        )
        up_total, down_total, out_total, qkv_total = (
            scatter_plain(g)
            for g in (
                jnp.concatenate([both_halves(up_keep, up_give), both_halves(keep_rest, give_rest)], axis=1),
                both_halves(down_keep, down_give),
                both_halves(out_keep, out_give),
                qkv_grad,
            )
        )
    prompt_resid = d_resid[:shard]
    if halved:
        kept = prompt_resid[:block]
        kept = jnp.where(is_long, kept, home), jnp.where(is_long, home, kept)
        prompt_resid = jnp.concatenate(kept, axis=0)
    own_rows = jnp.concatenate([own_prompt, branch], axis=0)
    own_grad = jnp.concatenate(
        [lax.dynamic_slice_in_dim(d_act_all, first_pos, shard, 0), d_act_all[prompt_len:]], axis=0
    )
    resid_rows = jnp.concatenate([prompt_resid, d_resid[shard:]], axis=0)
    prompt_grad, branch_grad = rows_back(others, own_grad, own_rows, resid_rows, attn_gain, length)
    prompt_grad = prompt_grad.T.reshape(groups, shard, width)
    continuation_grad = branch_grad.T.reshape(1, length, width)
    vectors = (
        attn_gain_grad,
        attn_shift_grad,
        query_bias_grad,
        value_bias_grad,
        out_bias_grad,
        mlp_gain_grad,
        mlp_shift_grad,
        up_bias_grad.reshape(-1),
        down_bias_grad,
    )
    joined = jnp.sum(lax.all_gather(jnp.concatenate(vectors), ("dp", "gx", "gy")), axis=0)
    totals = []
    at = 0
    for vector in vectors:
        totals.append(joined[at : at + vector.shape[0]])
        at += vector.shape[0]
    return (
        prompt_out,
        continuation_out,
        prompt_grad,
        continuation_grad,
        totals[0],
        totals[1],
        qkv_total,
        totals[2],
        totals[3],
        out_total,
        totals[4],
        totals[5],
        totals[6],
        up_total,
        totals[7],
        down_total.T,
        totals[8],
    )


def solution(mesh):
    placed = (
        P(("dp", "gx"), "gy", None),
        P(("dp", "gx", "gy"), None, None),
        P(("dp", "gx", "gy")),
        P(),
        P(),
        P("gx", "gy"),
        P(),
        P(),
        P("gx", "gy"),
        P(),
        P(),
        P(),
        P("gx", "gy"),
        P(),
        P("gy", "gx"),
        P(),
        P(("dp", "gx"), "gy", None),
        P(("dp", "gx", "gy"), None, None),
    )
    return jax.shard_map(
        local,
        mesh=mesh,
        in_specs=placed,
        out_specs=(
            P(("dp", "gx"), "gy", None),
            P(("dp", "gx", "gy"), None, None),
            P(("dp", "gx"), "gy", None),
            P(("dp", "gx", "gy"), None, None),
            P(),
            P(),
            P("gx", "gy"),
            P(),
            P(),
            P("gx", "gy"),
            P(),
            P(),
            P(),
            P("gx", "gy"),
            P(),
            P("gy", "gx"),
            P(),
        ),
        check_vma=False,
    )
```
